32 devices in a mesh: groups: 2 (over x), expert: 4 (over y, core), tensor: 4 (over z).
Axes of the slice: x: 2, y: 2, z: 4, core: 2. Of those that a mesh axis runs over, the one named last changes fastest.
Arguments:
- tokens: bfloat16 [2, 128, 7168], P(None, ('groups', 'expert')), parts along dimension 1, may hold values from -6 to 6
- expert_ids: int32 [2, 128, 2], P(None, ('groups', 'expert')), parts along dimension 1, may hold values from 0 to 3, all different within a row; in each aligned block of 16 rows (0 to 15, 16 to 31, ..., all dimensions but the last counted through in order) at most 12 rows name the same one
- gate_values: float32 [2, 128, 2], P(None, ('groups', 'expert')), parts along dimension 1, may hold values from 0.05 to 0.3
- tenant_ids: int32 [128], P(('groups', 'expert')), parts along dimension 0, may hold values from 0 to 15
- w_gate: bfloat16 [4, 7168, 1024], P('expert', None, 'tensor'), may hold values from -0.0625 to 0.0625
- w_up: bfloat16 [4, 7168, 1024], P('expert', None, 'tensor'), may hold values from -0.0625 to 0.0625
- routed_down_weight: bfloat16 [4, 1024, 7168], P('expert', 'tensor'), may hold values from -0.1875 to 0.1875
- shared_gate: bfloat16 [7168, 1024], P(None, 'tensor'), may hold values from -0.0625 to 0.0625
- shared_up: bfloat16 [7168, 1024], P(None, 'tensor'), may hold values from -0.0625 to 0.0625
- shared_down: bfloat16 [1024, 7168], P('tensor'), may hold values from -0.1875 to 0.1875
- store_a: bfloat16 [8, 16, 7168], P('expert'), may hold values from -0.0625 to 0.0625
- store_b: bfloat16 [8, 16, 1024], P('expert', None, 'tensor'), may hold values from -1.5 to 1.5
- pair_slot: int32 [4, 16], replicated, may hold values from -1 to 7, as said below
- shared_a: bfloat16 [16, 16, 7168], P('expert'), may hold values from -0.0625 to 0.0625
- shared_b: bfloat16 [16, 16, 1024], P('expert', None, 'tensor'), may hold values from -1.5 to 1.5
Outputs:
- mixed: bfloat16 [2, 128, 7168], P(None, ('groups', 'expert'), 'tensor'), parts along dimension 1
The draws below stay inside these ranges and needn't reach their ends.
There are 2 independent parts, one for each index of `groups`. The reference program is written for one: setup_inputs(seed, part) draws one part's arguments, and reference() takes and returns one part's arrays. A program takes and returns all parts, laid end to end along the dimension named above; an argument that names none is the same for every part. Nothing has to cross between parts.
Inputs may be any that keep to these rules, and one draw needn't show every extreme that they name: `expert_ids`: each row names 2 different experts. In each step, among the 16 rows of one index of expert, no expert is named by more than 12 rows, a bound that some block reaches. pair_slot[e, t] is the store slot that holds tenant t's adapter of routed expert e, or -1 where that pair has none. Store slot j lies on index j // 2 of expert. Every slot holds exactly one pair; each routed expert has exactly 2 adapted tenants, no two of them on the same index of expert.
All inputs are finite; a program needn't handle non-finite values.
Results may differ from the reference program's by a relative error of at most 0.017.
Values may be sent and summed in bfloat16 or wider, within the bound.
No kernel may reach another device: no remote copies, remote signals or barrier semaphores. Data moves between devices by JAX's collectives and lax.ppermute only.
A program may use at most 128 MiB of HBM per device.

```python
import math
import jax
import jax.numpy as jnp
import numpy as np
from jax import lax

D = 7168
HID = 1024
RANK = 16
TENANTS = 16
STEPS = 2
TOK_DEV = 16
HID_BLOCK = 256
EXPERTS = 4
TOPK = 2
CAP = 12
ADAPTED = 2
SLOTS = 8
TOKENS = 64
N_TENSOR = 4


def draw_pair_slot(key, part):
    key = jax.random.fold_in(key, 11)
    subkeys = jax.random.split(key, 4)
    offsets = jax.random.permutation(subkeys[0], EXPERTS)[:ADAPTED].astype(jnp.int32)
    store_label = jax.random.permutation(subkeys[1], EXPERTS).astype(jnp.int32)
    expert_label = jax.random.permutation(subkeys[2], EXPERTS).astype(jnp.int32)
    orders = jax.vmap(lambda subkey: jax.random.permutation(subkey, TENANTS))(jax.random.split(subkeys[3], EXPERTS)).astype(jnp.int32)
    store_index = jnp.arange(EXPERTS, dtype=jnp.int32)[:, None]
    slot_index = jnp.arange(ADAPTED, dtype=jnp.int32)[None, :]
    target = expert_label[(store_label[store_index] + offsets[slot_index]) % EXPERTS]
    tenant = orders[target, jnp.broadcast_to(slot_index, target.shape)]
    table = jnp.full((EXPERTS, TENANTS), -1, jnp.int32)
    return table.at[target, tenant].set((store_index * ADAPTED + slot_index).astype(jnp.int32))


def place_ends(entries, rng, low, largest):
    longest = entries.shape.index(max(entries.shape))
    spots = []
    for shift in (0, 1):
        where = [jax.random.randint(jax.random.fold_in(rng, axis), (), 0, length) for axis, length in enumerate(entries.shape)]
        where[longest] = (where[longest] + shift) % entries.shape[longest]
        spots.append(tuple(where))
    return entries.at[spots[0]].set(low).at[spots[1]].set(largest)


def block_levels(key, extent, cuts, low, top_value):
    level, own = 1.0, jax.random.fold_in(key, 6)
    for position, parts in cuts:
        heights = jnp.exp(jax.random.uniform(jax.random.fold_in(own, position), (parts,), jnp.float32, low / len(cuts), top_value / len(cuts)))
        level = level * jnp.repeat(heights, extent[position] // parts).reshape([-1 if axis == position else 1 for axis in range(len(extent))])
    return level


def routed_block(stream_key, own, number, rows, count, top, most, slope):
    sequence = jax.random.permutation(stream_key, count)
    heavy_load, ordinary = portions_of(count, rows * top, most, slope, True), portions_of(count, rows * top, most, slope, False)
    places = jnp.arange(count)

    def named(tallies, rotation):
        used = int((tallies > 0).sum())
        fixed = max(1, used // 4)
        passed = fixed + (places - fixed + rotation * (used - fixed)) % max(1, count - fixed)
        return jnp.zeros((count,), jnp.int32).at[sequence[jnp.where(places < fixed, places, passed)]].set(jnp.asarray(tallies, jnp.int32))

    tallies = jnp.where(number % 4 == 0, named(heavy_load, number // 4), named(ordinary, number - number // 4 - 1))
    mixed = jax.random.permutation(jax.random.fold_in(own, 3), count)
    giver, taker = mixed[0:count // 2 * 2:2], mixed[1:count // 2 * 2:2]
    slack = jnp.minimum(tallies[giver] - 1, most - tallies[taker]) // 2
    slack = jnp.where((giver == sequence[0]) | (taker == sequence[0]) | (tallies[taker] == 0), 0, jnp.maximum(slack, 0))
    passed = jax.random.randint(jax.random.fold_in(own, 4), (count // 2,), 0, 1 << 20) % (slack + 1)
    tallies = tallies.at[giver].add(-passed).at[taker].add(passed)
    labels = jnp.searchsorted(jnp.cumsum(tallies), jnp.arange(rows * top), side="right").astype(jnp.int32)
    table = labels.reshape(top, rows).T
    table = table[jax.random.permutation(jax.random.fold_in(own, 1), rows)]
    rotation = jax.random.randint(jax.random.fold_in(own, 2), (rows, 1), 0, top)
    return jnp.take_along_axis(table, (jnp.arange(top)[None, :] + rotation) % top, axis=1)


def portions_of(amount, total, bound, slope, full):
    loads = [(1 << 20) // math.isqrt(standing ** slope) + 1 for standing in range(1, amount + 1)]
    largest = bound if full else min(bound, max(-(-total // amount), total * loads[0] // sum(loads)))
    least = 1 if total - largest >= amount - 1 else 0
    given, spare = [largest] + [least] * (amount - 1), total - largest - least * (amount - 1)
    while spare > 0:
        free = [i for i in range(1, amount) if given[i] < largest] or [i for i in range(1, amount) if given[i] < bound]
        pool, remaining = sum([loads[i] for i in free]), spare
        for i in free:
            more = min(bound - given[i], max(1, remaining * loads[i] // pool), spare)
            given[i] = given[i] + more
            spare = spare - more
    return np.array(given)


def centred(own_key, dims, spread, reach, shards=(), held_as=jnp.bfloat16):
    array = jax.random.normal(own_key, dims, jnp.float32) * spread
    if len(shards) > 0:
        array = block_levels(own_key, dims, shards, -0.22, 0.18) * array
    return jnp.clip(array, min=-reach, max=reach).astype(held_as)


def setup_inputs(seed: int = 0, part: int = 0) -> dict:
    key_of = jax.random.split(jax.random.key(seed), 16)
    part_keys = jax.random.split(jax.random.fold_in(key_of[15], part), 16)
    tokens = centred(part_keys[0], (STEPS, TOKENS, D), 1.0, 6.0, ((1, 4),))
    expert_ids_keys = jax.random.split(jax.random.fold_in(part_keys[1], 1), STEPS * TOKENS // TOK_DEV)
    expert_ids_turns = jax.random.permutation(jax.random.fold_in(part_keys[1], 3), STEPS * TOKENS // TOK_DEV)
    expert_ids = jax.vmap(lambda own, number: routed_block(jax.random.fold_in(part_keys[1], 2), own, number, TOK_DEV, EXPERTS, TOPK, CAP, 2))(expert_ids_keys, expert_ids_turns).reshape((STEPS, TOKENS, TOPK))
    gate_values = jnp.clip(0.05 + 0.25 * jax.random.uniform(part_keys[2], (STEPS, TOKENS, TOPK), jnp.float32) ** block_levels(part_keys[2], (STEPS, TOKENS, TOPK), ((1, 4),), -0.2, 0.2), 0.05, 0.3)
    tenant_ids = place_ends(jax.random.randint(part_keys[3], (TOKENS,), 0, TENANTS), jax.random.fold_in(part_keys[3], 1), 0, TENANTS - 1).astype(jnp.int32)
    w_gate = centred(key_of[4], (EXPERTS, D, HID), D ** -0.5, 0.0625, ((0, 4), (2, 4)))
    w_up = centred(key_of[5], (EXPERTS, D, HID), D ** -0.5, 0.0625, ((0, 4), (2, 4)))
    routed_down_weight = centred(key_of[6], (EXPERTS, HID, D), HID ** -0.5, 0.1875, ((0, 4), (1, 4)))
    shared_gate = centred(key_of[7], (D, HID), D ** -0.5, 0.0625, ((1, 4),))
    shared_up = centred(key_of[8], (D, HID), D ** -0.5, 0.0625, ((1, 4),))
    shared_down = centred(key_of[9], (HID, D), HID ** -0.5, 0.1875, ((0, 4),))
    store_a = centred(key_of[10], (SLOTS, RANK, D), D ** -0.5, 0.0625, ((0, 4),))
    store_b = centred(key_of[11], (SLOTS, RANK, HID), RANK ** -0.5, 1.5, ((0, 4), (2, 4)))
    pair_slot = draw_pair_slot(jax.random.fold_in(key_of[15], 71), part)
    shared_a = centred(key_of[13], (TENANTS, RANK, D), D ** -0.5, 0.0625, ((0, 4),))
    shared_b = centred(key_of[14], (TENANTS, RANK, HID), RANK ** -0.5, 1.5, ((0, 4), (2, 4)))
    return dict(tokens=tokens, expert_ids=expert_ids, gate_values=gate_values, tenant_ids=tenant_ids, w_gate=w_gate, w_up=w_up, routed_down_weight=routed_down_weight, shared_gate=shared_gate, shared_up=shared_up, shared_down=shared_down, store_a=store_a, store_b=store_b, pair_slot=pair_slot, shared_a=shared_a, shared_b=shared_b)


def contract(token_row_block, factor):
    return lax.dot_general(token_row_block, factor, (((1,), (1,)), ((), ())), preferred_element_type=jnp.float32)


def hidden_units(token_row_block, tenant_hot, gate_weight, up_weight, factor_a, factor_b):
    gate = jnp.dot(token_row_block, gate_weight, preferred_element_type=jnp.float32)
    lifted = jnp.where(tenant_hot, contract(token_row_block, factor_a), 0.0).astype(jnp.bfloat16)
    upward = jnp.dot(token_row_block, up_weight, preferred_element_type=jnp.float32) + jnp.dot(lifted, factor_b, preferred_element_type=jnp.float32)
    return (jax.nn.silu(gate) * upward).astype(jnp.bfloat16)


def down_blocks(hidden, down_weight):
    count = hidden.shape[0]
    blocks = hidden.reshape(count, N_TENSOR, HID_BLOCK).astype(jnp.float32)
    pieces = down_weight.reshape(N_TENSOR, HID_BLOCK, D).astype(jnp.float32)
    partial_sums = jnp.einsum("nbh,bhd->bnd", blocks, pieces, precision=lax.Precision.HIGHEST)
    rounded = lax.optimization_barrier(partial_sums.astype(jnp.bfloat16))
    return jnp.sum(rounded.astype(jnp.float32), axis=0)


def reference(tokens, expert_ids, gate_values, tenant_ids, w_gate, w_up, routed_down_weight, shared_gate, shared_up, shared_down, store_a, store_b, pair_slot, shared_a, shared_b):
    tenant_columns = jnp.arange(TENANTS * RANK, dtype=jnp.int32) // RANK
    tenant_hot = tenant_ids[:, None] == tenant_columns[None, :]
    shared_flat_a = shared_a.reshape(TENANTS * RANK, D)
    shared_flat_b = shared_b.reshape(TENANTS * RANK, HID)
    results = []
    for step_index in range(STEPS):
        token_row_block = tokens[step_index]
        picks = expert_ids[step_index]
        weights = gate_values[step_index]
        shared_hidden = hidden_units(token_row_block, tenant_hot, shared_gate, shared_up, shared_flat_a, shared_flat_b)
        shared_out = down_blocks(shared_hidden, shared_down)

        def one_expert(total, inputs):
            gate_weight, up_weight, down_weight, slots, index = inputs
            present = slots >= 0
            safe = jnp.maximum(slots, 0)
            factor_a = jnp.where(present[:, None, None], jnp.take(store_a, safe, axis=0), jnp.zeros((), store_a.dtype))
            factor_b = jnp.where(present[:, None, None], jnp.take(store_b, safe, axis=0), jnp.zeros((), store_b.dtype))
            hidden = hidden_units(token_row_block, tenant_hot, gate_weight, up_weight, factor_a.reshape(TENANTS * RANK, D), factor_b.reshape(TENANTS * RANK, HID))
            expert_out = lax.optimization_barrier(down_blocks(hidden, down_weight).astype(jnp.bfloat16)).astype(jnp.float32)
            weight_row = jnp.sum(jnp.where(picks == index, weights, 0.0), axis=1)
            return total + weight_row[:, None] * expert_out, None

        routed, _ = lax.scan(one_expert, jnp.zeros((TOKENS, D), jnp.float32), (w_gate, w_up, routed_down_weight, pair_slot, jnp.arange(EXPERTS, dtype=jnp.int32)))
        results.append((shared_out + routed).astype(jnp.bfloat16))
    return jnp.stack(results, axis=0)
```

```python
import functools

import jax
import jax.numpy as jnp
from jax import lax
from jax.experimental import pallas as pl
from jax.experimental.pallas import tpu as pltpu
from jax.sharding import PartitionSpec as P

F32 = jnp.float32
BF16 = jnp.bfloat16
VMEM_LIMIT = 24 * 1024 * 1024


def params():
    return pltpu.CompilerParams(
        dimension_semantics=("arbitrary",), vmem_limit_bytes=VMEM_LIMIT
    )


def cost(flops, moved):
    return pl.CostEstimate(flops=int(flops), bytes_accessed=int(moved), transcendentals=0)


def swap(value, bit):
    count = lax.axis_size("expert")
    return lax.ppermute(value, "expert", [(i, i ^ bit) for i in range(count)])


def exchange_all(value):
    count = lax.axis_size("expert")
    pieces = {0: value}
    bit = count // 2
    while bit >= 1:
        pieces.update({r ^ bit: swap(piece, bit) for r, piece in list(pieces.items())})
        bit //= 2
    return [pieces[r] for r in range(count)]


def rows_of(refs):
    return jnp.concatenate([ref[...] for ref in refs], axis=0)


def gate_up_kernel(count, *refs):
    rows, gate_weight, up_weight, gate, up = refs[:count], *refs[count:]

    @pl.when(pl.program_id(0) == 0)
    def _():
        gate[...] = jnp.zeros_like(gate)
        up[...] = jnp.zeros_like(up)

    block = rows_of(rows)
    gate[...] += jnp.dot(block, gate_weight[...], preferred_element_type=F32)
    up[...] += jnp.dot(block, up_weight[...], preferred_element_type=F32)


def gate_up(rows, gate_weight, up_weight):
    depth, width = gate_weight.shape
    size = rows[0].shape[0]
    total = size * len(rows)
    chunk = 1024
    out = jax.ShapeDtypeStruct((total, width), F32)
    return pl.pallas_call(
        functools.partial(gate_up_kernel, len(rows)),
        grid=(depth // chunk,),
        in_specs=[pl.BlockSpec((size, chunk), lambda k: (0, k))] * len(rows)
        + [pl.BlockSpec((chunk, width), lambda k: (k, 0))] * 2,
        out_specs=[pl.BlockSpec((total, width), lambda k: (0, 0))] * 2,
        out_shape=[out, out],
        compiler_params=params(),
        cost_estimate=cost(4 * total * depth * width, 4 * depth * width),
    )(*rows, gate_weight, up_weight)


def inner_kernel(count, *refs):
    rows, factor_shared, factor_store, inner, total = refs[:count], *refs[count:]

    @pl.when(pl.program_id(0) == 0)
    def _():
        total[...] = jnp.zeros_like(total)

    block = rows_of(rows)
    factors = jnp.concatenate([factor_shared[...], factor_store[...]], axis=0)
    total[...] += lax.dot_general(
        block, factors, (((1,), (1,)), ((), ())), preferred_element_type=F32
    )

    @pl.when(pl.program_id(0) == pl.num_programs(0) - 1)
    def _():
        inner[...] = total[...].astype(BF16)


def inner_products(rows, factor_shared, factor_store):
    depth = factor_shared.shape[1]
    size = rows[0].shape[0]
    total = size * len(rows)
    shared_count, store_count = factor_shared.shape[0], factor_store.shape[0]
    width = shared_count + store_count
    chunk = 1792
    return pl.pallas_call(
        functools.partial(inner_kernel, len(rows)),
        grid=(depth // chunk,),
        in_specs=[pl.BlockSpec((size, chunk), lambda k: (0, k))] * len(rows)
        + [
            pl.BlockSpec((shared_count, chunk), lambda k: (0, k)),
            pl.BlockSpec((store_count, chunk), lambda k: (0, k)),
        ],
        out_specs=pl.BlockSpec((total, width), lambda k: (0, 0)),
        out_shape=jax.ShapeDtypeStruct((total, width), BF16),
        scratch_shapes=[pltpu.VMEM((total, width), F32)],
        compiler_params=params(),
        cost_estimate=cost(2 * total * depth * width, 2 * depth * width),
    )(*rows, factor_shared, factor_store)


def silu(value):
    return value / (1.0 + jnp.exp(-value))


def down_kernel(count, size, shared_count, *refs):
    gate, up, gate_own, up_own = refs[:4]
    inner = refs[4 : 4 + count]
    factors = refs[4 + count : 4 + 2 * count]
    row_tenant, slot_tenant, shared_tenant, share, down, down_own = refs[
        4 + 2 * count : 10 + 2 * count
    ]
    outs = refs[10 + 2 * count : 10 + 3 * count]
    hidden, hidden_own = refs[10 + 3 * count :]

    @pl.when(pl.program_id(0) == 0)
    def _():
        width = inner[0].shape[1]
        parts, parts_own = [], []
        for r in range(count):
            held = inner[r][...]
            blocks = [held[(k ^ r) * size : ((k ^ r) + 1) * size] for k in range(count)]
            parts.append(jnp.concatenate(blocks, axis=0)[:, shared_count:])
            parts_own.append(blocks[0][:, :shared_count])
        lifted = jnp.concatenate(parts, axis=1)
        lifted_own = jnp.concatenate(parts_own, axis=1)
        tenants = row_tenant[...]
        zero = jnp.zeros((), BF16)
        lifted = jnp.where(tenants == slot_tenant[...], lifted, zero)
        lifted_own = jnp.where(tenants[:size] == shared_tenant[...], lifted_own, zero)
        factor = jnp.concatenate([ref[shared_count:width] for ref in factors], axis=0)
        factor_own = jnp.concatenate([ref[:shared_count] for ref in factors], axis=0)
        upward = up[...] + jnp.dot(lifted, factor, preferred_element_type=F32)
        hidden[...] = (silu(gate[...]) * upward).astype(BF16)
        upward_own = up_own[...] + jnp.dot(lifted_own, factor_own, preferred_element_type=F32)
        hidden_own[...] = (silu(gate_own[...]) * upward_own).astype(BF16)

    routed = jnp.dot(hidden[...], down[...], preferred_element_type=F32) * share[...]
    own = jnp.dot(hidden_own[...], down_own[...], preferred_element_type=F32)
    outs[0][0] = (routed[:size] + own).astype(BF16)
    for r in range(1, count):
        outs[r][0] = routed[r * size : (r + 1) * size].astype(BF16)


def down_products(
    gate, up, gate_own, up_own, inner, factors, row_tenant, slot_tenant, shared_tenant, share,
    down, down_own, size, shared_count, blocks,
):
    count = len(inner)
    total, hid = gate.shape
    depth = down.shape[1]
    part = depth // blocks
    whole = [gate, up, gate_own, up_own, *inner, *factors, row_tenant, slot_tenant, shared_tenant, share]
    return pl.pallas_call(
        functools.partial(down_kernel, count, size, shared_count),
        grid=(blocks,),
        in_specs=[pl.BlockSpec(x.shape, lambda j: (0, 0)) for x in whole]
        + [pl.BlockSpec((hid, part), lambda j: (0, j))] * 2,
        out_specs=[pl.BlockSpec((1, size, part), lambda j: (j, 0, 0))] * count,
        out_shape=[jax.ShapeDtypeStruct((blocks, size, part), BF16)] * count,
        scratch_shapes=[pltpu.VMEM((total, hid), BF16), pltpu.VMEM((size, hid), BF16)],
        compiler_params=params(),
        cost_estimate=cost(2 * (total + size) * depth * hid, 4 * depth * hid),
    )(*whole, down, down_own)


def split3(value):
    first = lax.reduce_precision(value, 8, 7)
    second = lax.reduce_precision(value - first, 8, 7)
    return jnp.stack([first, second, value - first - second]).astype(BF16)


def local(
    tokens,
    expert_ids,
    gate_values,
    tenant_ids,
    w_gate,
    w_up,
    routed_down_weight,
    shared_gate,
    shared_up,
    shared_down,
    store_a,
    store_b,
    pair_slot,
    shared_a,
    shared_b,
):
    experts, tenants = pair_slot.shape
    adapted, rank, model_width = store_a.shape
    own_tenants = shared_a.shape[0]
    hid = store_b.shape[2]
    steps, size, _ = expert_ids.shape
    count = lax.axis_size("expert")
    n_tensor = lax.axis_size("tensor")
    own = lax.axis_index("expert")
    shared_count = own_tenants * rank

    gathered = [exchange_all(tokens[s]) for s in range(steps)]

    hits = expert_ids[..., None] == jnp.arange(experts, dtype=jnp.int32)
    dense = jnp.sum(jnp.where(hits, gate_values[..., None], 0.0), axis=2)
    dense = dense.reshape(steps * size * experts)
    extra = jnp.concatenate([split3(dense).reshape(-1), tenant_ids.astype(BF16)])
    extra_rows = -(-extra.shape[0] // (16 * hid)) * 16
    extra = jnp.pad(extra, (0, extra_rows * hid - extra.shape[0])).reshape(extra_rows, hid)
    pack = jnp.concatenate(
        [shared_b.reshape(shared_count, hid), store_b.reshape(adapted * rank, hid), extra], axis=0
    )
    packs = exchange_all(pack)
    base = shared_count + adapted * rank
    number = steps * size * experts
    shares, row_tenants = [], []
    for r in range(count):
        flat = packs[r][base:].reshape(-1)
        three = flat[: 3 * number].astype(F32).reshape(3, steps, size, experts)
        shares.append(three[0] + three[1] + three[2])
        row_tenants.append(flat[3 * number : 3 * number + size].astype(jnp.int32))
    share = jnp.concatenate(shares, axis=1)
    share = lax.dynamic_slice_in_dim(share, own, 1, axis=2)
    row_tenant = jnp.concatenate(row_tenants).reshape(count * size, 1)

    holders = own ^ jnp.arange(count, dtype=jnp.int32)
    slots = (holders[:, None] * adapted + jnp.arange(adapted, dtype=jnp.int32)).reshape(-1)
    own_row = lax.dynamic_index_in_dim(pair_slot, own, 0, keepdims=False)
    same = own_row[None, :] == slots[:, None]
    slot_tenant = jnp.max(
        jnp.where(same, jnp.arange(tenants, dtype=jnp.int32)[None, :], -1), axis=1
    )
    slot_tenant = jnp.repeat(slot_tenant, rank).reshape(1, -1)
    shared_tenant = (
        holders[:, None] * own_tenants + jnp.arange(own_tenants, dtype=jnp.int32)
    ).reshape(-1)
    shared_tenant = jnp.repeat(shared_tenant, rank).reshape(1, -1)

    gate_own, up_own = gate_up([tokens.reshape(steps * size, model_width)], shared_gate, shared_up)
    factor_shared = shared_a.reshape(shared_count, model_width)
    factor_store = store_a.reshape(adapted * rank, model_width)
    results = []
    for s in range(steps):
        rows = gathered[s]
        inner = exchange_all(inner_products(rows, factor_shared, factor_store))
        gate, up = gate_up(rows, w_gate[0], w_up[0])
        pieces = down_products(
            gate,
            up,
            gate_own[s * size : (s + 1) * size],
            up_own[s * size : (s + 1) * size],
            inner,
            packs,
            row_tenant,
            slot_tenant,
            shared_tenant,
            share[s],
            routed_down_weight[0],
            shared_down,
            size,
            shared_count,
            n_tensor,
        )
        held = dict(enumerate(pieces))
        bit = 1
        while bit < count:
            for r in sorted([r for r in held if r & bit], reverse=True):
                arrived = swap(held.pop(r), bit)
                held[r ^ bit] = (held[r ^ bit].astype(F32) + arrived.astype(F32)).astype(BF16)
            bit *= 2
        parts = lax.all_to_all(held[0], "tensor", split_axis=0, concat_axis=0, tiled=True)
        results.append(jnp.sum(parts.astype(F32), axis=0).astype(BF16))
    return jnp.stack(results, axis=0)


def solution(mesh):
    return jax.shard_map(
        local,
        mesh=mesh,
        in_specs=(
            P(None, ("groups", "expert"), None),
            P(None, ("groups", "expert"), None),
            P(None, ("groups", "expert"), None),
            P(("groups", "expert")),
            P("expert", None, "tensor"),
            P("expert", None, "tensor"),
            P("expert", "tensor", None),
            P(None, "tensor"),
            P(None, "tensor"),
            P("tensor", None),
            P("expert", None, None),
            P("expert", None, "tensor"),
            P(),
            P("expert", None, None),
            P("expert", None, "tensor"),
        ),
        out_specs=P(None, ("groups", "expert"), "tensor"),
        check_vma=False,
    )
```

```python
import functools

import jax
import jax.numpy as jnp
from jax import lax
from jax.experimental import pallas as pl
from jax.experimental.pallas import tpu as pltpu
from jax.sharding import PartitionSpec as P

F32 = jnp.float32
BF16 = jnp.bfloat16
VMEM_LIMIT = 56 * 1024 * 1024


def params():
    return pltpu.CompilerParams(
        dimension_semantics=("arbitrary",), vmem_limit_bytes=VMEM_LIMIT
    )


def cost(flops, moved):
    return pl.CostEstimate(flops=int(flops), bytes_accessed=int(moved), transcendentals=0)


def swap(value, bits, axis="expert"):
    count = lax.axis_size(axis)
    return lax.ppermute(value, axis, [(i, i ^ bits) for i in range(count)])


def add(one, other):
    return (one.astype(F32) + other.astype(F32)).astype(BF16)


def exchange_all(value):
    count = lax.axis_size("expert")
    pieces = {0: value}
    bit = count // 2
    while bit >= 1:
        pieces.update({r ^ bit: swap(piece, bit) for r, piece in list(pieces.items())})
        bit //= 2
    return [pieces[r] for r in range(count)]


def rows_of(refs):
    return jnp.concatenate([ref[...] for ref in refs], axis=0)


def gate_up_kernel(count, *refs):
    rows, gate_weight, up_weight, gate, up = refs[:count], *refs[count:]

    @pl.when(pl.program_id(0) == 0)
    def _():
        gate[...] = jnp.zeros_like(gate)
        up[...] = jnp.zeros_like(up)

    block = rows_of(rows)
    gate[...] += jnp.dot(block, gate_weight[...], preferred_element_type=F32)
    up[...] += jnp.dot(block, up_weight[...], preferred_element_type=F32)


def gate_up(rows, gate_weight, up_weight):
    depth, width = gate_weight.shape
    size = rows[0].shape[0]
    total = size * len(rows)
    chunk = 1024
    out = jax.ShapeDtypeStruct((total, width), F32)
    return pl.pallas_call(
        functools.partial(gate_up_kernel, len(rows)),
        grid=(depth // chunk,),
        in_specs=[pl.BlockSpec((size, chunk), lambda k: (0, k))] * len(rows)
        + [pl.BlockSpec((chunk, width), lambda k: (k, 0))] * 2,
        out_specs=[pl.BlockSpec((total, width), lambda k: (0, 0))] * 2,
        out_shape=[out, out],
        compiler_params=params(),
        cost_estimate=cost(4 * total * depth * width, 4 * depth * width),
    )(*rows, gate_weight, up_weight)


def inner_kernel(count, *refs):
    rows, factor_shared, factor_store, inner, total = refs[:count], *refs[count:]

    @pl.when(pl.program_id(0) == 0)
    def _():
        total[...] = jnp.zeros_like(total)

    block = rows_of(rows)
    factors = jnp.concatenate([factor_shared[...], factor_store[...]], axis=0)
    total[...] += lax.dot_general(
        block, factors, (((1,), (1,)), ((), ())), preferred_element_type=F32
    )

    @pl.when(pl.program_id(0) == pl.num_programs(0) - 1)
    def _():
        inner[...] = total[...].astype(BF16)


def inner_products(rows, factor_shared, factor_store):
    depth = factor_shared.shape[1]
    size = rows[0].shape[0]
    total = size * len(rows)
    shared_count, store_count = factor_shared.shape[0], factor_store.shape[0]
    width = shared_count + store_count
    chunk = 1792
    return pl.pallas_call(
        functools.partial(inner_kernel, len(rows)),
        grid=(depth // chunk,),
        in_specs=[pl.BlockSpec((size, chunk), lambda k: (0, k))] * len(rows)
        + [
            pl.BlockSpec((shared_count, chunk), lambda k: (0, k)),
            pl.BlockSpec((store_count, chunk), lambda k: (0, k)),
        ],
        out_specs=pl.BlockSpec((total, width), lambda k: (0, 0)),
        out_shape=jax.ShapeDtypeStruct((total, width), BF16),
        scratch_shapes=[pltpu.VMEM((total, width), F32)],
        compiler_params=params(),
        cost_estimate=cost(2 * total * depth * width, 2 * depth * width),
    )(*rows, factor_shared, factor_store)


def silu(value):
    return value / (1.0 + jnp.exp(-value))


def down_kernel(count, size, shared_count, order, place, *refs):
    gate, up, gate_own, up_own = refs[:4]
    inner = refs[4 : 4 + count]
    factors = refs[4 + count : 4 + 2 * count]
    row_tenant, slot_tenant, shared_tenant, share, down, down_own, keep, send = refs[
        4 + 2 * count : 12 + 2 * count
    ]
    hidden, hidden_own = refs[12 + 2 * count :]

    @pl.when(pl.program_id(0) == 0)
    def _():
        width = inner[0].shape[1]
        parts, parts_own = [], []
        for r in range(count):
            held = inner[r][...]
            blocks = [held[(k ^ r) * size : ((k ^ r) + 1) * size] for k in range(count)]
            parts.append(jnp.concatenate(blocks, axis=0)[:, shared_count:])
            parts_own.append(blocks[0][:, :shared_count])
        lifted = jnp.concatenate(parts, axis=1)
        lifted_own = jnp.concatenate(parts_own, axis=1)
        tenants = row_tenant[...]
        zero = jnp.zeros((), BF16)
        lifted = jnp.where(tenants == slot_tenant[...], lifted, zero)
        lifted_own = jnp.where(tenants[:size] == shared_tenant[...], lifted_own, zero)
        factor = jnp.concatenate([ref[shared_count:width] for ref in factors], axis=0)
        factor_own = jnp.concatenate([ref[:shared_count] for ref in factors], axis=0)
        upward = up[...] + jnp.dot(lifted, factor, preferred_element_type=F32)
        hidden[...] = (silu(gate[...]) * upward).astype(BF16)
        upward_own = up_own[...] + jnp.dot(lifted_own, factor_own, preferred_element_type=F32)
        hidden_own[...] = (silu(gate_own[...]) * upward_own).astype(BF16)

    routed = jnp.dot(hidden[...], down[...], preferred_element_type=F32) * share[...]
    own = jnp.dot(hidden_own[...], down_own[...], preferred_element_type=F32)
    half = count // 2
    for place_of, r in enumerate(order):
        block = routed[r * size : (r + 1) * size]
        if r == 0:
            block = block + own
        target, row = (keep, place_of) if place_of < half else (send, place_of - half)
        target[0, row] = block.astype(BF16)


def down_products(
    gate, up, gate_own, up_own, inner, factors, row_tenant, slot_tenant, shared_tenant, share,
    down, down_own, place, first, blocks, parts, order, shared_count,
):
    count = len(inner)
    total, hid = gate.shape
    size = total // count
    depth = down.shape[1]
    part = depth // parts
    whole = [gate, up, gate_own, up_own, *inner, *factors, row_tenant, slot_tenant, shared_tenant, share]
    out = jax.ShapeDtypeStruct((blocks, count // 2, size, part), BF16)
    return pl.pallas_call(
        functools.partial(down_kernel, count, size, shared_count, order),
        grid_spec=pltpu.PrefetchScalarGridSpec(
            num_scalar_prefetch=1,
            grid=(blocks,),
            in_specs=[pl.BlockSpec(x.shape, lambda j, place: (0, 0)) for x in whole]
            + [pl.BlockSpec((hid, part), lambda j, place: (0, (first + j) ^ place[0]))] * 2,
            out_specs=[pl.BlockSpec((1, count // 2, size, part), lambda j, place: (j, 0, 0, 0))] * 2,
            scratch_shapes=[pltpu.VMEM((total, hid), BF16), pltpu.VMEM((size, hid), BF16)],
        ),
        out_shape=[out, out],
        compiler_params=params(),
        cost_estimate=cost(
            2 * (total + size) * part * blocks * hid, 4 * part * blocks * hid
        ),
    )(place, *whole, down, down_own)


def split3(value):
    first = lax.reduce_precision(value, 8, 7)
    second = lax.reduce_precision(value - first, 8, 7)
    return jnp.stack([first, second, value - first - second]).astype(BF16)


def local(
    tokens,
    expert_ids,
    gate_values,
    tenant_ids,
    w_gate,
    w_up,
    routed_down_weight,
    shared_gate,
    shared_up,
    shared_down,
    store_a,
    store_b,
    pair_slot,
    shared_a,
    shared_b,
):
    experts, tenants = pair_slot.shape
    adapted, rank, model_width = store_a.shape
    own_tenants = shared_a.shape[0]
    hid = store_b.shape[2]
    steps, size, _ = expert_ids.shape
    count = lax.axis_size("expert")
    n_tensor = lax.axis_size("tensor")
    own = lax.axis_index("expert")
    shared_count = own_tenants * rank

    rows_own = tokens.reshape(steps * size, model_width)
    rows = exchange_all(rows_own)

    hits = expert_ids[..., None] == jnp.arange(experts, dtype=jnp.int32)
    dense = jnp.sum(jnp.where(hits, gate_values[..., None], 0.0), axis=2)
    dense = dense.reshape(steps * size * experts)
    extra = jnp.concatenate([split3(dense).reshape(-1), tenant_ids.astype(BF16)])
    extra_rows = -(-extra.shape[0] // (16 * hid)) * 16
    extra = jnp.pad(extra, (0, extra_rows * hid - extra.shape[0])).reshape(extra_rows, hid)
    pack = jnp.concatenate(
        [shared_b.reshape(shared_count, hid), store_b.reshape(adapted * rank, hid), extra], axis=0
    )
    packs = exchange_all(pack)
    base = shared_count + adapted * rank
    number = steps * size * experts
    shares, row_tenants = [], []
    for r in range(count):
        flat = packs[r][base:].reshape(-1)
        three = flat[: 3 * number].astype(F32).reshape(3, steps * size, experts)
        shares.append(three[0] + three[1] + three[2])
        row_tenants += [flat[3 * number : 3 * number + size].astype(jnp.int32)] * steps
    share = jnp.concatenate(shares, axis=0)
    share = lax.dynamic_slice_in_dim(share, own, 1, axis=1)
    row_tenant = jnp.concatenate(row_tenants).reshape(count * steps * size, 1)

    holders = own ^ jnp.arange(count, dtype=jnp.int32)
    slots = (holders[:, None] * adapted + jnp.arange(adapted, dtype=jnp.int32)).reshape(-1)
    own_row = lax.dynamic_index_in_dim(pair_slot, own, 0, keepdims=False)
    same = own_row[None, :] == slots[:, None]
    slot_tenant = jnp.max(
        jnp.where(same, jnp.arange(tenants, dtype=jnp.int32)[None, :], -1), axis=1
    )
    slot_tenant = jnp.repeat(slot_tenant, rank).reshape(1, -1)
    shared_tenant = (
        holders[:, None] * own_tenants + jnp.arange(own_tenants, dtype=jnp.int32)
    ).reshape(-1)
    shared_tenant = jnp.repeat(shared_tenant, rank).reshape(1, -1)

    gate_own, up_own = gate_up([rows_own], shared_gate, shared_up)
    inner = inner_products(
        rows,
        shared_a.reshape(shared_count, model_width),
        store_a.reshape(adapted * rank, model_width),
    )
    inners = [inner] + [swap(inner, r) for r in range(1, count)]
    gate, up = gate_up(rows, w_gate[0], w_up[0])

    order = [0]
    bit = count // 2
    while bit >= 1:
        order = order + [r | bit for r in order]
        bit //= 2
    place = lax.axis_index("tensor").astype(jnp.int32).reshape(1)
    columns = {}
    group = max(1, n_tensor // 2)
    for first in range(n_tensor - group, -1, -group):
        keep, send = down_products(
            gate, up, gate_own, up_own, inners, packs, row_tenant, slot_tenant, shared_tenant,
            share, routed_down_weight[0], shared_down, place, first, group, n_tensor, order,
            shared_count,
        )
        for j in range(group - 1, -1, -1):
            held, leaving = keep[j], send[j]
            bit = 1
            while bit < count:
                arrived = swap(leaving, bit)
                half = held.shape[0] // 2
                leaving = add(held[half:], arrived[half:])
                held = add(held[:half], arrived[:half])
                bit *= 2
            columns[first + j] = leaving[0]
    bit = 1
    while bit < n_tensor:
        for j in sorted([j for j in columns if j & bit], reverse=True):
            columns[j ^ bit] = add(columns[j ^ bit], swap(columns.pop(j), bit, "tensor"))
        bit *= 2
    return columns[0].reshape(steps, size, model_width // n_tensor)


def solution(mesh):
    return jax.shard_map(
        local,
        mesh=mesh,
        in_specs=(
            P(None, ("groups", "expert"), None),
            P(None, ("groups", "expert"), None),
            P(None, ("groups", "expert"), None),
            P(("groups", "expert")),
            P("expert", None, "tensor"),
            P("expert", None, "tensor"),
            P("expert", "tensor", None),
            P(None, "tensor"),
            P(None, "tensor"),
            P("tensor", None),
            P("expert", None, None),
            P("expert", None, "tensor"),
            P(),
            P("expert", None, None),
            P("expert", None, "tensor"),
        ),
        out_specs=P(None, ("groups", "expert"), "tensor"),
        check_vma=False,
    )
```

```python
import functools

import jax
import jax.numpy as jnp
from jax import lax
from jax.experimental import pallas as pl
from jax.experimental.pallas import tpu as pltpu
from jax.sharding import PartitionSpec as P

F32 = jnp.float32
BF16 = jnp.bfloat16
MIB = 1024 * 1024


def params(mebibytes):
    return pltpu.CompilerParams(vmem_limit_bytes=mebibytes * MIB)


def cost(flops, moved):
    return pl.CostEstimate(flops=int(flops), bytes_accessed=int(moved), transcendentals=0)


def in_vmem(value):
    return pltpu.with_memory_space_constraint(value, pltpu.VMEM)


def in_hbm(value):
    return pltpu.with_memory_space_constraint(value, pltpu.HBM)


def vmem_shape(value):
    return pltpu.VMEM(value.shape, value.dtype)


VMEM_SPEC = pl.BlockSpec(memory_space=pltpu.VMEM)
HBM_SPEC = pl.BlockSpec(memory_space=pltpu.HBM)
SMEM_SPEC = pl.BlockSpec(memory_space=pltpu.SMEM)


def swap(value, bits, axis="expert"):
    count = lax.axis_size(axis)
    return lax.ppermute(value, axis, [(i, i ^ bits) for i in range(count)])


def add(one, other):
    return (one.astype(F32) + other.astype(F32)).astype(BF16)


def exchange_all(values, after):
    count = lax.axis_size("expert")
    bit = count // 2
    arrived = [swap(value, bit) for value in values]
    arrived, after = lax.optimization_barrier((arrived, after))
    pieces = {0: values, bit: arrived}
    bit //= 2
    while bit >= 1:
        for r, piece in list(pieces.items()):
            pieces[r ^ bit] = [swap(value, bit) for value in piece]
        bit //= 2
    return *zip(*[pieces[r] for r in range(count)]), after


def tile_of(width):
    return 256 if width % 256 == 0 else 128


def pack_kernel(experts, ids, values, tenants, shared_b, store_b, pack):
    shared_count, width = shared_b.shape
    store_count = store_b.shape[0]
    count, top = ids.shape
    pack[:shared_count] = shared_b[...]
    pack[shared_count : shared_count + store_count] = store_b[...]
    lane = lax.broadcasted_iota(jnp.int32, (count, width), 1)
    expert = lane % experts
    weight = jnp.zeros((count, width), F32)
    for k in range(top):
        weight = weight + jnp.where(ids[:, k : k + 1] == expert, values[:, k : k + 1], 0.0)
    first = weight.astype(BF16).astype(F32)
    second = (weight - first).astype(BF16).astype(F32)
    third = weight - first - second
    meta = jnp.where(lane < experts, first, jnp.where(lane < 2 * experts, second, third))
    meta = jnp.where(lane < 3 * experts, meta, tenants[...].astype(F32))
    pack[shared_count + store_count :] = meta.astype(BF16)


def make_pack(experts, ids, values, tenants, shared_b, store_b):
    rows = ids.shape[0] + shared_b.shape[0] + store_b.shape[0]
    return pl.pallas_call(
        functools.partial(pack_kernel, experts),
        in_specs=[VMEM_SPEC] * 5,
        out_specs=VMEM_SPEC,
        out_shape=jax.ShapeDtypeStruct((rows, shared_b.shape[1]), BF16),
        compiler_params=params(4),
        cost_estimate=cost(1e5, 2e5),
    )(ids, values, tenants, shared_b, store_b)


def first_kernel(pieces, rows, gate_weight, up_weight, *refs):
    staged = len(refs) // 2 - 3
    sources = refs[:staged]
    gate, up = refs[staged : staged + 2]
    targets = refs[staged + 2 : 2 * staged + 2]
    gate_held, up_held, sems, staged_sems = refs[2 * staged + 2 :]
    depth, width = gate_weight.shape
    chunk = depth // pieces
    copies = []
    for k in range(pieces):
        part = pl.ds(k * chunk, chunk)
        pair = [
            pltpu.make_async_copy(gate_weight.at[part], gate_held.at[part], sems.at[0, k]),
            pltpu.make_async_copy(up_weight.at[part], up_held.at[part], sems.at[1, k]),
        ]
        for copy in pair:
            copy.start()
        copies.append(pair)
    staging = []
    for n in range(staged):
        size = sources[n].shape[0] // STAGE_PIECES
        for k in range(STAGE_PIECES):
            part = pl.ds(k * size, size)
            copy = pltpu.make_async_copy(
                sources[n].at[part], targets[n].at[part], staged_sems.at[n, k]
            )
            copy.start()
            staging.append(copy)
    total_gate = jnp.zeros(gate.shape, F32)
    total_up = jnp.zeros(up.shape, F32)
    for k in range(pieces):
        part = pl.ds(k * chunk, chunk)
        for copy in copies[k]:
            copy.wait()
        block = rows[:, part]
        total_gate += jnp.dot(block, gate_held[part], preferred_element_type=F32)
        total_up += jnp.dot(block, up_held[part], preferred_element_type=F32)
    gate[...] = total_gate
    up[...] = total_up
    for copy in staging:
        copy.wait()


STAGE_PIECES = 4


def first_products(rows, gate_weight, up_weight, weights):
    depth, width = gate_weight.shape
    pieces = 7
    out = jax.ShapeDtypeStruct((rows.shape[0], width), F32)
    moved = 2 * depth * width * (2 + len(weights))
    return pl.pallas_call(
        functools.partial(first_kernel, pieces),
        in_specs=[VMEM_SPEC] + [HBM_SPEC] * (2 + len(weights)),
        out_specs=[VMEM_SPEC] * (2 + len(weights)),
        out_shape=[out, out] + [vmem_shape(w) for w in weights],
        scratch_shapes=[
            pltpu.VMEM((depth, width), BF16),
            pltpu.VMEM((depth, width), BF16),
            pltpu.SemaphoreType.DMA((2, pieces)),
            pltpu.SemaphoreType.DMA((len(weights), STAGE_PIECES)),
        ],
        compiler_params=params(12),
        cost_estimate=cost(4 * rows.shape[0] * depth * width, moved),
    )(in_vmem(rows), *[in_hbm(w) for w in (gate_weight, up_weight, *weights)])


def inner_kernel(count, chunk, *refs):
    rows, factor_shared, factor_store, inner = refs[:count], *refs[count:]
    depth = factor_shared.shape[1]
    size = rows[0].shape[0]
    split = factor_shared.shape[0]
    width = split + factor_store.shape[0]
    total = jnp.zeros((count * size, width), F32)
    for k in range(depth // chunk):
        part = pl.ds(k * chunk, chunk)
        block = jnp.concatenate([ref[:, part] for ref in rows], axis=0)
        factors = jnp.concatenate([factor_shared[:, part], factor_store[:, part]], axis=0)
        total += lax.dot_general(
            block, factors, (((1,), (1,)), ((), ())), preferred_element_type=F32
        )
    inner[...] = total.astype(BF16)


def inner_products(rows, factor_shared, factor_store):
    depth = factor_shared.shape[1]
    total = rows[0].shape[0] * len(rows)
    width = factor_shared.shape[0] + factor_store.shape[0]
    return pl.pallas_call(
        functools.partial(inner_kernel, len(rows), 1024),
        in_specs=[VMEM_SPEC] * (len(rows) + 2),
        out_specs=VMEM_SPEC,
        out_shape=jax.ShapeDtypeStruct((total, width), BF16),
        compiler_params=params(12),
        cost_estimate=cost(2 * total * depth * width, 2 * depth * width),
    )(*[in_vmem(x) for x in (*rows, factor_shared, factor_store)])


def gate_up_kernel(count, chunk, *refs):
    rows, gate_weight, up_weight, gate, up = refs[:count], *refs[count:]
    depth = gate_weight.shape[0]
    total_gate = jnp.zeros(gate.shape, F32)
    total_up = jnp.zeros(up.shape, F32)
    for k in range(depth // chunk):
        part = pl.ds(k * chunk, chunk)
        block = jnp.concatenate([ref[:, part] for ref in rows], axis=0)
        total_gate += jnp.dot(block, gate_weight[part], preferred_element_type=F32)
        total_up += jnp.dot(block, up_weight[part], preferred_element_type=F32)
    gate[...] = total_gate
    up[...] = total_up


def gate_up(rows, gate_weight, up_weight):
    depth, width = gate_weight.shape
    total = rows[0].shape[0] * len(rows)
    out = jax.ShapeDtypeStruct((total, width), F32)
    return pl.pallas_call(
        functools.partial(gate_up_kernel, len(rows), 1024),
        in_specs=[VMEM_SPEC] * (len(rows) + 2),
        out_specs=[VMEM_SPEC] * 2,
        out_shape=[out, out],
        compiler_params=params(12),
        cost_estimate=cost(4 * total * depth * width, 4 * depth * width),
    )(*[in_vmem(x) for x in (*rows, gate_weight, up_weight)])


def silu(value):
    return value / (1.0 + jnp.exp(-value))


def down_kernel(count, shared_count, store_count, experts, adapted, chunks, order, *refs):
    place, pair_slot, gate, up, gate_own, up_own = refs[:6]
    inner = refs[6 : 6 + count]
    packs = refs[6 + count : 6 + 2 * count]
    down, down_own = refs[6 + 2 * count : 8 + 2 * count]
    outs = refs[8 + 2 * count :]
    own, own_part = place[0], place[1]
    total, hid = gate.shape
    size = total // count
    half = count // 2
    width = shared_count + store_count
    tenants = pair_slot.shape[1]

    meta = jnp.concatenate([ref[width:] for ref in packs], axis=0).astype(F32)
    lane = lax.broadcasted_iota(jnp.int32, meta.shape, 1)
    mine = (lane < 3 * experts) & (lane % experts == own)
    share = jnp.sum(jnp.where(mine, meta, 0.0), axis=1, keepdims=True)
    row_tenant = jnp.sum(jnp.where(lane == 3 * experts, meta, 0.0), axis=1, keepdims=True)
    row_tenant = row_tenant.astype(jnp.int32)

    column = lax.broadcasted_iota(jnp.int32, (1, count * shared_count), 1)
    rank = store_count // adapted
    own_tenants = shared_count // rank
    shared_tenant = (own ^ (column // shared_count)) * own_tenants + (column % shared_count) // rank
    column = lax.broadcasted_iota(jnp.int32, (1, count * store_count), 1)
    slot = (own ^ (column // store_count)) * adapted + (column % store_count) // rank
    slot_tenant = jnp.full(slot.shape, -1, jnp.int32)
    for t in range(tenants):
        slot_tenant = jnp.where(slot == pair_slot[own, t], t, slot_tenant)

    parts, parts_own = [], []
    for r in range(count):
        held = inner[r][...]
        blocks = [held[(k ^ r) * size : ((k ^ r) + 1) * size] for k in range(count)]
        parts.append(jnp.concatenate(blocks, axis=0)[:, shared_count:])
        parts_own.append(blocks[0][:, :shared_count])
    lifted = jnp.concatenate(parts, axis=1)
    lifted_own = jnp.concatenate(parts_own, axis=1)
    zero = jnp.zeros((), BF16)
    lifted = jnp.where(row_tenant == slot_tenant, lifted, zero)
    lifted_own = jnp.where(row_tenant[:size] == shared_tenant, lifted_own, zero)
    factor = jnp.concatenate([ref[shared_count:width] for ref in packs], axis=0)
    factor_own = jnp.concatenate([ref[:shared_count] for ref in packs], axis=0)
    upward = up[...] + jnp.dot(lifted, factor, preferred_element_type=F32)
    hidden = (silu(gate[...]) * upward).astype(BF16)
    upward_own = up_own[...] + jnp.dot(lifted_own, factor_own, preferred_element_type=F32)
    hidden_own = (silu(gate_own[...]) * upward_own).astype(BF16)

    part = outs[0].shape[-1]
    tile = tile_of(part)
    for n, chunk in enumerate(chunks):
        keep, send = outs[2 * n : 2 * n + 2]
        for place_in, j in enumerate(chunk):
            start = (own_part ^ j) * part
            for c in range(part // tile):
                columns = pl.ds(pl.multiple_of(start + c * tile, tile), tile)
                routed = jnp.dot(hidden, down[:, columns], preferred_element_type=F32) * share
                shared = jnp.dot(hidden_own, down_own[:, columns], preferred_element_type=F32)
                for at, r in enumerate(order):
                    block = routed[r * size : (r + 1) * size]
                    if r == 0:
                        block = block + shared
                    target, row = (keep, at) if at < half else (send, at - half)
                    target[row, place_in, :, c * tile : (c + 1) * tile] = block.astype(BF16)


def down_products(
    place, pair_slot, gate, up, gate_own, up_own, inner, packs, down, down_own, experts,
    adapted, chunks, order, shared_count, store_count, parts,
):
    count = len(inner)
    total, hid = gate.shape
    size = total // count
    depth = down.shape[1]
    part = depth // parts
    whole = [gate, up, gate_own, up_own, *inner, *packs, down, down_own]
    outs = []
    for chunk in chunks:
        outs += [jax.ShapeDtypeStruct((count // 2, len(chunk), size, part), BF16)] * 2
    return pl.pallas_call(
        functools.partial(
            down_kernel, count, shared_count, store_count, experts, adapted, chunks, order
        ),
        in_specs=[SMEM_SPEC] * 2 + [VMEM_SPEC] * len(whole),
        out_specs=[VMEM_SPEC] * len(outs),
        out_shape=outs,
        compiler_params=params(16),
        cost_estimate=cost(2 * (total + size) * depth * hid, 4 * depth * hid),
    )(place, pair_slot, *[in_vmem(x) for x in whole])


def local(
    tokens,
    expert_ids,
    gate_values,
    tenant_ids,
    w_gate,
    w_up,
    routed_down_weight,
    shared_gate,
    shared_up,
    shared_down,
    store_a,
    store_b,
    pair_slot,
    shared_a,
    shared_b,
):
    experts = pair_slot.shape[0]
    adapted, rank, model_width = store_a.shape
    own_tenants = shared_a.shape[0]
    hid = store_b.shape[2]
    steps, size, top_count = expert_ids.shape
    count = lax.axis_size("expert")
    n_tensor = lax.axis_size("tensor")
    own = lax.axis_index("expert")
    shared_count, store_count = own_tenants * rank, adapted * rank

    rows_own = tokens.reshape(steps * size, model_width)
    pack = make_pack(
        experts,
        expert_ids.reshape(steps * size, top_count),
        gate_values.reshape(steps * size, top_count),
        jnp.tile(tenant_ids[:, None], (steps, 1)),
        shared_b.reshape(shared_count, hid),
        store_b.reshape(store_count, hid),
    )
    rows_first, pack = lax.optimization_barrier((rows_own, pack))
    first = first_products(
        rows_first, shared_gate, shared_up, [w_gate[0], w_up[0], routed_down_weight[0], shared_down]
    )
    rows, packs, first = exchange_all([rows_own, pack], first)
    gate_own, up_own, gate_weight, up_weight, down, down_own = first
    inner = inner_products(
        rows,
        shared_a.reshape(shared_count, model_width),
        store_a.reshape(store_count, model_width),
    )
    inners = [inner] + [swap(inner, r) for r in range(1, count)]
    gate, up = gate_up(rows, gate_weight, up_weight)

    order = [0]
    bit = count // 2
    while bit >= 1:
        order = order + [r | bit for r in order]
        bit //= 2
    chunks = [[j] for j in range(n_tensor - 1, 1, -1)] + [[1, 0]]
    place = jnp.stack([own, lax.axis_index("tensor")]).astype(jnp.int32)
    outs = down_products(
        place, pair_slot, gate, up, gate_own, up_own, inners, packs, down, down_own, experts,
        adapted, chunks, order, shared_count, store_count, n_tensor,
    )
    arrived_parts = []
    for n, chunk in enumerate(chunks):
        held, leaving = outs[2 * n : 2 * n + 2]
        bit = 1
        while bit < count:
            arrived = swap(leaving, bit)
            half = held.shape[0] // 2
            leaving = add(held[half:], arrived[half:])
            held = add(held[:half], arrived[:half])
            bit *= 2
        for place_in, j in enumerate(chunk):
            value = leaving[0, place_in]
            arrived_parts.append(swap(value, j, "tensor") if j else value)
    total = sum(value.astype(F32) for value in arrived_parts)
    return total.astype(BF16).reshape(steps, size, model_width // n_tensor)


def solution(mesh):
    return jax.shard_map(
        local,
        mesh=mesh,
        in_specs=(
            P(None, ("groups", "expert"), None),
            P(None, ("groups", "expert"), None),
            P(None, ("groups", "expert"), None),
            P(("groups", "expert")),
            P("expert", None, "tensor"),
            P("expert", None, "tensor"),
            P("expert", "tensor", None),
            P(None, "tensor"),
            P(None, "tensor"),
            P("tensor", None),
            P("expert", None, None),
            P("expert", None, "tensor"),
            P(),
            P("expert", None, None),
            P("expert", None, "tensor"),
        ),
        out_specs=P(None, ("groups", "expert"), "tensor"),
        check_vma=False,
    )
```

```python
import functools

import jax
import jax.numpy as jnp
from jax import lax
from jax.experimental import pallas as pl
from jax.experimental.pallas import tpu as pltpu
from jax.sharding import PartitionSpec as P

F32 = jnp.float32
BF16 = jnp.bfloat16
MIB = 1024 * 1024


def params(mebibytes):
    return pltpu.CompilerParams(vmem_limit_bytes=mebibytes * MIB)


def cost(flops, moved):
    return pl.CostEstimate(flops=int(flops), bytes_accessed=int(moved), transcendentals=0)


def in_vmem(value):
    return pltpu.with_memory_space_constraint(value, pltpu.VMEM)


def in_hbm(value):
    return pltpu.with_memory_space_constraint(value, pltpu.HBM)


def vmem_shape(value):
    return pltpu.VMEM(value.shape, value.dtype)


VMEM_SPEC = pl.BlockSpec(memory_space=pltpu.VMEM)
HBM_SPEC = pl.BlockSpec(memory_space=pltpu.HBM)


def swap(value, bits, axis="expert"):
    count = lax.axis_size(axis)
    return lax.ppermute(value, axis, [(i, i ^ bits) for i in range(count)])


def add(one, other):
    return (one.astype(F32) + other.astype(F32)).astype(BF16)


def exchange_rest(value, arrived):
    count = lax.axis_size("expert")
    bit = count // 2
    pieces = {0: value, bit: arrived}
    bit //= 2
    while bit >= 1:
        pieces.update({r ^ bit: swap(piece, bit) for r, piece in list(pieces.items())})
        bit //= 2
    return [pieces[r] for r in range(count)]


def tile_of(width):
    return 256 if width % 256 == 0 else 128


def column_of(row, size):
    lane = lax.broadcasted_iota(jnp.int32, (size, row.shape[1]), 1)
    place = lax.broadcasted_iota(jnp.int32, (size, row.shape[1]), 0)
    return jnp.sum(jnp.where(lane == place, row.astype(F32), 0.0), axis=1, keepdims=True)


def first_kernel(
    experts, pieces, rows, gate_weight, up_weight, ids, values, tenants, pair_slot, shared_b,
    store_b, factor_shared, factor_store, gate_weight_routed, up_weight_routed, down, down_own,
    gate, up, pack, columns, rows_out, factor_shared_out, factor_store_out, gate_out, up_out,
    down_out, down_own_out, gate_held, up_held, ids_held, values_held, tenants_held,
    pair_slot_held, small_sems, sems, stage_sems,
):
    own, own_part = lax.axis_index("expert"), lax.axis_index("tensor")
    parts = lax.axis_size("tensor")
    depth = gate_weight.shape[0]
    shared_count, width = shared_b.shape
    store_count = store_b.shape[0]
    base = shared_count + store_count

    small = [
        (rows, rows_out),
        (ids, ids_held),
        (values, values_held),
        (tenants, tenants_held),
        (pair_slot, pair_slot_held),
        (shared_b, pack.at[pl.ds(0, shared_count)]),
        (store_b, pack.at[pl.ds(shared_count, store_count)]),
    ]
    small = [
        pltpu.make_async_copy(source, target, small_sems.at[n])
        for n, (source, target) in enumerate(small)
    ]
    for copy in small:
        copy.start()
    chunk = depth // pieces
    copies = []
    for k in range(pieces):
        part = pl.ds(k * chunk, chunk)
        pair = [
            pltpu.make_async_copy(gate_weight.at[part], gate_held.at[part], sems.at[0, k]),
            pltpu.make_async_copy(up_weight.at[part], up_held.at[part], sems.at[1, k]),
        ]
        for copy in pair:
            copy.start()
        copies.append(pair)
    staged = [(factor_shared, factor_shared_out), (factor_store, factor_store_out)]
    for source, target in ((gate_weight_routed, gate_out), (up_weight_routed, up_out)):
        piece = depth // parts
        for k in range(parts):
            part = pl.ds(k * piece, piece)
            staged.append((source.at[part], target.at[part]))
    piece = depth // parts
    for source, target in ((down, down_out), (down_own, down_own_out)):
        for j in range(parts):
            start = pl.multiple_of((own_part ^ j) * piece, piece)
            staged.append((source.at[:, pl.ds(start, piece)], target.at[:, pl.ds(j * piece, piece)]))
    staged = [
        pltpu.make_async_copy(source, target, stage_sems.at[n])
        for n, (source, target) in enumerate(staged)
    ]
    for copy in staged:
        copy.start()
    for copy in small:
        copy.wait()

    steps, top, size = ids_held.shape
    tenant = column_of(tenants_held[...], size)
    lane = lax.broadcasted_iota(jnp.int32, (size, width), 1)
    for s in range(steps):
        weight = jnp.zeros((size, width), F32)
        for k in range(top):
            expert = column_of(ids_held[s, k : k + 1], size).astype(jnp.int32)
            value = column_of(values_held[s, k : k + 1], size)
            weight = weight + jnp.where(expert == lane % experts, value, 0.0)
        high = weight.astype(BF16).astype(F32)
        middle = (weight - high).astype(BF16).astype(F32)
        low = weight - high - middle
        meta = jnp.where(lane < experts, high, jnp.where(lane < 2 * experts, middle, low))
        meta = jnp.where(lane < 3 * experts, meta, tenant)
        pack[base + s * size : base + (s + 1) * size] = meta.astype(BF16)

    tenant_count = pair_slot_held.shape[1]
    place = lax.broadcasted_iota(jnp.int32, pair_slot_held.shape, 0)
    own_row = jnp.sum(
        jnp.where(place == own, pair_slot_held[...].astype(F32), 0.0), axis=0, keepdims=True
    )
    own_slots = column_of(own_row, tenant_count).astype(jnp.int32)
    total = columns.shape[1]
    per_device = tenant_count // lax.axis_size("expert")
    rank = shared_count // per_device
    column = lax.broadcasted_iota(jnp.int32, (1, total), 1)
    shared_tenant = (own ^ (column // shared_count)) * per_device + column % shared_count // rank
    slot = (own ^ (column // store_count)) * (store_count // rank) + column % store_count // rank
    tenant_number = lax.broadcasted_iota(jnp.int32, (tenant_count, total), 0)
    slot_tenant = jnp.max(jnp.where(own_slots == slot, tenant_number, -1), axis=0, keepdims=True)
    columns[0:1] = shared_tenant
    columns[1:2] = slot_tenant
    columns[2:3] = jnp.full((1, total), own, jnp.int32)
    columns[3:8] = jnp.zeros((5, total), jnp.int32)

    total_gate = jnp.zeros(gate.shape, F32)
    total_up = jnp.zeros(up.shape, F32)
    for k in range(pieces):
        part = pl.ds(k * chunk, chunk)
        for copy in copies[k]:
            copy.wait()
        block = rows_out[:, part]
        total_gate += jnp.dot(block, gate_held[part], preferred_element_type=F32)
        total_up += jnp.dot(block, up_held[part], preferred_element_type=F32)
    gate[...] = total_gate
    up[...] = total_up
    for copy in staged:
        copy.wait()


def first_products(
    experts, rows, gate_weight, up_weight, ids, values, tenants, pair_slot, shared_b, store_b,
    staged,
):
    depth, width = gate_weight.shape
    count, parts = lax.axis_size("expert"), lax.axis_size("tensor")
    pieces = 7
    product = jax.ShapeDtypeStruct((rows.shape[0], width), F32)
    pack = jax.ShapeDtypeStruct(
        (shared_b.shape[0] + store_b.shape[0] + rows.shape[0], width), BF16
    )
    columns = count * max(shared_b.shape[0], store_b.shape[0])
    columns = jax.ShapeDtypeStruct((8, columns), jnp.int32)
    inputs = [
        rows, gate_weight, up_weight, ids, values, tenants, pair_slot, shared_b, store_b, *staged
    ]
    moved = sum(value.size * 2 for value in (rows, gate_weight, up_weight, *staged))
    outs = [product, product, pack, columns, *[vmem_shape(value) for value in (rows, *staged)]]
    return pl.pallas_call(
        functools.partial(first_kernel, experts, pieces),
        in_specs=[HBM_SPEC] * len(inputs),
        out_specs=[VMEM_SPEC] * len(outs),
        out_shape=outs,
        scratch_shapes=[
            pltpu.VMEM((depth, width), BF16),
            pltpu.VMEM((depth, width), BF16),
            pltpu.VMEM(ids.shape, jnp.int32),
            pltpu.VMEM(values.shape, F32),
            pltpu.VMEM(tenants.shape, jnp.int32),
            pltpu.VMEM(pair_slot.shape, jnp.int32),
            pltpu.SemaphoreType.DMA((7,)),
            pltpu.SemaphoreType.DMA((2, pieces)),
            pltpu.SemaphoreType.DMA((2 + 4 * parts,)),
        ],
        compiler_params=params(12),
        cost_estimate=cost(4 * rows.shape[0] * depth * width, moved),
    )(*[in_hbm(value) for value in inputs])


def inner_kernel(count, chunk, *refs):
    rows, factor_shared, factor_store, inner = refs[:count], *refs[count:]
    depth = factor_shared.shape[1]
    size = rows[0].shape[0]
    split = factor_shared.shape[0]
    width = split + factor_store.shape[0]
    total = jnp.zeros((count * size, width), F32)
    for k in range(depth // chunk):
        part = pl.ds(k * chunk, chunk)
        block = jnp.concatenate([ref[:, part] for ref in rows], axis=0)
        factors = jnp.concatenate([factor_shared[:, part], factor_store[:, part]], axis=0)
        total += lax.dot_general(
            block, factors, (((1,), (1,)), ((), ())), preferred_element_type=F32
        )
    inner[...] = total.astype(BF16)


def inner_products(rows, factor_shared, factor_store):
    depth = factor_shared.shape[1]
    total = rows[0].shape[0] * len(rows)
    width = factor_shared.shape[0] + factor_store.shape[0]
    return pl.pallas_call(
        functools.partial(inner_kernel, len(rows), 1024),
        in_specs=[VMEM_SPEC] * (len(rows) + 2),
        out_specs=VMEM_SPEC,
        out_shape=jax.ShapeDtypeStruct((total, width), BF16),
        compiler_params=params(12),
        cost_estimate=cost(2 * total * depth * width, 2 * depth * width),
    )(*[in_vmem(x) for x in (*rows, factor_shared, factor_store)])


def gate_up_kernel(count, chunk, *refs):
    rows, gate_weight, up_weight, gate, up = refs[:count], *refs[count:]
    depth = gate_weight.shape[0]
    total_gate = jnp.zeros(gate.shape, F32)
    total_up = jnp.zeros(up.shape, F32)
    for k in range(depth // chunk):
        part = pl.ds(k * chunk, chunk)
        block = jnp.concatenate([ref[:, part] for ref in rows], axis=0)
        total_gate += jnp.dot(block, gate_weight[part], preferred_element_type=F32)
        total_up += jnp.dot(block, up_weight[part], preferred_element_type=F32)
    gate[...] = total_gate
    up[...] = total_up


def gate_up(rows, gate_weight, up_weight):
    depth, width = gate_weight.shape
    total = rows[0].shape[0] * len(rows)
    out = jax.ShapeDtypeStruct((total, width), F32)
    return pl.pallas_call(
        functools.partial(gate_up_kernel, len(rows), 1024),
        in_specs=[VMEM_SPEC] * (len(rows) + 2),
        out_specs=[VMEM_SPEC] * 2,
        out_shape=[out, out],
        compiler_params=params(12),
        cost_estimate=cost(4 * total * depth * width, 4 * depth * width),
    )(*[in_vmem(x) for x in (*rows, gate_weight, up_weight)])


def silu(value):
    return value / (1.0 + jnp.exp(-value))


def down_kernel(shared_count, store_count, experts, chunks, order, *refs):
    count = len(order)
    gate, up, gate_own, up_own, columns = refs[:5]
    inner = refs[5 : 5 + count]
    packs = refs[5 + count : 5 + 2 * count]
    down, down_own = refs[5 + 2 * count : 7 + 2 * count]
    outs = refs[7 + 2 * count :]
    total, hid = gate.shape
    size = total // count
    half = count // 2
    width = shared_count + store_count

    meta = jnp.concatenate([ref[width:] for ref in packs], axis=0).astype(F32)
    lane = lax.broadcasted_iota(jnp.int32, meta.shape, 1)
    mine = (lane < 3 * experts) & (lane % experts == columns[2:3, :1])
    share = jnp.sum(jnp.where(mine, meta, 0.0), axis=1, keepdims=True)
    row_tenant = jnp.sum(jnp.where(lane == 3 * experts, meta, 0.0), axis=1, keepdims=True)
    row_tenant = row_tenant.astype(jnp.int32)

    parts, parts_own = [], []
    for r in range(count):
        held = inner[r][...]
        blocks = [held[(k ^ r) * size : ((k ^ r) + 1) * size] for k in range(count)]
        parts.append(jnp.concatenate(blocks, axis=0)[:, shared_count:])
        parts_own.append(blocks[0][:, :shared_count])
    lifted = jnp.concatenate(parts, axis=1)
    lifted_own = jnp.concatenate(parts_own, axis=1)
    zero = jnp.zeros((), BF16)
    slot_tenant = columns[1:2, : count * store_count]
    shared_tenant = columns[0:1, : count * shared_count]
    lifted = jnp.where(row_tenant == slot_tenant, lifted, zero)
    lifted_own = jnp.where(row_tenant[:size] == shared_tenant, lifted_own, zero)
    factor = jnp.concatenate([ref[shared_count:width] for ref in packs], axis=0)
    factor_own = jnp.concatenate([ref[:shared_count] for ref in packs], axis=0)
    upward = up[...] + jnp.dot(lifted, factor, preferred_element_type=F32)
    hidden = (silu(gate[...]) * upward).astype(BF16)
    upward_own = up_own[...] + jnp.dot(lifted_own, factor_own, preferred_element_type=F32)
    hidden_own = (silu(gate_own[...]) * upward_own).astype(BF16)

    part = outs[0].shape[-1]
    tile = tile_of(part)
    for n, chunk in enumerate(chunks):
        keep, send = outs[2 * n : 2 * n + 2]
        for place, j in enumerate(chunk):
            for c in range(part // tile):
                cut = slice(j * part + c * tile, j * part + (c + 1) * tile)
                routed = jnp.dot(hidden, down[:, cut], preferred_element_type=F32) * share
                shared = jnp.dot(hidden_own, down_own[:, cut], preferred_element_type=F32)
                for at, r in enumerate(order):
                    block = routed[r * size : (r + 1) * size]
                    if r == 0:
                        block = block + shared
                    target, row = (keep, at) if at < half else (send, at - half)
                    target[row, place, :, c * tile : (c + 1) * tile] = block.astype(BF16)


def down_products(
    gate, up, gate_own, up_own, columns, inner, packs, down, down_own, experts, chunks, order,
    shared_count, store_count,
):
    count = len(inner)
    total, hid = gate.shape
    size = total // count
    depth = down.shape[1]
    part = depth // lax.axis_size("tensor")
    whole = [gate, up, gate_own, up_own, columns, *inner, *packs, down, down_own]
    outs = []
    for chunk in chunks:
        outs += [jax.ShapeDtypeStruct((count // 2, len(chunk), size, part), BF16)] * 2
    return pl.pallas_call(
        functools.partial(down_kernel, shared_count, store_count, experts, chunks, order),
        in_specs=[VMEM_SPEC] * len(whole),
        out_specs=[VMEM_SPEC] * len(outs),
        out_shape=outs,
        compiler_params=params(16),
        cost_estimate=cost(2 * (total + size) * depth * hid, 4 * depth * hid),
    )(*[in_vmem(x) for x in whole])


def local(
    tokens,
    expert_ids,
    gate_values,
    tenant_ids,
    w_gate,
    w_up,
    routed_down_weight,
    shared_gate,
    shared_up,
    shared_down,
    store_a,
    store_b,
    pair_slot,
    shared_a,
    shared_b,
):
    experts = pair_slot.shape[0]
    adapted, rank, model_width = store_a.shape
    hid = store_b.shape[2]
    steps, size, _ = expert_ids.shape
    count = lax.axis_size("expert")
    n_tensor = lax.axis_size("tensor")
    shared_count, store_count = shared_a.shape[0] * rank, adapted * rank

    rows_own = tokens.reshape(steps * size, model_width)
    arrived = swap(rows_own, count // 2)
    first = first_products(
        experts,
        rows_own,
        shared_gate,
        shared_up,
        jnp.swapaxes(expert_ids, 1, 2),
        jnp.swapaxes(gate_values, 1, 2),
        tenant_ids.reshape(1, size),
        pair_slot,
        shared_b.reshape(shared_count, hid),
        store_b.reshape(store_count, hid),
        [
            shared_a.reshape(shared_count, model_width),
            store_a.reshape(store_count, model_width),
            w_gate[0],
            w_up[0],
            routed_down_weight[0],
            shared_down,
        ],
    )
    arrived, first = lax.optimization_barrier((arrived, first))
    gate_own, up_own, pack, columns, rows_held, factor_shared, factor_store = first[:7]
    gate_weight, up_weight, down, down_own = first[7:]
    rows = exchange_rest(rows_own, arrived)
    rows[0] = rows_held
    pack_arrived = swap(pack, count // 2)
    inner = inner_products(rows, factor_shared, factor_store)
    pack_arrived, inner = lax.optimization_barrier((pack_arrived, inner))
    inners = [inner] + [swap(inner, r) for r in range(1, count)]
    packs = exchange_rest(pack, pack_arrived)
    gate, up = gate_up(rows, gate_weight, up_weight)

    order = [0]
    bit = count // 2
    while bit >= 1:
        order = order + [r | bit for r in order]
        bit //= 2
    chunks = [[j] for j in range(n_tensor - 1, 1, -1)] + [[1, 0]]
    outs = down_products(
        gate, up, gate_own, up_own, columns, inners, packs, down, down_own, experts, chunks, order,
        shared_count, store_count,
    )
    held, leaving = list(outs[0::2]), list(outs[1::2])
    bit = 1
    while bit < count:
        half = count // (2 * bit) // 2
        arrived = []
        for n in range(len(chunks)):
            if bit > 1 and n > 1:
                leaving[n], arrived[n - 2] = lax.optimization_barrier((leaving[n], arrived[n - 2]))
            arrived.append(swap(leaving[n], bit))
        leaving = [add(h[half:], a[half:]) for h, a in zip(held, arrived)]
        held = [add(h[:half], a[:half]) for h, a in zip(held, arrived)]
        bit *= 2
    total = None
    for n, chunk in enumerate(chunks):
        for place, j in enumerate(chunk):
            value = leaving[n][0, place]
            value = (swap(value, j, "tensor") if j else value).astype(F32)
            total = value if total is None else total + value
    return total.astype(BF16).reshape(steps, size, model_width // n_tensor)


def solution(mesh):
    return jax.shard_map(
        local,
        mesh=mesh,
        in_specs=(
            P(None, ("groups", "expert"), None),
            P(None, ("groups", "expert"), None),
            P(None, ("groups", "expert"), None),
            P(("groups", "expert")),
            P("expert", None, "tensor"),
            P("expert", None, "tensor"),
            P("expert", "tensor", None),
            P(None, "tensor"),
            P(None, "tensor"),
            P("tensor", None),
            P("expert", None, None),
            P("expert", None, "tensor"),
            P(),
            P("expert", None, None),
            P("expert", None, "tensor"),
        ),
        out_specs=P(None, ("groups", "expert"), "tensor"),
        check_vma=False,
    )
```

```python
import functools

import jax
import jax.numpy as jnp
from jax import lax
from jax.experimental import pallas as pl
from jax.experimental.pallas import tpu as pltpu
from jax.sharding import PartitionSpec as P

F32 = jnp.float32
BF16 = jnp.bfloat16
MIB = 1024 * 1024


def params(mebibytes):
    return pltpu.CompilerParams(vmem_limit_bytes=mebibytes * MIB)


def cost(flops, moved):
    return pl.CostEstimate(flops=int(flops), bytes_accessed=int(moved), transcendentals=0)


def in_vmem(value):
    return pltpu.with_memory_space_constraint(value, pltpu.VMEM)


def in_hbm(value):
    return pltpu.with_memory_space_constraint(value, pltpu.HBM)


def vmem_shape(value):
    return pltpu.VMEM(value.shape, value.dtype)


VMEM_SPEC = pl.BlockSpec(memory_space=pltpu.VMEM)
HBM_SPEC = pl.BlockSpec(memory_space=pltpu.HBM)


def swap(value, bits, axis="expert"):
    count = lax.axis_size(axis)
    return lax.ppermute(value, axis, [(i, i ^ bits) for i in range(count)])


def add(one, other):
    return (one.astype(F32) + other.astype(F32)).astype(BF16)


def total_of(values):
    return sum(value.astype(F32) for value in values).astype(BF16)


def exchange_rest(value, arrived):
    count = lax.axis_size("expert")
    bit = count // 2
    pieces = {0: value, bit: arrived}
    bit //= 2
    while bit >= 1:
        pieces.update({r ^ bit: swap(piece, bit) for r, piece in list(pieces.items())})
        bit //= 2
    return [pieces[r] for r in range(count)]


def tile_of(width):
    return 256 if width % 256 == 0 else 128


def stage_kernel(source, target, sem):
    copy = pltpu.make_async_copy(source, target, sem)
    copy.start()
    copy.wait()


def stage(value):
    return pl.pallas_call(
        stage_kernel,
        in_specs=[HBM_SPEC],
        out_specs=VMEM_SPEC,
        out_shape=vmem_shape(value),
        scratch_shapes=[pltpu.SemaphoreType.DMA],
        compiler_params=params(1),
        cost_estimate=cost(0, 2 * value.size),
    )(in_hbm(value))


def column_of(row, size):
    lane = lax.broadcasted_iota(jnp.int32, (size, row.shape[1]), 1)
    place = lax.broadcasted_iota(jnp.int32, (size, row.shape[1]), 0)
    return jnp.sum(jnp.where(lane == place, row.astype(F32), 0.0), axis=1, keepdims=True)


def first_kernel(
    experts, pieces, rows, gate_weight, up_weight, ids, values, tenants, pair_slot, shared_b,
    store_b, factor_shared, factor_store, gate_weight_routed, up_weight_routed, down, down_own,
    gate, up, pack, columns, factor_shared_out, factor_store_out, gate_out, up_out,
    down_out, down_own_out, gate_held, up_held, ids_held, values_held, tenants_held,
    pair_slot_held, small_sems, sems, stage_sems,
):
    own, own_part = lax.axis_index("expert"), lax.axis_index("tensor")
    parts = lax.axis_size("tensor")
    depth = gate_weight.shape[0]
    shared_count, width = shared_b.shape
    store_count = store_b.shape[0]
    base = shared_count + store_count

    small = [
        (ids, ids_held),
        (values, values_held),
        (tenants, tenants_held),
        (pair_slot, pair_slot_held),
        (shared_b, pack.at[pl.ds(0, shared_count)]),
        (store_b, pack.at[pl.ds(shared_count, store_count)]),
    ]
    small = [
        pltpu.make_async_copy(source, target, small_sems.at[n])
        for n, (source, target) in enumerate(small)
    ]
    for copy in small:
        copy.start()
    chunk = depth // pieces
    copies = []
    for k in range(pieces):
        part = pl.ds(k * chunk, chunk)
        pair = [
            pltpu.make_async_copy(gate_weight.at[part], gate_held.at[part], sems.at[0, k]),
            pltpu.make_async_copy(up_weight.at[part], up_held.at[part], sems.at[1, k]),
        ]
        for copy in pair:
            copy.start()
        copies.append(pair)
    staged = [(factor_shared, factor_shared_out), (factor_store, factor_store_out)]
    for source, target in ((gate_weight_routed, gate_out), (up_weight_routed, up_out)):
        piece = depth // parts
        for k in range(parts):
            part = pl.ds(k * piece, piece)
            staged.append((source.at[part], target.at[part]))
    piece = depth // parts
    for source, target in ((down, down_out), (down_own, down_own_out)):
        for j in range(parts):
            start = pl.multiple_of((own_part ^ j) * piece, piece)
            staged.append((source.at[:, pl.ds(start, piece)], target.at[:, pl.ds(j * piece, piece)]))
    staged = [
        pltpu.make_async_copy(source, target, stage_sems.at[n])
        for n, (source, target) in enumerate(staged)
    ]
    for copy in staged:
        copy.start()
    for copy in small:
        copy.wait()

    steps, top, size = ids_held.shape
    tenant = column_of(tenants_held[...], size)
    lane = lax.broadcasted_iota(jnp.int32, (size, width), 1)
    for s in range(steps):
        weight = jnp.zeros((size, width), F32)
        for k in range(top):
            expert = column_of(ids_held[s, k : k + 1], size).astype(jnp.int32)
            value = column_of(values_held[s, k : k + 1], size)
            weight = weight + jnp.where(expert == lane % experts, value, 0.0)
        high = weight.astype(BF16).astype(F32)
        middle = (weight - high).astype(BF16).astype(F32)
        low = weight - high - middle
        meta = jnp.where(lane < experts, high, jnp.where(lane < 2 * experts, middle, low))
        meta = jnp.where(lane < 3 * experts, meta, tenant)
        pack[base + s * size : base + (s + 1) * size] = meta.astype(BF16)

    tenant_count = pair_slot_held.shape[1]
    place = lax.broadcasted_iota(jnp.int32, pair_slot_held.shape, 0)
    own_row = jnp.sum(
        jnp.where(place == own, pair_slot_held[...].astype(F32), 0.0), axis=0, keepdims=True
    )
    own_slots = column_of(own_row, tenant_count).astype(jnp.int32)
    total = columns.shape[1]
    per_device = tenant_count // lax.axis_size("expert")
    rank = shared_count // per_device
    column = lax.broadcasted_iota(jnp.int32, (1, total), 1)
    shared_tenant = (own ^ (column // shared_count)) * per_device + column % shared_count // rank
    slot = (own ^ (column // store_count)) * (store_count // rank) + column % store_count // rank
    tenant_number = lax.broadcasted_iota(jnp.int32, (tenant_count, total), 0)
    slot_tenant = jnp.max(jnp.where(own_slots == slot, tenant_number, -1), axis=0, keepdims=True)
    columns[0:1] = shared_tenant
    columns[1:2] = slot_tenant
    columns[2:3] = jnp.full((1, total), own, jnp.int32)
    columns[3:8] = jnp.zeros((5, total), jnp.int32)

    total_gate = jnp.zeros(gate.shape, F32)
    total_up = jnp.zeros(up.shape, F32)
    for k in range(pieces):
        part = pl.ds(k * chunk, chunk)
        for copy in copies[k]:
            copy.wait()
        block = rows[:, part]
        total_gate += jnp.dot(block, gate_held[part], preferred_element_type=F32)
        total_up += jnp.dot(block, up_held[part], preferred_element_type=F32)
    gate[...] = total_gate
    up[...] = total_up
    for copy in staged:
        copy.wait()


def first_products(
    experts, rows, gate_weight, up_weight, ids, values, tenants, pair_slot, shared_b, store_b,
    staged,
):
    depth, width = gate_weight.shape
    count, parts = lax.axis_size("expert"), lax.axis_size("tensor")
    pieces = 7
    product = jax.ShapeDtypeStruct((rows.shape[0], width), F32)
    pack = jax.ShapeDtypeStruct(
        (shared_b.shape[0] + store_b.shape[0] + rows.shape[0], width), BF16
    )
    columns = count * max(shared_b.shape[0], store_b.shape[0])
    columns = jax.ShapeDtypeStruct((8, columns), jnp.int32)
    inputs = [gate_weight, up_weight, ids, values, tenants, pair_slot, shared_b, store_b, *staged]
    moved = sum(value.size * 2 for value in (gate_weight, up_weight, *staged))
    outs = [product, product, pack, columns, *[vmem_shape(value) for value in staged]]
    return pl.pallas_call(
        functools.partial(first_kernel, experts, pieces),
        in_specs=[VMEM_SPEC] + [HBM_SPEC] * len(inputs),
        out_specs=[VMEM_SPEC] * len(outs),
        out_shape=outs,
        scratch_shapes=[
            pltpu.VMEM((depth, width), BF16),
            pltpu.VMEM((depth, width), BF16),
            pltpu.VMEM(ids.shape, jnp.int32),
            pltpu.VMEM(values.shape, F32),
            pltpu.VMEM(tenants.shape, jnp.int32),
            pltpu.VMEM(pair_slot.shape, jnp.int32),
            pltpu.SemaphoreType.DMA((6,)),
            pltpu.SemaphoreType.DMA((2, pieces)),
            pltpu.SemaphoreType.DMA((2 + 4 * parts,)),
        ],
        compiler_params=params(12),
        cost_estimate=cost(4 * rows.shape[0] * depth * width, moved),
    )(in_vmem(rows), *[in_hbm(value) for value in inputs])


def inner_kernel(count, chunk, *refs):
    rows, factor_shared, factor_store, inner = refs[:count], *refs[count:]
    depth = factor_shared.shape[1]
    size = rows[0].shape[0]
    split = factor_shared.shape[0]
    width = split + factor_store.shape[0]
    total = jnp.zeros((count * size, width), F32)
    for k in range(depth // chunk):
        part = pl.ds(k * chunk, chunk)
        block = jnp.concatenate([ref[:, part] for ref in rows], axis=0)
        factors = jnp.concatenate([factor_shared[:, part], factor_store[:, part]], axis=0)
        total += lax.dot_general(
            block, factors, (((1,), (1,)), ((), ())), preferred_element_type=F32
        )
    inner[...] = total.astype(BF16)


def inner_products(rows, factor_shared, factor_store):
    depth = factor_shared.shape[1]
    total = rows[0].shape[0] * len(rows)
    width = factor_shared.shape[0] + factor_store.shape[0]
    return pl.pallas_call(
        functools.partial(inner_kernel, len(rows), 1024),
        in_specs=[VMEM_SPEC] * (len(rows) + 2),
        out_specs=VMEM_SPEC,
        out_shape=jax.ShapeDtypeStruct((total, width), BF16),
        compiler_params=params(12),
        cost_estimate=cost(2 * total * depth * width, 2 * depth * width),
    )(*[in_vmem(x) for x in (*rows, factor_shared, factor_store)])


def gate_up_kernel(count, chunk, *refs):
    rows, gate_weight, up_weight, gate, up = refs[:count], *refs[count:]
    depth = gate_weight.shape[0]
    total_gate = jnp.zeros(gate.shape, F32)
    total_up = jnp.zeros(up.shape, F32)
    for k in range(depth // chunk):
        part = pl.ds(k * chunk, chunk)
        block = jnp.concatenate([ref[:, part] for ref in rows], axis=0)
        total_gate += jnp.dot(block, gate_weight[part], preferred_element_type=F32)
        total_up += jnp.dot(block, up_weight[part], preferred_element_type=F32)
    gate[...] = total_gate
    up[...] = total_up


def gate_up(rows, gate_weight, up_weight):
    depth, width = gate_weight.shape
    total = rows[0].shape[0] * len(rows)
    out = jax.ShapeDtypeStruct((total, width), F32)
    return pl.pallas_call(
        functools.partial(gate_up_kernel, len(rows), 1024),
        in_specs=[VMEM_SPEC] * (len(rows) + 2),
        out_specs=[VMEM_SPEC] * 2,
        out_shape=[out, out],
        compiler_params=params(12),
        cost_estimate=cost(4 * total * depth * width, 4 * depth * width),
    )(*[in_vmem(x) for x in (*rows, gate_weight, up_weight)])


def silu(value):
    return value / (1.0 + jnp.exp(-value))


def down_kernel(shared_count, store_count, experts, chunks, order, *refs):
    count = len(order)
    gate, up, gate_own, up_own, columns = refs[:5]
    inner = refs[5 : 5 + count]
    packs = refs[5 + count : 5 + 2 * count]
    down, down_own = refs[5 + 2 * count : 7 + 2 * count]
    outs = refs[7 + 2 * count :]
    total, hid = gate.shape
    size = total // count
    half = count // 2
    width = shared_count + store_count

    meta = jnp.concatenate([ref[width:] for ref in packs], axis=0).astype(F32)
    lane = lax.broadcasted_iota(jnp.int32, meta.shape, 1)
    mine = (lane < 3 * experts) & (lane % experts == columns[2:3, :1])
    share = jnp.sum(jnp.where(mine, meta, 0.0), axis=1, keepdims=True)
    row_tenant = jnp.sum(jnp.where(lane == 3 * experts, meta, 0.0), axis=1, keepdims=True)
    row_tenant = row_tenant.astype(jnp.int32)

    parts, parts_own = [], []
    for r in range(count):
        held = inner[r][...]
        blocks = [held[(k ^ r) * size : ((k ^ r) + 1) * size] for k in range(count)]
        parts.append(jnp.concatenate(blocks, axis=0)[:, shared_count:])
        parts_own.append(blocks[0][:, :shared_count])
    lifted = jnp.concatenate(parts, axis=1)
    lifted_own = jnp.concatenate(parts_own, axis=1)
    zero = jnp.zeros((), BF16)
    slot_tenant = columns[1:2, : count * store_count]
    shared_tenant = columns[0:1, : count * shared_count]
    lifted = jnp.where(row_tenant == slot_tenant, lifted, zero)
    lifted_own = jnp.where(row_tenant[:size] == shared_tenant, lifted_own, zero)
    factor = jnp.concatenate([ref[shared_count:width] for ref in packs], axis=0)
    factor_own = jnp.concatenate([ref[:shared_count] for ref in packs], axis=0)
    upward = up[...] + jnp.dot(lifted, factor, preferred_element_type=F32)
    hidden = (silu(gate[...]) * upward).astype(BF16)
    upward_own = up_own[...] + jnp.dot(lifted_own, factor_own, preferred_element_type=F32)
    hidden_own = (silu(gate_own[...]) * upward_own).astype(BF16)

    part = outs[0].shape[-1]
    tile = tile_of(part)
    for n, chunk in enumerate(chunks):
        keep, send = outs[2 * n : 2 * n + 2]
        for place, j in enumerate(chunk):
            for c in range(part // tile):
                cut = slice(j * part + c * tile, j * part + (c + 1) * tile)
                routed = jnp.dot(hidden, down[:, cut], preferred_element_type=F32) * share
                shared = jnp.dot(hidden_own, down_own[:, cut], preferred_element_type=F32)
                for at, r in enumerate(order):
                    block = routed[r * size : (r + 1) * size]
                    if r == 0:
                        block = block + shared
                    target, row = (keep, at) if at < half else (send, at - half)
                    target[row, place, :, c * tile : (c + 1) * tile] = block.astype(BF16)


def down_products(
    gate, up, gate_own, up_own, columns, inner, packs, down, down_own, experts, chunks, order,
    shared_count, store_count,
):
    count = len(inner)
    total, hid = gate.shape
    size = total // count
    depth = down.shape[1]
    part = depth // lax.axis_size("tensor")
    whole = [gate, up, gate_own, up_own, columns, *inner, *packs, down, down_own]
    outs = []
    for chunk in chunks:
        outs += [jax.ShapeDtypeStruct((count // 2, len(chunk), size, part), BF16)] * 2
    return pl.pallas_call(
        functools.partial(down_kernel, shared_count, store_count, experts, chunks, order),
        in_specs=[VMEM_SPEC] * len(whole),
        out_specs=[VMEM_SPEC] * len(outs),
        out_shape=outs,
        compiler_params=params(16),
        cost_estimate=cost(2 * (total + size) * depth * hid, 4 * depth * hid),
    )(*[in_vmem(x) for x in whole])


def local(
    tokens,
    expert_ids,
    gate_values,
    tenant_ids,
    w_gate,
    w_up,
    routed_down_weight,
    shared_gate,
    shared_up,
    shared_down,
    store_a,
    store_b,
    pair_slot,
    shared_a,
    shared_b,
):
    experts = pair_slot.shape[0]
    adapted, rank, model_width = store_a.shape
    hid = store_b.shape[2]
    steps, size, _ = expert_ids.shape
    count = lax.axis_size("expert")
    n_tensor = lax.axis_size("tensor")
    shared_count, store_count = shared_a.shape[0] * rank, adapted * rank

    rows_own = stage(tokens.reshape(steps * size, model_width))
    arrived = swap(rows_own, count // 2)
    first = first_products(
        experts,
        rows_own,
        shared_gate,
        shared_up,
        jnp.swapaxes(expert_ids, 1, 2),
        jnp.swapaxes(gate_values, 1, 2),
        tenant_ids.reshape(1, size),
        pair_slot,
        shared_b.reshape(shared_count, hid),
        store_b.reshape(store_count, hid),
        [
            shared_a.reshape(shared_count, model_width),
            store_a.reshape(store_count, model_width),
            w_gate[0],
            w_up[0],
            routed_down_weight[0],
            shared_down,
        ],
    )
    arrived, first = lax.optimization_barrier((arrived, first))
    gate_own, up_own, pack, columns, factor_shared, factor_store = first[:6]
    gate_weight, up_weight, down, down_own = first[6:]
    rows = exchange_rest(rows_own, arrived)
    pack_arrived = swap(pack, count // 2)
    inner = inner_products(rows, factor_shared, factor_store)
    inner_arrived = swap(inner, count // 2)
    gate, up = gate_up(rows, gate_weight, up_weight)
    pack_arrived, inner_arrived, gate = lax.optimization_barrier(
        (pack_arrived, inner_arrived, gate)
    )
    inners = exchange_rest(inner, inner_arrived)
    packs = exchange_rest(pack, pack_arrived)

    order = [0]
    bit = count // 2
    while bit >= 1:
        order = order + [r | bit for r in order]
        bit //= 2
    blocks = list(range(n_tensor - 1, -1, -1))
    chunks = [blocks[: n_tensor // 2], blocks[n_tensor // 2 :]]
    outs = down_products(
        gate, up, gate_own, up_own, columns, inners, packs, down, down_own, experts, chunks, order,
        shared_count, store_count,
    )
    held, leaving = list(outs[0::2]), list(outs[1::2])
    bit = 1
    while bit < count:
        half = count // (2 * bit) // 2
        arrived = []
        for n in range(len(chunks)):
            if bit > 1 and n > 0:
                leaving[n], arrived[n - 1] = lax.optimization_barrier((leaving[n], arrived[n - 1]))
            arrived.append(swap(leaving[n], bit))
        if 2 * bit < count:
            leaving = [add(h[half:], a[half:]) for h, a in zip(held, arrived)]
            held = [add(h[:half], a[:half]) for h, a in zip(held, arrived)]
        bit *= 2
    parts = {}
    for n, chunk in enumerate(chunks):
        for place, j in enumerate(chunk):
            parts[j] = [held[n][0, place], arrived[n][0, place]]
    bit = 1
    while bit < n_tensor:
        for j in sorted([j for j in parts if j & bit], reverse=True):
            parts[j ^ bit].append(swap(total_of(parts.pop(j)), bit, "tensor"))
        bit *= 2
    return total_of(parts[0]).reshape(steps, size, model_width // n_tensor)


def solution(mesh):
    return jax.shard_map(
        local,
        mesh=mesh,
        in_specs=(
            P(None, ("groups", "expert"), None),
            P(None, ("groups", "expert"), None),
            P(None, ("groups", "expert"), None),
            P(("groups", "expert")),
            P("expert", None, "tensor"),
            P("expert", None, "tensor"),
            P("expert", "tensor", None),
            P(None, "tensor"),
            P(None, "tensor"),
            P("tensor", None),
            P("expert", None, None),
            P("expert", None, "tensor"),
            P(),
            P("expert", None, None),
            P("expert", None, "tensor"),
        ),
        out_specs=P(None, ("groups", "expert"), "tensor"),
        check_vma=False,
    )
```

```python
import functools

import jax
import jax.numpy as jnp
from jax import lax
from jax.experimental import pallas as pl
from jax.experimental.pallas import tpu as pltpu
from jax.sharding import PartitionSpec as P

F32 = jnp.float32
BF16 = jnp.bfloat16
MIB = 1024 * 1024


def params(mebibytes):
    return pltpu.CompilerParams(vmem_limit_bytes=mebibytes * MIB)


def cost(flops, moved):
    return pl.CostEstimate(flops=int(flops), bytes_accessed=int(moved), transcendentals=0)


def in_vmem(value):
    return pltpu.with_memory_space_constraint(value, pltpu.VMEM)


def in_hbm(value):
    return pltpu.with_memory_space_constraint(value, pltpu.HBM)


def vmem_shape(value):
    return pltpu.VMEM(value.shape, value.dtype)


VMEM_SPEC = pl.BlockSpec(memory_space=pltpu.VMEM)
HBM_SPEC = pl.BlockSpec(memory_space=pltpu.HBM)


def swap(value, bits, axis="expert"):
    count = lax.axis_size(axis)
    return lax.ppermute(value, axis, [(i, i ^ bits) for i in range(count)])


def add(one, other):
    return (one.astype(F32) + other.astype(F32)).astype(BF16)


def total_of(values):
    return sum(value.astype(F32) for value in values).astype(BF16)


def exchange_rest(value, arrived):
    count = lax.axis_size("expert")
    bit = count // 2
    pieces = {0: value, bit: arrived}
    bit //= 2
    while bit >= 1:
        pieces.update({r ^ bit: swap(piece, bit) for r, piece in list(pieces.items())})
        bit //= 2
    return [pieces[r] for r in range(count)]


def tile_of(width):
    return 256 if width % 256 == 0 else 128


def column_of(row, size):
    lane = lax.broadcasted_iota(jnp.int32, (size, row.shape[1]), 1)
    place = lax.broadcasted_iota(jnp.int32, (size, row.shape[1]), 0)
    return jnp.sum(jnp.where(lane == place, row.astype(F32), 0.0), axis=1, keepdims=True)


def first_kernel(
    experts, pieces, rows, gate_weight, up_weight, ids, values, tenants, pair_slot, shared_b,
    store_b, factor_shared, factor_store, gate_weight_routed, up_weight_routed, down, down_own,
    gate, up, pack, columns, rows_out, factor_shared_out, factor_store_out, gate_out, up_out,
    down_out, down_own_out, gate_held, up_held, ids_held, values_held, tenants_held,
    pair_slot_held, small_sems, sems, stage_sems,
):
    own, own_part = lax.axis_index("expert"), lax.axis_index("tensor")
    parts = lax.axis_size("tensor")
    depth = gate_weight.shape[0]
    shared_count, width = shared_b.shape
    store_count = store_b.shape[0]
    base = shared_count + store_count

    small = [
        (rows, rows_out),
        (ids, ids_held),
        (values, values_held),
        (tenants, tenants_held),
        (pair_slot, pair_slot_held),
        (shared_b, pack.at[pl.ds(0, shared_count)]),
        (store_b, pack.at[pl.ds(shared_count, store_count)]),
    ]
    small = [
        pltpu.make_async_copy(source, target, small_sems.at[n])
        for n, (source, target) in enumerate(small)
    ]
    for copy in small:
        copy.start()
    chunk = depth // pieces
    copies = []
    for k in range(pieces):
        part = pl.ds(k * chunk, chunk)
        pair = [
            pltpu.make_async_copy(gate_weight.at[part], gate_held.at[part], sems.at[0, k]),
            pltpu.make_async_copy(up_weight.at[part], up_held.at[part], sems.at[1, k]),
        ]
        for copy in pair:
            copy.start()
        copies.append(pair)
    staged = [(factor_shared, factor_shared_out), (factor_store, factor_store_out)]
    for source, target in ((gate_weight_routed, gate_out), (up_weight_routed, up_out)):
        piece = depth // parts
        for k in range(parts):
            part = pl.ds(k * piece, piece)
            staged.append((source.at[part], target.at[part]))
    piece = depth // parts
    for source, target in ((down, down_out), (down_own, down_own_out)):
        for j in range(parts):
            start = pl.multiple_of((own_part ^ j) * piece, piece)
            staged.append((source.at[:, pl.ds(start, piece)], target.at[:, pl.ds(j * piece, piece)]))
    staged = [
        pltpu.make_async_copy(source, target, stage_sems.at[n])
        for n, (source, target) in enumerate(staged)
    ]
    for copy in staged:
        copy.start()
    for copy in small:
        copy.wait()

    steps, top, size = ids_held.shape
    tenant = column_of(tenants_held[...], size)
    lane = lax.broadcasted_iota(jnp.int32, (size, width), 1)
    for s in range(steps):
        weight = jnp.zeros((size, width), F32)
        for k in range(top):
            expert = column_of(ids_held[s, k : k + 1], size).astype(jnp.int32)
            value = column_of(values_held[s, k : k + 1], size)
            weight = weight + jnp.where(expert == lane % experts, value, 0.0)
        high = weight.astype(BF16).astype(F32)
        middle = (weight - high).astype(BF16).astype(F32)
        low = weight - high - middle
        meta = jnp.where(lane < experts, high, jnp.where(lane < 2 * experts, middle, low))
        meta = jnp.where(lane < 3 * experts, meta, tenant)
        pack[base + s * size : base + (s + 1) * size] = meta.astype(BF16)

    tenant_count = pair_slot_held.shape[1]
    place = lax.broadcasted_iota(jnp.int32, pair_slot_held.shape, 0)
    own_row = jnp.sum(
        jnp.where(place == own, pair_slot_held[...].astype(F32), 0.0), axis=0, keepdims=True
    )
    own_slots = column_of(own_row, tenant_count).astype(jnp.int32)
    total = columns.shape[1]
    per_device = tenant_count // lax.axis_size("expert")
    rank = shared_count // per_device
    column = lax.broadcasted_iota(jnp.int32, (1, total), 1)
    shared_tenant = (own ^ (column // shared_count)) * per_device + column % shared_count // rank
    slot = (own ^ (column // store_count)) * (store_count // rank) + column % store_count // rank
    tenant_number = lax.broadcasted_iota(jnp.int32, (tenant_count, total), 0)
    slot_tenant = jnp.max(jnp.where(own_slots == slot, tenant_number, -1), axis=0, keepdims=True)
    columns[0:1] = shared_tenant
    columns[1:2] = slot_tenant
    columns[2:3] = jnp.full((1, total), own, jnp.int32)
    columns[3:8] = jnp.zeros((5, total), jnp.int32)

    total_gate = jnp.zeros(gate.shape, F32)
    total_up = jnp.zeros(up.shape, F32)
    for k in range(pieces):
        part = pl.ds(k * chunk, chunk)
        for copy in copies[k]:
            copy.wait()
        block = rows_out[:, part]
        total_gate += jnp.dot(block, gate_held[part], preferred_element_type=F32)
        total_up += jnp.dot(block, up_held[part], preferred_element_type=F32)
    gate[...] = total_gate
    up[...] = total_up
    for copy in staged:
        copy.wait()


def first_products(
    experts, rows, gate_weight, up_weight, ids, values, tenants, pair_slot, shared_b, store_b,
    staged,
):
    depth, width = gate_weight.shape
    count, parts = lax.axis_size("expert"), lax.axis_size("tensor")
    pieces = 7
    product = jax.ShapeDtypeStruct((rows.shape[0], width), F32)
    pack = jax.ShapeDtypeStruct(
        (shared_b.shape[0] + store_b.shape[0] + rows.shape[0], width), BF16
    )
    columns = count * max(shared_b.shape[0], store_b.shape[0])
    columns = jax.ShapeDtypeStruct((8, columns), jnp.int32)
    inputs = [
        rows, gate_weight, up_weight, ids, values, tenants, pair_slot, shared_b, store_b, *staged
    ]
    moved = sum(value.size * 2 for value in (rows, gate_weight, up_weight, *staged))
    outs = [product, product, pack, columns, *[vmem_shape(value) for value in (rows, *staged)]]
    return pl.pallas_call(
        functools.partial(first_kernel, experts, pieces),
        in_specs=[HBM_SPEC] * len(inputs),
        out_specs=[VMEM_SPEC] * len(outs),
        out_shape=outs,
        scratch_shapes=[
            pltpu.VMEM((depth, width), BF16),
            pltpu.VMEM((depth, width), BF16),
            pltpu.VMEM(ids.shape, jnp.int32),
            pltpu.VMEM(values.shape, F32),
            pltpu.VMEM(tenants.shape, jnp.int32),
            pltpu.VMEM(pair_slot.shape, jnp.int32),
            pltpu.SemaphoreType.DMA((7,)),
            pltpu.SemaphoreType.DMA((2, pieces)),
            pltpu.SemaphoreType.DMA((2 + 4 * parts,)),
        ],
        compiler_params=params(12),
        cost_estimate=cost(4 * rows.shape[0] * depth * width, moved),
    )(*[in_hbm(value) for value in inputs])


def inner_kernel(count, chunk, *refs):
    rows, shared, stored, outs = refs[:count], refs[count : count + 2], refs[count + 2 : count + 4], refs[count + 4 :]
    size, depth = rows[0].shape
    columns = (((1,), (1,)), ((), ()))
    total_shared, total_stored = 0.0, 0.0
    for k in range(depth // chunk):
        part = pl.ds(k * chunk, chunk)
        held = [ref[:, part] for ref in rows]
        total_stored += lax.dot_general(
            jnp.concatenate(held, axis=0),
            jnp.concatenate([ref[:, part] for ref in stored], axis=0),
            columns,
            preferred_element_type=F32,
        )
        total_shared += lax.dot_general(
            jnp.concatenate(held[::2], axis=0),
            jnp.concatenate([ref[:, part] for ref in shared], axis=0),
            columns,
            preferred_element_type=F32,
        )
    total_stored = total_stored.astype(BF16)
    total_shared = total_shared.astype(BF16)
    for n, out in enumerate(outs):
        blocks = [total_shared[n * size : (n + 1) * size]]
        blocks += [total_stored[k * size : (k + 1) * size] for k in range(count)]
        out[...] = jnp.concatenate(blocks, axis=1)


def inner_products(rows, shared, stored):
    size, depth = rows[0].shape
    count = len(rows)
    width = 2 * shared[0].shape[0] + 2 * stored[0].shape[0] * count
    flops = 4 * size * depth * (shared[0].shape[0] * count // 2 + stored[0].shape[0] * count)
    inputs = [*rows, *shared, *stored]
    return pl.pallas_call(
        functools.partial(inner_kernel, count, 1024),
        in_specs=[VMEM_SPEC] * len(inputs),
        out_specs=[VMEM_SPEC] * (count // 2),
        out_shape=[jax.ShapeDtypeStruct((size, width), BF16)] * (count // 2),
        compiler_params=params(12),
        cost_estimate=cost(flops, 2 * sum(value.size for value in inputs)),
    )(*[in_vmem(value) for value in inputs])


def gate_up_kernel(count, chunk, *refs):
    rows, gate_weight, up_weight, gate, up = refs[:count], *refs[count:]
    depth = gate_weight.shape[0]
    total_gate = jnp.zeros(gate.shape, F32)
    total_up = jnp.zeros(up.shape, F32)
    for k in range(depth // chunk):
        part = pl.ds(k * chunk, chunk)
        block = jnp.concatenate([ref[:, part] for ref in rows], axis=0)
        total_gate += jnp.dot(block, gate_weight[part], preferred_element_type=F32)
        total_up += jnp.dot(block, up_weight[part], preferred_element_type=F32)
    gate[...] = total_gate
    up[...] = total_up


def gate_up(rows, gate_weight, up_weight):
    depth, width = gate_weight.shape
    total = rows[0].shape[0] * len(rows)
    out = jax.ShapeDtypeStruct((total, width), F32)
    return pl.pallas_call(
        functools.partial(gate_up_kernel, len(rows), 1024),
        in_specs=[VMEM_SPEC] * (len(rows) + 2),
        out_specs=[VMEM_SPEC] * 2,
        out_shape=[out, out],
        compiler_params=params(12),
        cost_estimate=cost(4 * total * depth * width, 4 * depth * width),
    )(*[in_vmem(x) for x in (*rows, gate_weight, up_weight)])


def silu(value):
    return value / (1.0 + jnp.exp(-value))


def down_kernel(shared_count, store_count, experts, chunks, order, *refs):
    count = len(order)
    half = count // 2
    gate, up, gate_own, up_own, columns = refs[:5]
    inner = refs[5 : 5 + half]
    packs = refs[5 + half : 5 + half + count]
    down, down_own = refs[5 + half + count : 7 + half + count]
    outs = refs[7 + half + count :]
    total, hid = gate.shape
    size = total // count
    width = shared_count + store_count

    meta = jnp.concatenate([ref[width:] for ref in packs], axis=0).astype(F32)
    lane = lax.broadcasted_iota(jnp.int32, meta.shape, 1)
    mine = (lane < 3 * experts) & (lane % experts == columns[2:3, :1])
    share = jnp.sum(jnp.where(mine, meta, 0.0), axis=1, keepdims=True)
    row_tenant = jnp.sum(jnp.where(lane == 3 * experts, meta, 0.0), axis=1, keepdims=True)
    row_tenant = row_tenant.astype(jnp.int32)

    start, stored = 2 * shared_count, 2 * store_count
    held = [ref[...] for ref in inner]
    lifted_own = jnp.concatenate([value[:, :start] for value in held], axis=1)
    lifted = []
    for k in range(count):
        places = [start + stored * (k ^ (2 * n)) for n in range(half)]
        blocks = [value[:, place : place + stored] for value, place in zip(held, places)]
        lifted.append(jnp.concatenate(blocks, axis=1))
    lifted = jnp.concatenate(lifted, axis=0)
    zero = jnp.zeros((), BF16)
    slot_tenant = columns[1:2, : count * store_count]
    shared_tenant = columns[0:1, : count * shared_count]
    lifted = jnp.where(row_tenant == slot_tenant, lifted, zero)
    lifted_own = jnp.where(row_tenant[:size] == shared_tenant, lifted_own, zero)
    factor = jnp.concatenate([ref[shared_count:width] for ref in packs], axis=0)
    factor_own = jnp.concatenate([ref[:shared_count] for ref in packs], axis=0)
    upward = up[...] + jnp.dot(lifted, factor, preferred_element_type=F32)
    hidden = (silu(gate[...]) * upward).astype(BF16)
    upward_own = up_own[...] + jnp.dot(lifted_own, factor_own, preferred_element_type=F32)
    hidden_own = (silu(gate_own[...]) * upward_own).astype(BF16)

    part = outs[0].shape[-1]
    tile = tile_of(part)
    for n, chunk in enumerate(chunks):
        keep, send = outs[2 * n : 2 * n + 2]
        for place, j in enumerate(chunk):
            for c in range(part // tile):
                cut = slice(j * part + c * tile, j * part + (c + 1) * tile)
                routed = jnp.dot(hidden, down[:, cut], preferred_element_type=F32) * share
                shared = jnp.dot(hidden_own, down_own[:, cut], preferred_element_type=F32)
                for at, r in enumerate(order):
                    block = routed[r * size : (r + 1) * size]
                    if r == 0:
                        block = block + shared
                    target, row = (keep, at) if at < half else (send, at - half)
                    target[row, place, :, c * tile : (c + 1) * tile] = block.astype(BF16)


def down_products(
    gate, up, gate_own, up_own, columns, inner, packs, down, down_own, experts, chunks, order,
    shared_count, store_count,
):
    count = len(packs)
    total, hid = gate.shape
    size = total // count
    depth = down.shape[1]
    part = depth // lax.axis_size("tensor")
    whole = [gate, up, gate_own, up_own, columns, *inner, *packs, down, down_own]
    outs = []
    for chunk in chunks:
        outs += [jax.ShapeDtypeStruct((count // 2, len(chunk), size, part), BF16)] * 2
    return pl.pallas_call(
        functools.partial(down_kernel, shared_count, store_count, experts, chunks, order),
        in_specs=[VMEM_SPEC] * len(whole),
        out_specs=[VMEM_SPEC] * len(outs),
        out_shape=outs,
        compiler_params=params(16),
        cost_estimate=cost(2 * (total + size) * depth * hid, 4 * depth * hid),
    )(*[in_vmem(x) for x in whole])


def local(
    tokens,
    expert_ids,
    gate_values,
    tenant_ids,
    w_gate,
    w_up,
    routed_down_weight,
    shared_gate,
    shared_up,
    shared_down,
    store_a,
    store_b,
    pair_slot,
    shared_a,
    shared_b,
):
    experts = pair_slot.shape[0]
    adapted, rank, model_width = store_a.shape
    hid = store_b.shape[2]
    steps, size, _ = expert_ids.shape
    count = lax.axis_size("expert")
    n_tensor = lax.axis_size("tensor")
    shared_count, store_count = shared_a.shape[0] * rank, adapted * rank

    rows_own = tokens.reshape(steps * size, model_width)
    arrived = swap(rows_own, count // 2)
    shared_other = swap(shared_a, 1).reshape(shared_count, model_width)
    store_other = swap(store_a, 1).reshape(store_count, model_width)
    first = first_products(
        experts,
        rows_own,
        shared_gate,
        shared_up,
        jnp.swapaxes(expert_ids, 1, 2),
        jnp.swapaxes(gate_values, 1, 2),
        tenant_ids.reshape(1, size),
        pair_slot,
        shared_b.reshape(shared_count, hid),
        store_b.reshape(store_count, hid),
        [
            shared_a.reshape(shared_count, model_width),
            store_a.reshape(store_count, model_width),
            w_gate[0],
            w_up[0],
            routed_down_weight[0],
            shared_down,
        ],
    )
    arrived, first, store_other = lax.optimization_barrier((arrived, first, store_other))
    gate_own, up_own, pack, columns, rows_held, factor_shared, factor_store = first[:7]
    gate_weight, up_weight, down, down_own = first[7:]
    rows = exchange_rest(rows_own, arrived)
    rows[0] = rows_held
    packs = [pack] + [swap(pack, r) for r in range(1, count)]
    inner = inner_products(rows, [factor_shared, shared_other], [factor_store, store_other])
    rows, inner = lax.optimization_barrier((rows, inner))
    inners = [inner[0]] + [swap(inner[n], 2 * n) for n in range(1, count // 2)]
    gate, up = gate_up(rows, gate_weight, up_weight)

    order = [0]
    bit = count // 2
    while bit >= 1:
        order = order + [r | bit for r in order]
        bit //= 2
    chunks = [[j] for j in range(n_tensor - 1, 1, -1)] + [[1, 0]]
    outs = down_products(
        gate, up, gate_own, up_own, columns, inners, packs, down, down_own, experts, chunks, order,
        shared_count, store_count,
    )
    held, leaving = list(outs[0::2]), list(outs[1::2])
    bit = 1
    while bit < count:
        half = count // (2 * bit) // 2
        arrived = [swap(value, bit) for value in leaving]
        if bit > 1:
            arrived[0], *_ = lax.optimization_barrier((arrived[0], *leaving))
        if 2 * bit < count:
            leaving = [add(h[half:], a[half:]) for h, a in zip(held, arrived)]
            held = [add(h[:half], a[:half]) for h, a in zip(held, arrived)]
        bit *= 2
    parts = {}
    for n, chunk in enumerate(chunks):
        for place, j in enumerate(chunk):
            parts[j] = [held[n][0, place], arrived[n][0, place]]
    bit = 1
    while bit < n_tensor:
        for j in sorted([j for j in parts if j & bit], reverse=True):
            parts[j ^ bit].append(swap(total_of(parts.pop(j)), bit, "tensor"))
        bit *= 2
    return total_of(parts[0]).reshape(steps, size, model_width // n_tensor)


def solution(mesh):
    return jax.shard_map(
        local,
        mesh=mesh,
        in_specs=(
            P(None, ("groups", "expert"), None),
            P(None, ("groups", "expert"), None),
            P(None, ("groups", "expert"), None),
            P(("groups", "expert")),
            P("expert", None, "tensor"),
            P("expert", None, "tensor"),
            P("expert", "tensor", None),
            P(None, "tensor"),
            P(None, "tensor"),
            P("tensor", None),
            P("expert", None, None),
            P("expert", None, "tensor"),
            P(),
            P("expert", None, None),
            P("expert", None, "tensor"),
        ),
        out_specs=P(None, ("groups", "expert"), "tensor"),
        check_vma=False,
    )
```

```python
import functools

import jax
import jax.numpy as jnp
from jax import lax
from jax.experimental import pallas as pl
from jax.experimental.pallas import tpu as pltpu
from jax.sharding import PartitionSpec as P

F32 = jnp.float32
BF16 = jnp.bfloat16
MIB = 1024 * 1024


def params(mebibytes):
    return pltpu.CompilerParams(vmem_limit_bytes=mebibytes * MIB)


def cost(flops, moved):
    return pl.CostEstimate(flops=int(flops), bytes_accessed=int(moved), transcendentals=0)


def in_vmem(value):
    return pltpu.with_memory_space_constraint(value, pltpu.VMEM)


def in_hbm(value):
    return pltpu.with_memory_space_constraint(value, pltpu.HBM)


def vmem_shape(value):
    return pltpu.VMEM(value.shape, value.dtype)


VMEM_SPEC = pl.BlockSpec(memory_space=pltpu.VMEM)
HBM_SPEC = pl.BlockSpec(memory_space=pltpu.HBM)


def swap(value, bits, axis="expert"):
    count = lax.axis_size(axis)
    return lax.ppermute(value, axis, [(i, i ^ bits) for i in range(count)])


def add(one, other):
    return (one.astype(F32) + other.astype(F32)).astype(BF16)


def total_of(values):
    return sum(value.astype(F32) for value in values).astype(BF16)


def exchange_rest(value, arrived):
    count = lax.axis_size("expert")
    bit = count // 2
    pieces = {0: value, bit: arrived}
    bit //= 2
    while bit >= 1:
        pieces.update({r ^ bit: swap(piece, bit) for r, piece in list(pieces.items())})
        bit //= 2
    return [pieces[r] for r in range(count)]


def tile_of(width):
    return 256 if width % 256 == 0 else 128


def column_of(row, size):
    lane = lax.broadcasted_iota(jnp.int32, (size, row.shape[1]), 1)
    place = lax.broadcasted_iota(jnp.int32, (size, row.shape[1]), 0)
    return jnp.sum(jnp.where(lane == place, row.astype(F32), 0.0), axis=1, keepdims=True)


def first_kernel(
    experts, pieces, rows, gate_weight, up_weight, ids, values, tenants, pair_slot, shared_b,
    store_b, factor_shared, factor_store, gate_weight_routed, up_weight_routed, down, down_own,
    gate, up, pack, columns, rows_out, factor_shared_out, factor_store_out, gate_out, up_out,
    down_out, down_own_out, gate_held, up_held, ids_held, values_held, tenants_held,
    pair_slot_held, small_sems, sems, stage_sems,
):
    own, own_part = lax.axis_index("expert"), lax.axis_index("tensor")
    parts = lax.axis_size("tensor")
    depth = gate_weight.shape[0]
    shared_count, width = shared_b.shape
    store_count = store_b.shape[0]
    base = shared_count + store_count

    small = [
        (rows, rows_out),
        (ids, ids_held),
        (values, values_held),
        (tenants, tenants_held),
        (pair_slot, pair_slot_held),
        (shared_b, pack.at[pl.ds(0, shared_count)]),
        (store_b, pack.at[pl.ds(shared_count, store_count)]),
    ]
    small = [
        pltpu.make_async_copy(source, target, small_sems.at[n])
        for n, (source, target) in enumerate(small)
    ]
    for copy in small:
        copy.start()
    chunk = depth // pieces
    copies = []
    for k in range(pieces):
        part = pl.ds(k * chunk, chunk)
        pair = [
            pltpu.make_async_copy(gate_weight.at[part], gate_held.at[part], sems.at[0, k]),
            pltpu.make_async_copy(up_weight.at[part], up_held.at[part], sems.at[1, k]),
        ]
        for copy in pair:
            copy.start()
        copies.append(pair)
    staged = [(factor_shared, factor_shared_out), (factor_store, factor_store_out)]
    for source, target in ((gate_weight_routed, gate_out), (up_weight_routed, up_out)):
        piece = depth // parts
        for k in range(parts):
            part = pl.ds(k * piece, piece)
            staged.append((source.at[part], target.at[part]))
    piece = depth // parts
    for source, target in ((down, down_out), (down_own, down_own_out)):
        for j in range(parts):
            start = pl.multiple_of((own_part ^ j) * piece, piece)
            staged.append((source.at[:, pl.ds(start, piece)], target.at[:, pl.ds(j * piece, piece)]))
    staged = [
        pltpu.make_async_copy(source, target, stage_sems.at[n])
        for n, (source, target) in enumerate(staged)
    ]
    for copy in staged:
        copy.start()
    for copy in small:
        copy.wait()

    steps, top, size = ids_held.shape
    tenant = column_of(tenants_held[...], size)
    lane = lax.broadcasted_iota(jnp.int32, (size, width), 1)
    for s in range(steps):
        weight = jnp.zeros((size, width), F32)
        for k in range(top):
            expert = column_of(ids_held[s, k : k + 1], size).astype(jnp.int32)
            value = column_of(values_held[s, k : k + 1], size)
            weight = weight + jnp.where(expert == lane % experts, value, 0.0)
        high = weight.astype(BF16).astype(F32)
        middle = (weight - high).astype(BF16).astype(F32)
        low = weight - high - middle
        meta = jnp.where(lane < experts, high, jnp.where(lane < 2 * experts, middle, low))
        meta = jnp.where(lane < 3 * experts, meta, tenant)
        pack[base + s * size : base + (s + 1) * size] = meta.astype(BF16)

    tenant_count = pair_slot_held.shape[1]
    place = lax.broadcasted_iota(jnp.int32, pair_slot_held.shape, 0)
    own_row = jnp.sum(
        jnp.where(place == own, pair_slot_held[...].astype(F32), 0.0), axis=0, keepdims=True
    )
    own_slots = column_of(own_row, tenant_count).astype(jnp.int32)
    total = columns.shape[1]
    per_device = tenant_count // lax.axis_size("expert")
    rank = shared_count // per_device
    column = lax.broadcasted_iota(jnp.int32, (1, total), 1)
    shared_tenant = (own ^ (column // shared_count)) * per_device + column % shared_count // rank
    slot = (own ^ (column // store_count)) * (store_count // rank) + column % store_count // rank
    tenant_number = lax.broadcasted_iota(jnp.int32, (tenant_count, total), 0)
    slot_tenant = jnp.max(jnp.where(own_slots == slot, tenant_number, -1), axis=0, keepdims=True)
    columns[0:1] = shared_tenant
    columns[1:2] = slot_tenant
    columns[2:3] = jnp.full((1, total), own, jnp.int32)
    columns[3:8] = jnp.zeros((5, total), jnp.int32)

    total_gate = jnp.zeros(gate.shape, F32)
    total_up = jnp.zeros(up.shape, F32)
    for k in range(pieces):
        part = pl.ds(k * chunk, chunk)
        for copy in copies[k]:
            copy.wait()
        block = rows_out[:, part]
        total_gate += jnp.dot(block, gate_held[part], preferred_element_type=F32)
        total_up += jnp.dot(block, up_held[part], preferred_element_type=F32)
    gate[...] = total_gate
    up[...] = total_up
    for copy in staged:
        copy.wait()


def first_products(
    experts, rows, gate_weight, up_weight, ids, values, tenants, pair_slot, shared_b, store_b,
    staged,
):
    depth, width = gate_weight.shape
    count, parts = lax.axis_size("expert"), lax.axis_size("tensor")
    pieces = 7
    product = jax.ShapeDtypeStruct((rows.shape[0], width), F32)
    pack = jax.ShapeDtypeStruct(
        (shared_b.shape[0] + store_b.shape[0] + rows.shape[0], width), BF16
    )
    columns = count * max(shared_b.shape[0], store_b.shape[0])
    columns = jax.ShapeDtypeStruct((8, columns), jnp.int32)
    inputs = [
        rows, gate_weight, up_weight, ids, values, tenants, pair_slot, shared_b, store_b, *staged
    ]
    moved = sum(value.size * 2 for value in (rows, gate_weight, up_weight, *staged))
    outs = [product, product, pack, columns, *[vmem_shape(value) for value in (rows, *staged)]]
    return pl.pallas_call(
        functools.partial(first_kernel, experts, pieces),
        in_specs=[HBM_SPEC] * len(inputs),
        out_specs=[VMEM_SPEC] * len(outs),
        out_shape=outs,
        scratch_shapes=[
            pltpu.VMEM((depth, width), BF16),
            pltpu.VMEM((depth, width), BF16),
            pltpu.VMEM(ids.shape, jnp.int32),
            pltpu.VMEM(values.shape, F32),
            pltpu.VMEM(tenants.shape, jnp.int32),
            pltpu.VMEM(pair_slot.shape, jnp.int32),
            pltpu.SemaphoreType.DMA((7,)),
            pltpu.SemaphoreType.DMA((2, pieces)),
            pltpu.SemaphoreType.DMA((2 + 4 * parts,)),
        ],
        compiler_params=params(12),
        cost_estimate=cost(4 * rows.shape[0] * depth * width, moved),
    )(*[in_hbm(value) for value in inputs])


def inner_kernel(count, chunk, *refs):
    rows, shared, stored, outs = refs[:count], refs[count : count + 2], refs[count + 2 : count + 4], refs[count + 4 :]
    size, depth = rows[0].shape
    split = 2 * shared[0].shape[0]
    total = 0.0
    for k in range(depth // chunk):
        part = pl.ds(k * chunk, chunk)
        total += lax.dot_general(
            jnp.concatenate([ref[:, part] for ref in rows], axis=0),
            jnp.concatenate([ref[:, part] for ref in (*shared, *stored)], axis=0),
            (((1,), (1,)), ((), ())),
            preferred_element_type=F32,
        )
    total = total.astype(BF16)
    total_shared = jnp.concatenate(
        [total[r * size : (r + 1) * size, :split] for r in range(0, count, 2)], axis=0
    )
    total_stored = total[:, split:]
    for n, out in enumerate(outs):
        blocks = [total_shared[n * size : (n + 1) * size]]
        blocks += [total_stored[k * size : (k + 1) * size] for k in range(count)]
        out[...] = jnp.concatenate(blocks, axis=1)


def inner_products(rows, shared, stored):
    size, depth = rows[0].shape
    count = len(rows)
    width = 2 * shared[0].shape[0] + 2 * stored[0].shape[0] * count
    flops = 4 * size * depth * (shared[0].shape[0] * count // 2 + stored[0].shape[0] * count)
    inputs = [*rows, *shared, *stored]
    return pl.pallas_call(
        functools.partial(inner_kernel, count, 1024),
        in_specs=[VMEM_SPEC] * len(inputs),
        out_specs=[VMEM_SPEC] * (count // 2),
        out_shape=[jax.ShapeDtypeStruct((size, width), BF16)] * (count // 2),
        compiler_params=params(12),
        cost_estimate=cost(flops, 2 * sum(value.size for value in inputs)),
    )(*[in_vmem(value) for value in inputs])


def gate_up_kernel(count, chunk, *refs):
    rows, gate_weight, up_weight, gate, up = refs[:count], *refs[count:]
    depth = gate_weight.shape[0]
    total_gate = jnp.zeros(gate.shape, F32)
    total_up = jnp.zeros(up.shape, F32)
    for k in range(depth // chunk):
        part = pl.ds(k * chunk, chunk)
        block = jnp.concatenate([ref[:, part] for ref in rows], axis=0)
        total_gate += jnp.dot(block, gate_weight[part], preferred_element_type=F32)
        total_up += jnp.dot(block, up_weight[part], preferred_element_type=F32)
    gate[...] = total_gate
    up[...] = total_up


def gate_up(rows, gate_weight, up_weight):
    depth, width = gate_weight.shape
    total = rows[0].shape[0] * len(rows)
    out = jax.ShapeDtypeStruct((total, width), F32)
    return pl.pallas_call(
        functools.partial(gate_up_kernel, len(rows), 1024),
        in_specs=[VMEM_SPEC] * (len(rows) + 2),
        out_specs=[VMEM_SPEC] * 2,
        out_shape=[out, out],
        compiler_params=params(12),
        cost_estimate=cost(4 * total * depth * width, 4 * depth * width),
    )(*[in_vmem(x) for x in (*rows, gate_weight, up_weight)])


def silu(value):
    return value / (1.0 + jnp.exp(-value))


def down_kernel(shared_count, store_count, experts, chunks, order, *refs):
    count = len(order)
    half = count // 2
    gate, up, gate_own, up_own, columns = refs[:5]
    inner = refs[5 : 5 + half]
    packs = refs[5 + half : 5 + half + count]
    down, down_own = refs[5 + half + count : 7 + half + count]
    outs = refs[7 + half + count :]
    total, hid = gate.shape
    size = total // count
    width = shared_count + store_count

    meta = jnp.concatenate([ref[width:] for ref in packs], axis=0).astype(F32)
    lane = lax.broadcasted_iota(jnp.int32, meta.shape, 1)
    mine = (lane < 3 * experts) & (lane % experts == columns[2:3, :1])
    share = jnp.sum(jnp.where(mine, meta, 0.0), axis=1, keepdims=True)
    row_tenant = jnp.sum(jnp.where(lane == 3 * experts, meta, 0.0), axis=1, keepdims=True)
    row_tenant = row_tenant.astype(jnp.int32)

    start, stored = 2 * shared_count, 2 * store_count
    held = [ref[...] for ref in inner]
    lifted_own = jnp.concatenate([value[:, :start] for value in held], axis=1)
    lifted = []
    for k in range(count):
        places = [start + stored * (k ^ (2 * n)) for n in range(half)]
        blocks = [value[:, place : place + stored] for value, place in zip(held, places)]
        lifted.append(jnp.concatenate(blocks, axis=1))
    lifted = jnp.concatenate(lifted, axis=0)
    zero = jnp.zeros((), BF16)
    slot_tenant = columns[1:2, : count * store_count]
    shared_tenant = columns[0:1, : count * shared_count]
    lifted = jnp.where(row_tenant == slot_tenant, lifted, zero)
    lifted_own = jnp.where(row_tenant[:size] == shared_tenant, lifted_own, zero)
    factor = jnp.concatenate([ref[shared_count:width] for ref in packs], axis=0)
    factor_own = jnp.concatenate([ref[:shared_count] for ref in packs], axis=0)
    upward = up[...] + jnp.dot(lifted, factor, preferred_element_type=F32)
    hidden = (silu(gate[...]) * upward).astype(BF16)
    upward_own = up_own[...] + jnp.dot(lifted_own, factor_own, preferred_element_type=F32)
    hidden_own = (silu(gate_own[...]) * upward_own).astype(BF16)

    part = outs[0].shape[-1]
    tile = tile_of(part)
    for n, chunk in enumerate(chunks):
        keep, send = outs[2 * n : 2 * n + 2]
        for place, j in enumerate(chunk):
            for c in range(part // tile):
                cut = slice(j * part + c * tile, j * part + (c + 1) * tile)
                routed = jnp.dot(hidden, down[:, cut], preferred_element_type=F32) * share
                shared = jnp.dot(hidden_own, down_own[:, cut], preferred_element_type=F32)
                for at, r in enumerate(order):
                    block = routed[r * size : (r + 1) * size]
                    if r == 0:
                        block = block + shared
                    target, row = (keep, at) if at < half else (send, at - half)
                    target[row, place, :, c * tile : (c + 1) * tile] = block.astype(BF16)


def down_products(
    gate, up, gate_own, up_own, columns, inner, packs, down, down_own, experts, chunks, order,
    shared_count, store_count,
):
    count = len(packs)
    total, hid = gate.shape
    size = total // count
    depth = down.shape[1]
    part = depth // lax.axis_size("tensor")
    whole = [gate, up, gate_own, up_own, columns, *inner, *packs, down, down_own]
    outs = []
    for chunk in chunks:
        outs += [jax.ShapeDtypeStruct((count // 2, len(chunk), size, part), BF16)] * 2
    return pl.pallas_call(
        functools.partial(down_kernel, shared_count, store_count, experts, chunks, order),
        in_specs=[VMEM_SPEC] * len(whole),
        out_specs=[VMEM_SPEC] * len(outs),
        out_shape=outs,
        compiler_params=params(16),
        cost_estimate=cost(2 * (total + size) * depth * hid, 4 * depth * hid),
    )(*[in_vmem(x) for x in whole])


def local(
    tokens,
    expert_ids,
    gate_values,
    tenant_ids,
    w_gate,
    w_up,
    routed_down_weight,
    shared_gate,
    shared_up,
    shared_down,
    store_a,
    store_b,
    pair_slot,
    shared_a,
    shared_b,
):
    experts = pair_slot.shape[0]
    adapted, rank, model_width = store_a.shape
    hid = store_b.shape[2]
    steps, size, _ = expert_ids.shape
    count = lax.axis_size("expert")
    n_tensor = lax.axis_size("tensor")
    shared_count, store_count = shared_a.shape[0] * rank, adapted * rank

    rows_own = tokens.reshape(steps * size, model_width)
    arrived = swap(rows_own, count // 2)
    shared_other = swap(shared_a, 1).reshape(shared_count, model_width)
    store_other = swap(store_a, 1).reshape(store_count, model_width)
    first = first_products(
        experts,
        rows_own,
        shared_gate,
        shared_up,
        jnp.swapaxes(expert_ids, 1, 2),
        jnp.swapaxes(gate_values, 1, 2),
        tenant_ids.reshape(1, size),
        pair_slot,
        shared_b.reshape(shared_count, hid),
        store_b.reshape(store_count, hid),
        [
            shared_a.reshape(shared_count, model_width),
            store_a.reshape(store_count, model_width),
            w_gate[0],
            w_up[0],
            routed_down_weight[0],
            shared_down,
        ],
    )
    arrived, first, store_other = lax.optimization_barrier((arrived, first, store_other))
    gate_own, up_own, pack, columns, rows_held, factor_shared, factor_store = first[:7]
    gate_weight, up_weight, down, down_own = first[7:]
    rows = exchange_rest(rows_own, arrived)
    rows[0] = rows_held
    pack_arrived = swap(pack, count // 2)
    inner = inner_products(rows, [factor_shared, shared_other], [factor_store, store_other])
    rows, inner, pack_arrived = lax.optimization_barrier((rows, inner, pack_arrived))
    packs = exchange_rest(pack, pack_arrived)
    inners = [inner[0]] + [swap(inner[n], 2 * n) for n in range(1, count // 2)]
    gate, up = gate_up(rows, gate_weight, up_weight)

    order = [0]
    bit = count // 2
    while bit >= 1:
        order = order + [r | bit for r in order]
        bit //= 2
    chunks = [[j] for j in range(n_tensor - 1, 1, -1)] + [[1, 0]]
    outs = down_products(
        gate, up, gate_own, up_own, columns, inners, packs, down, down_own, experts, chunks, order,
        shared_count, store_count,
    )
    held, leaving = list(outs[0::2]), list(outs[1::2])
    bit = 1
    while bit < count:
        half = count // (2 * bit) // 2
        arrived = [swap(value, bit) for value in leaving]
        if bit > 1:
            arrived[0], *_ = lax.optimization_barrier((arrived[0], *leaving))
        if 2 * bit < count:
            leaving = [add(h[half:], a[half:]) for h, a in zip(held, arrived)]
            held = [add(h[:half], a[:half]) for h, a in zip(held, arrived)]
        bit *= 2
    parts = {}
    for n, chunk in enumerate(chunks):
        for place, j in enumerate(chunk):
            parts[j] = [held[n][0, place], arrived[n][0, place]]
    bit = 1
    while bit < n_tensor:
        for j in sorted([j for j in parts if j & bit], reverse=True):
            parts[j ^ bit].append(swap(total_of(parts.pop(j)), bit, "tensor"))
        bit *= 2
    return total_of(parts[0]).reshape(steps, size, model_width // n_tensor)


def solution(mesh):
    return jax.shard_map(
        local,
        mesh=mesh,
        in_specs=(
            P(None, ("groups", "expert"), None),
            P(None, ("groups", "expert"), None),
            P(None, ("groups", "expert"), None),
            P(("groups", "expert")),
            P("expert", None, "tensor"),
            P("expert", None, "tensor"),
            P("expert", "tensor", None),
            P(None, "tensor"),
            P(None, "tensor"),
            P("tensor", None),
            P("expert", None, None),
            P("expert", None, "tensor"),
            P(),
            P("expert", None, None),
            P("expert", None, "tensor"),
        ),
        out_specs=P(None, ("groups", "expert"), "tensor"),
        check_vma=False,
    )
```

```python
import functools

import jax
import jax.numpy as jnp
from jax import lax
from jax.experimental import pallas as pl
from jax.experimental.pallas import tpu as pltpu
from jax.sharding import PartitionSpec as P

F32 = jnp.float32
BF16 = jnp.bfloat16
MIB = 1024 * 1024


def params(mebibytes):
    return pltpu.CompilerParams(vmem_limit_bytes=mebibytes * MIB)


def cost(flops, moved):
    return pl.CostEstimate(flops=int(flops), bytes_accessed=int(moved), transcendentals=0)


def in_vmem(value):
    return pltpu.with_memory_space_constraint(value, pltpu.VMEM)


def in_hbm(value):
    return pltpu.with_memory_space_constraint(value, pltpu.HBM)


def vmem_shape(value):
    return pltpu.VMEM(value.shape, value.dtype)


VMEM_SPEC = pl.BlockSpec(memory_space=pltpu.VMEM)
HBM_SPEC = pl.BlockSpec(memory_space=pltpu.HBM)


def swap(value, bits, axis="expert"):
    count = lax.axis_size(axis)
    return lax.ppermute(value, axis, [(i, i ^ bits) for i in range(count)])


def add(one, other):
    return (one.astype(F32) + other.astype(F32)).astype(BF16)


def total_of(values):
    return sum(value.astype(F32) for value in values).astype(BF16)


def exchange_rest(value, arrived):
    count = lax.axis_size("expert")
    bit = count // 2
    pieces = {0: value, bit: arrived}
    bit //= 2
    while bit >= 1:
        pieces.update({r ^ bit: swap(piece, bit) for r, piece in list(pieces.items())})
        bit //= 2
    return [pieces[r] for r in range(count)]


def tile_of(width):
    return 256 if width % 256 == 0 else 128


def column_of(row, size):
    lane = lax.broadcasted_iota(jnp.int32, (size, row.shape[1]), 1)
    place = lax.broadcasted_iota(jnp.int32, (size, row.shape[1]), 0)
    return jnp.sum(jnp.where(lane == place, row.astype(F32), 0.0), axis=1, keepdims=True)


def first_kernel(
    experts, ids, values, tenants, pair_slot, rows, store_b, shared_b, factor_store, factor_shared,
    gate_weight, up_weight, gate_shared, up_shared, down, down_shared, meta, columns, *refs
):
    targets, (ids_held, values_held, tenants_held, pair_slot_held, small_sems, sems) = refs[:-6], refs[-6:]
    own, own_part = lax.axis_index("expert"), lax.axis_index("tensor")
    parts = lax.axis_size("tensor")
    small = [
        (ids, ids_held), (values, values_held), (tenants, tenants_held), (pair_slot, pair_slot_held)
    ]
    small = [
        pltpu.make_async_copy(source, target, small_sems.at[n])
        for n, (source, target) in enumerate(small)
    ]
    sources = [
        rows, store_b, shared_b, factor_store, factor_shared, gate_weight, up_weight, gate_shared,
        up_shared, down, down_shared,
    ]
    staged = list(zip(sources[:5], targets[:5]))
    piece = gate_weight.shape[0] // parts
    for source, target in zip(sources[5:9], targets[5:9]):
        for k in range(parts):
            part = pl.ds(k * piece, piece)
            staged.append((source.at[part], target.at[part]))
    for source, target in zip(sources[9:], targets[9:]):
        for j in range(parts):
            start = pl.multiple_of((own_part ^ j) * piece, piece)
            staged.append((source.at[:, pl.ds(start, piece)], target.at[:, pl.ds(j * piece, piece)]))
    staged = [
        pltpu.make_async_copy(source, target, sems.at[n])
        for n, (source, target) in enumerate(staged)
    ]
    for copy in (*small, *staged):
        copy.start()
    for copy in small:
        copy.wait()

    steps, top, size = ids_held.shape
    tenant = column_of(tenants_held[...], size)
    lane = lax.broadcasted_iota(jnp.int32, (size, meta.shape[1]), 1)
    for s in range(steps):
        weight = jnp.zeros(lane.shape, F32)
        for k in range(top):
            expert = column_of(ids_held[s, k : k + 1], size).astype(jnp.int32)
            value = column_of(values_held[s, k : k + 1], size)
            weight = weight + jnp.where(expert == lane % experts, value, 0.0)
        high = weight.astype(BF16).astype(F32)
        middle = (weight - high).astype(BF16).astype(F32)
        low = weight - high - middle
        found = jnp.where(lane < experts, high, jnp.where(lane < 2 * experts, middle, low))
        found = jnp.where(lane < 3 * experts, found, tenant)
        meta[s * size : (s + 1) * size] = found.astype(BF16)

    tenant_count = pair_slot_held.shape[1]
    place = lax.broadcasted_iota(jnp.int32, pair_slot_held.shape, 0)
    own_row = jnp.sum(
        jnp.where(place == own, pair_slot_held[...].astype(F32), 0.0), axis=0, keepdims=True
    )
    own_slots = column_of(own_row, tenant_count).astype(jnp.int32)
    total = columns.shape[1]
    per_device = tenant_count // lax.axis_size("expert")
    shared_count, store_count = shared_b.shape[0], store_b.shape[0]
    rank = shared_count // per_device
    column = lax.broadcasted_iota(jnp.int32, (1, total), 1)
    shared_tenant = own * per_device + column % shared_count // rank
    slot = (own ^ (column // store_count)) * (store_count // rank) + column % store_count // rank
    tenant_number = lax.broadcasted_iota(jnp.int32, (tenant_count, total), 0)
    slot_tenant = jnp.max(jnp.where(own_slots == slot, tenant_number, -1), axis=0, keepdims=True)
    columns[0:1] = shared_tenant
    columns[1:2] = slot_tenant
    columns[2:3] = jnp.full((1, total), own, jnp.int32)
    columns[3:8] = jnp.zeros((5, total), jnp.int32)
    for copy in staged:
        copy.wait()


def first_call(experts, ids, values, tenants, pair_slot, staged):
    parts = lax.axis_size("tensor")
    steps, _, size = ids.shape
    columns = max(lax.axis_size("expert") * staged[1].shape[0], staged[2].shape[0])
    outs = [
        jax.ShapeDtypeStruct((steps * size, META), BF16),
        jax.ShapeDtypeStruct((8, columns), jnp.int32),
        *[vmem_shape(value) for value in staged],
    ]
    inputs = [ids, values, tenants, pair_slot, *staged]
    return pl.pallas_call(
        functools.partial(first_kernel, experts),
        in_specs=[HBM_SPEC] * len(inputs),
        out_specs=[VMEM_SPEC] * len(outs),
        out_shape=outs,
        scratch_shapes=[
            pltpu.VMEM(ids.shape, jnp.int32),
            pltpu.VMEM(values.shape, F32),
            pltpu.VMEM(tenants.shape, jnp.int32),
            pltpu.VMEM(pair_slot.shape, jnp.int32),
            pltpu.SemaphoreType.DMA((4,)),
            pltpu.SemaphoreType.DMA((5 + 6 * parts,)),
        ],
        compiler_params=params(4),
        cost_estimate=cost(0, 2 * sum(value.size for value in staged)),
    )(*[in_hbm(value) for value in inputs])


META = 128


def message_layout(count, store_count):
    wide = max(128, 2 * store_count)
    per = wide // (2 * store_count)
    return wide + META, per, -(-(count // 2) // per)


def message_kernel(chunk, *refs):
    half = len(refs) - 5
    rows, (factor, factor_other, store_b, meta, out) = refs[:half], refs[half:]
    size, depth = rows[0].shape
    store_count, width = store_b.shape
    total = 0.0
    for k in range(depth // chunk):
        part = pl.ds(k * chunk, chunk)
        total += lax.dot_general(
            jnp.concatenate([ref[:, part] for ref in rows], axis=0),
            jnp.concatenate([factor[:, part], factor_other[:, part]], axis=0),
            (((1,), (1,)), ((), ())),
            preferred_element_type=F32,
        )
    total = total.astype(BF16)
    wide, per, lines = message_layout(2 * half, store_count)
    out[:store_count, :width] = store_b[...]
    if width < wide:
        out[:store_count, width:] = jnp.zeros((store_count, wide - width), BF16)
    for line in range(lines):
        blocks = [
            total[n * size : (n + 1) * size] if n < half else jnp.zeros((size, 2 * store_count), BF16)
            for n in range(line * per, (line + 1) * per)
        ]
        blocks.append(meta[...] if line == 0 else jnp.zeros(meta.shape, BF16))
        start = store_count + line * size
        out[start : start + size] = jnp.concatenate(blocks, axis=1)


def make_message(rows, factor, factor_other, store_b, meta):
    size, depth = rows[0].shape
    store_count = store_b.shape[0]
    wide, _, lines = message_layout(2 * len(rows), store_count)
    inputs = [*rows, factor, factor_other, store_b, meta]
    return pl.pallas_call(
        functools.partial(message_kernel, 1024),
        in_specs=[VMEM_SPEC] * len(inputs),
        out_specs=VMEM_SPEC,
        out_shape=jax.ShapeDtypeStruct((store_count + lines * size, wide), BF16),
        compiler_params=params(8),
        cost_estimate=cost(4 * size * len(rows) * depth * store_count, 2 * depth * store_count * 2),
    )(*[in_vmem(value) for value in inputs])


def gate_up_kernel(count, chunk, *refs):
    rows, factor, weights, inner, outs = refs[:count], refs[count], refs[count + 1 : count + 5], refs[count + 5], refs[count + 6 :]
    depth = factor.shape[1]
    pieces = [pl.ds(k * chunk, chunk) for k in range(depth // chunk)]
    for weight, out in zip(weights, outs):
        total = jnp.zeros(out.shape, F32)
        for part in pieces:
            block = jnp.concatenate([ref[:, part] for ref in rows], axis=0)
            total += jnp.dot(block, weight[part], preferred_element_type=F32)
        out[...] = total
    total = jnp.zeros(inner.shape, F32)
    for part in pieces:
        block = jnp.concatenate([ref[:, part] for ref in rows], axis=0)
        total += lax.dot_general(
            block, factor[:, part], (((1,), (1,)), ((), ())), preferred_element_type=F32
        )
    inner[...] = total.astype(BF16)


def gate_up(rows, factor, weights):
    depth, width = weights[0].shape
    total = rows[0].shape[0] * len(rows)
    inputs = [*rows, factor, *weights]
    out = jax.ShapeDtypeStruct((total, width), F32)
    return pl.pallas_call(
        functools.partial(gate_up_kernel, len(rows), 1024),
        in_specs=[VMEM_SPEC] * len(inputs),
        out_specs=[VMEM_SPEC] * (1 + len(weights)),
        out_shape=[jax.ShapeDtypeStruct((total, factor.shape[0]), BF16)] + [out] * len(weights),
        compiler_params=params(12),
        cost_estimate=cost(2 * len(weights) * total * depth * width, 2 * len(weights) * depth * width),
    )(*[in_vmem(x) for x in inputs])


def silu(value):
    return value / (1.0 + jnp.exp(-value))


def down_kernel(experts, chunks, order, *refs):
    count = len(order)
    half = count // 2
    inner_shared, gate, up, gate_shared, up_shared, columns, shared_b = refs[:7]
    messages = refs[7 : 7 + count]
    down, down_shared = refs[7 + count : 9 + count]
    outs = refs[9 + count :]
    total, width = gate.shape
    size = total // count
    shared_count = shared_b.shape[0]
    store_count = columns.shape[1] // count
    wide, per, _ = message_layout(count, store_count)
    own = columns[2:3, :1]

    meta = jnp.concatenate(
        [ref[store_count : store_count + size, wide - META :] for ref in messages], axis=0
    ).astype(F32)
    lane = lax.broadcasted_iota(jnp.int32, meta.shape, 1)
    mine = (lane < 3 * experts) & (lane % experts == own)
    share = jnp.sum(jnp.where(mine, meta, 0.0), axis=1, keepdims=True)
    row_tenant = jnp.sum(jnp.where(lane == 3 * experts, meta, 0.0), axis=1, keepdims=True)
    row_tenant = row_tenant.astype(jnp.int32)

    lifted = []
    for k in range(count):
        parts = []
        for h in range(0, count, 2):
            sender = h + k % 2
            n = (k ^ sender) // 2
            rows = slice(store_count + n // per * size, store_count + (n // per + 1) * size)
            lanes = slice(n % per * 2 * store_count, (n % per + 1) * 2 * store_count)
            block = messages[sender][rows, lanes]
            if k % 2:
                block = jnp.concatenate([block[:, store_count:], block[:, :store_count]], axis=1)
            parts.append(block)
        lifted.append(jnp.concatenate(parts, axis=1))
    lifted = jnp.concatenate(lifted, axis=0)
    zero = jnp.zeros((), BF16)
    lifted = jnp.where(row_tenant == columns[1:2], lifted, zero)
    shared_tenant = columns[0:1, :shared_count]
    lifted_shared = jnp.where(row_tenant == shared_tenant, inner_shared[...], zero)
    factor = jnp.concatenate([ref[:store_count, :width] for ref in messages], axis=0)
    upward = up[...] + jnp.dot(lifted, factor, preferred_element_type=F32)
    hidden = (silu(gate[...]) * upward).astype(BF16)
    upward = up_shared[...] + jnp.dot(lifted_shared, shared_b[...], preferred_element_type=F32)
    here = (row_tenant >= shared_tenant[:, :1]) & (row_tenant <= shared_tenant[:, shared_count - 1 :])
    hidden_shared = jnp.where(here, silu(gate_shared[...]) * upward, 0.0).astype(BF16)

    part = outs[0].shape[-1]
    tile = tile_of(part)
    for n, chunk in enumerate(chunks):
        keep, send = outs[2 * n : 2 * n + 2]
        for place, j in enumerate(chunk):
            for c in range(part // tile):
                cut = slice(j * part + c * tile, j * part + (c + 1) * tile)
                routed = jnp.dot(hidden, down[:, cut], preferred_element_type=F32) * share
                routed += jnp.dot(hidden_shared, down_shared[:, cut], preferred_element_type=F32)
                for at, r in enumerate(order):
                    block = routed[r * size : (r + 1) * size].astype(BF16)
                    target, row = (keep, at) if at < half else (send, at - half)
                    target[row, place, :, c * tile : (c + 1) * tile] = block


def down_products(gated, columns, shared_b, messages, down, down_shared, experts, chunks, order):
    count = len(messages)
    total, width = gated[1].shape
    size = total // count
    depth = down.shape[1]
    part = depth // lax.axis_size("tensor")
    whole = [*gated, columns, shared_b, *messages, down, down_shared]
    outs = []
    for chunk in chunks:
        outs += [jax.ShapeDtypeStruct((count // 2, len(chunk), size, part), BF16)] * 2
    return pl.pallas_call(
        functools.partial(down_kernel, experts, chunks, order),
        in_specs=[VMEM_SPEC] * len(whole),
        out_specs=[VMEM_SPEC] * len(outs),
        out_shape=outs,
        compiler_params=params(16),
        cost_estimate=cost(4 * total * depth * width, 4 * depth * width),
    )(*[in_vmem(x) for x in whole])


def local(
    tokens,
    expert_ids,
    gate_values,
    tenant_ids,
    w_gate,
    w_up,
    routed_down_weight,
    shared_gate,
    shared_up,
    shared_down,
    store_a,
    store_b,
    pair_slot,
    shared_a,
    shared_b,
):
    experts = pair_slot.shape[0]
    adapted, rank, model_width = store_a.shape
    hid = store_b.shape[2]
    steps, size, _ = expert_ids.shape
    count = lax.axis_size("expert")
    n_tensor = lax.axis_size("tensor")
    shared_count, store_count = shared_a.shape[0] * rank, adapted * rank

    rows_own = tokens.reshape(steps * size, model_width)
    arrived = swap(rows_own, count // 2)
    store_other = swap(store_a, 1).reshape(store_count, model_width)
    first = first_call(
        experts,
        jnp.swapaxes(expert_ids, 1, 2),
        jnp.swapaxes(gate_values, 1, 2),
        tenant_ids.reshape(1, size),
        pair_slot,
        [
            rows_own,
            store_b.reshape(store_count, hid),
            shared_b.reshape(shared_count, hid),
            store_a.reshape(store_count, model_width),
            shared_a.reshape(shared_count, model_width),
            w_gate[0],
            w_up[0],
            shared_gate,
            shared_up,
            routed_down_weight[0],
            shared_down,
        ],
    )
    arrived, first, store_other = lax.optimization_barrier((arrived, first, store_other))
    meta, columns, rows_held, store_b_held, shared_b_held, factor_store, factor_shared = first[:7]
    weights, down, down_own = first[7:11], first[11], first[12]
    rows = exchange_rest(rows_own, arrived)
    rows[0] = rows_held
    message = make_message(rows[::2], factor_store, store_other, store_b_held, meta)
    messages = [message] + [swap(message, r) for r in range(1, count)]
    rows[0], message = lax.optimization_barrier((rows[0], message))
    gated = gate_up(rows, factor_shared, weights)

    order = [0]
    bit = count // 2
    while bit >= 1:
        order = order + [r | bit for r in order]
        bit //= 2
    chunks = [[j] for j in range(n_tensor - 1, 1, -1)] + [[1, 0]]
    outs = down_products(
        gated, columns, shared_b_held, messages, down, down_own, experts, chunks, order
    )
    held, leaving = list(outs[0::2]), list(outs[1::2])
    bit = 1
    while bit < count:
        half = count // (2 * bit) // 2
        if bit > 1:
            leaving[1], *_ = lax.optimization_barrier((leaving[1], leaving[0]))
        arrived = [swap(value, bit) for value in leaving]
        if bit > 1:
            arrived[0], *_ = lax.optimization_barrier((arrived[0], *leaving))
        if 2 * bit < count:
            leaving = [add(h[half:], a[half:]) for h, a in zip(held, arrived)]
            held = [add(h[:half], a[:half]) for h, a in zip(held, arrived)]
        bit *= 2
    parts = {}
    for n, chunk in enumerate(chunks):
        for place, j in enumerate(chunk):
            parts[j] = [held[n][0, place], arrived[n][0, place]]
    bit = 1
    while bit < n_tensor:
        for j in sorted([j for j in parts if j & bit], reverse=True):
            parts[j ^ bit].append(swap(total_of(parts.pop(j)), bit, "tensor"))
        bit *= 2
    return total_of(parts[0]).reshape(steps, size, model_width // n_tensor)


def solution(mesh):
    return jax.shard_map(
        local,
        mesh=mesh,
        in_specs=(
            P(None, ("groups", "expert"), None),
            P(None, ("groups", "expert"), None),
            P(None, ("groups", "expert"), None),
            P(("groups", "expert")),
            P("expert", None, "tensor"),
            P("expert", None, "tensor"),
            P("expert", "tensor", None),
            P(None, "tensor"),
            P(None, "tensor"),
            P("tensor", None),
            P("expert", None, None),
            P("expert", None, "tensor"),
            P(),
            P("expert", None, None),
            P("expert", None, "tensor"),
        ),
        out_specs=P(None, ("groups", "expert"), "tensor"),
        check_vma=False,
    )
```

```python
import functools

import jax
import jax.numpy as jnp
from jax import lax
from jax.experimental import pallas as pl
from jax.experimental.pallas import tpu as pltpu
from jax.sharding import PartitionSpec as P

F32 = jnp.float32
BF16 = jnp.bfloat16
MIB = 1024 * 1024


def params(mebibytes):
    return pltpu.CompilerParams(vmem_limit_bytes=mebibytes * MIB)


def cost(flops, moved):
    return pl.CostEstimate(flops=int(flops), bytes_accessed=int(moved), transcendentals=0)


def in_vmem(value):
    return pltpu.with_memory_space_constraint(value, pltpu.VMEM)


def in_hbm(value):
    return pltpu.with_memory_space_constraint(value, pltpu.HBM)


def vmem_shape(value):
    return pltpu.VMEM(value.shape, value.dtype)


VMEM_SPEC = pl.BlockSpec(memory_space=pltpu.VMEM)
HBM_SPEC = pl.BlockSpec(memory_space=pltpu.HBM)


def swap(value, bits, axis="expert"):
    count = lax.axis_size(axis)
    return lax.ppermute(value, axis, [(i, i ^ bits) for i in range(count)])


def add(one, other):
    return (one.astype(F32) + other.astype(F32)).astype(BF16)


def total_of(values):
    return sum(value.astype(F32) for value in values).astype(BF16)


def far_rows(arrived, rows_own):
    count = lax.axis_size("expert")
    bit = count // 2
    pieces = {0: rows_own, bit: arrived}
    bit //= 2
    while bit > 1:
        pieces.update({r ^ bit: swap(piece, bit) for r, piece in list(pieces.items())})
        bit //= 2
    return [pieces[r] for r in range(2, count, 2)]


def tile_of(width):
    return 256 if width % 256 == 0 else 128


def column_of(row, size):
    lane = lax.broadcasted_iota(jnp.int32, (size, row.shape[1]), 1)
    place = lax.broadcasted_iota(jnp.int32, (size, row.shape[1]), 0)
    return jnp.sum(jnp.where(lane == place, row.astype(F32), 0.0), axis=1, keepdims=True)


def first_kernel(
    experts, ids, values, tenants, pair_slot, rows, store_b, shared_b, factor_store, factor_shared,
    gate_weight, up_weight, gate_shared, up_shared, down, down_shared, meta, columns, *refs
):
    targets, (ids_held, values_held, tenants_held, pair_slot_held, small_sems, sems) = refs[:-6], refs[-6:]
    own, own_part = lax.axis_index("expert"), lax.axis_index("tensor")
    parts = lax.axis_size("tensor")
    small = [
        (ids, ids_held), (values, values_held), (tenants, tenants_held), (pair_slot, pair_slot_held)
    ]
    small = [
        pltpu.make_async_copy(source, target, small_sems.at[n])
        for n, (source, target) in enumerate(small)
    ]
    sources = [
        rows, store_b, shared_b, factor_store, factor_shared, gate_weight, up_weight, gate_shared,
        up_shared, down, down_shared,
    ]
    staged = list(zip(sources[:5], targets[:5]))
    piece = gate_weight.shape[0] // parts
    for source, target in zip(sources[5:9], targets[5:9]):
        for k in range(parts):
            part = pl.ds(k * piece, piece)
            staged.append((source.at[part], target.at[part]))
    for source, target in zip(sources[9:], targets[9:]):
        for j in range(parts):
            start = pl.multiple_of((own_part ^ j) * piece, piece)
            staged.append((source.at[:, pl.ds(start, piece)], target.at[:, pl.ds(j * piece, piece)]))
    staged = [
        pltpu.make_async_copy(source, target, sems.at[n])
        for n, (source, target) in enumerate(staged)
    ]
    for copy in (*small, *staged):
        copy.start()
    for copy in small:
        copy.wait()

    steps, top, size = ids_held.shape
    tenant = column_of(tenants_held[...], size)
    lane = lax.broadcasted_iota(jnp.int32, (size, meta.shape[1]), 1)
    for s in range(steps):
        weight = jnp.zeros(lane.shape, F32)
        for k in range(top):
            expert = column_of(ids_held[s, k : k + 1], size).astype(jnp.int32)
            value = column_of(values_held[s, k : k + 1], size)
            weight = weight + jnp.where(expert == lane % experts, value, 0.0)
        high = weight.astype(BF16).astype(F32)
        middle = (weight - high).astype(BF16).astype(F32)
        low = weight - high - middle
        found = jnp.where(lane < experts, high, jnp.where(lane < 2 * experts, middle, low))
        found = jnp.where(lane < 3 * experts, found, tenant)
        meta[s * size : (s + 1) * size] = found.astype(BF16)

    tenant_count = pair_slot_held.shape[1]
    place = lax.broadcasted_iota(jnp.int32, pair_slot_held.shape, 0)
    own_row = jnp.sum(
        jnp.where(place == own, pair_slot_held[...].astype(F32), 0.0), axis=0, keepdims=True
    )
    own_slots = column_of(own_row, tenant_count).astype(jnp.int32)
    total = columns.shape[1]
    per_device = tenant_count // lax.axis_size("expert")
    shared_count, store_count = shared_b.shape[0], store_b.shape[0]
    rank = shared_count // per_device
    column = lax.broadcasted_iota(jnp.int32, (1, total), 1)
    shared_tenant = own * per_device + column % shared_count // rank
    slot = (own ^ (column // store_count)) * (store_count // rank) + column % store_count // rank
    tenant_number = lax.broadcasted_iota(jnp.int32, (tenant_count, total), 0)
    slot_tenant = jnp.max(jnp.where(own_slots == slot, tenant_number, -1), axis=0, keepdims=True)
    columns[0:1] = shared_tenant
    columns[1:2] = slot_tenant
    columns[2:3] = jnp.full((1, total), own, jnp.int32)
    columns[3:8] = jnp.zeros((5, total), jnp.int32)
    for copy in staged:
        copy.wait()


def first_call(experts, ids, values, tenants, pair_slot, staged):
    parts = lax.axis_size("tensor")
    steps, _, size = ids.shape
    columns = max(lax.axis_size("expert") * staged[1].shape[0], staged[2].shape[0])
    outs = [
        jax.ShapeDtypeStruct((steps * size, META), BF16),
        jax.ShapeDtypeStruct((8, columns), jnp.int32),
        *[vmem_shape(value) for value in staged],
    ]
    inputs = [ids, values, tenants, pair_slot, *staged]
    return pl.pallas_call(
        functools.partial(first_kernel, experts),
        in_specs=[HBM_SPEC] * len(inputs),
        out_specs=[VMEM_SPEC] * len(outs),
        out_shape=outs,
        scratch_shapes=[
            pltpu.VMEM(ids.shape, jnp.int32),
            pltpu.VMEM(values.shape, F32),
            pltpu.VMEM(tenants.shape, jnp.int32),
            pltpu.VMEM(pair_slot.shape, jnp.int32),
            pltpu.SemaphoreType.DMA((4,)),
            pltpu.SemaphoreType.DMA((5 + 6 * parts,)),
        ],
        compiler_params=params(4),
        cost_estimate=cost(0, 2 * sum(value.size for value in staged)),
    )(*[in_hbm(value) for value in inputs])


META = 128


def message_layout(count, store_count):
    wide = max(128, 2 * store_count)
    per = wide // (2 * store_count)
    return wide + META, per, -(-(count // 2) // per)


def message_kernel(chunk, *refs):
    half = len(refs) - 5
    rows, (factor, factor_other, store_b, meta, out) = refs[:half], refs[half:]
    size, depth = rows[0].shape
    store_count, width = store_b.shape
    total = 0.0
    for k in range(depth // chunk):
        part = pl.ds(k * chunk, chunk)
        total += lax.dot_general(
            jnp.concatenate([ref[:, part] for ref in rows], axis=0),
            jnp.concatenate([factor[:, part], factor_other[:, part]], axis=0),
            (((1,), (1,)), ((), ())),
            preferred_element_type=F32,
        )
    total = total.astype(BF16)
    wide, per, lines = message_layout(2 * half, store_count)
    out[:store_count, :width] = store_b[...]
    if width < wide:
        out[:store_count, width:] = jnp.zeros((store_count, wide - width), BF16)
    for line in range(lines):
        blocks = [
            total[n * size : (n + 1) * size] if n < half else jnp.zeros((size, 2 * store_count), BF16)
            for n in range(line * per, (line + 1) * per)
        ]
        blocks.append(meta[...] if line == 0 else jnp.zeros(meta.shape, BF16))
        start = store_count + line * size
        out[start : start + size] = jnp.concatenate(blocks, axis=1)


def make_message(rows, factor, factor_other, store_b, meta):
    size, depth = rows[0].shape
    store_count = store_b.shape[0]
    wide, _, lines = message_layout(2 * len(rows), store_count)
    inputs = [*rows, factor, factor_other, store_b, meta]
    return pl.pallas_call(
        functools.partial(message_kernel, 1024),
        in_specs=[VMEM_SPEC] * len(inputs),
        out_specs=VMEM_SPEC,
        out_shape=jax.ShapeDtypeStruct((store_count + lines * size, wide), BF16),
        compiler_params=params(8),
        cost_estimate=cost(4 * size * len(rows) * depth * store_count, 2 * depth * store_count * 2),
    )(*[in_vmem(value) for value in inputs])


def gate_up_kernel(count, chunk, *refs):
    rows, factor, weights, inner, outs = refs[:count], refs[count], refs[count + 1 : count + 5], refs[count + 5], refs[count + 6 :]
    depth = factor.shape[1]
    pieces = [pl.ds(k * chunk, chunk) for k in range(depth // chunk)]
    for weight, out in zip(weights, outs):
        total = jnp.zeros(out.shape, F32)
        for part in pieces:
            block = jnp.concatenate([ref[:, part] for ref in rows], axis=0)
            total += jnp.dot(block, weight[part], preferred_element_type=F32)
        out[...] = total
    total = jnp.zeros(inner.shape, F32)
    for part in pieces:
        block = jnp.concatenate([ref[:, part] for ref in rows], axis=0)
        total += lax.dot_general(
            block, factor[:, part], (((1,), (1,)), ((), ())), preferred_element_type=F32
        )
    inner[...] = total.astype(BF16)


def gate_up(rows, factor, weights):
    depth, width = weights[0].shape
    total = rows[0].shape[0] * len(rows)
    inputs = [*rows, factor, *weights]
    out = jax.ShapeDtypeStruct((total, width), F32)
    return pl.pallas_call(
        functools.partial(gate_up_kernel, len(rows), 1024),
        in_specs=[VMEM_SPEC] * len(inputs),
        out_specs=[VMEM_SPEC] * (1 + len(weights)),
        out_shape=[jax.ShapeDtypeStruct((total, factor.shape[0]), BF16)] + [out] * len(weights),
        compiler_params=params(12),
        cost_estimate=cost(2 * len(weights) * total * depth * width, 2 * len(weights) * depth * width),
    )(*[in_vmem(x) for x in inputs])


def silu(value):
    return value / (1.0 + jnp.exp(-value))


def down_blocks(hidden, hidden_shared, share, down, down_shared, outs, chunks, order):
    size = hidden.shape[0] // len(order)
    half = len(order) // 2
    part = outs[0].shape[-1]
    tile = tile_of(part)
    for n, chunk in enumerate(chunks):
        keep, send = outs[2 * n : 2 * n + 2]
        for place, j in enumerate(chunk):
            for c in range(part // tile):
                cut = slice(j * part + c * tile, j * part + (c + 1) * tile)
                routed = jnp.dot(hidden, down[:, cut], preferred_element_type=F32) * share
                routed += jnp.dot(hidden_shared, down_shared[:, cut], preferred_element_type=F32)
                for at, r in enumerate(order):
                    block = routed[r * size : (r + 1) * size].astype(BF16)
                    target, row = (keep, at) if at < half else (send, at - half)
                    target[row, place, :, c * tile : (c + 1) * tile] = block


def down_next_kernel(chunks, order, hidden, hidden_shared, share, down, down_shared, *outs):
    down_blocks(
        hidden[...], hidden_shared[...], share[:, :1], down, down_shared, outs, chunks, order
    )


def down_kernel(experts, chunks, order, *refs):
    count = len(order)
    half = count // 2
    near, far, refs = refs[:5], refs[5:10], refs[10:]
    columns, shared_b = refs[:2]
    messages = refs[2 : 2 + count]
    down, down_shared = refs[2 + count : 4 + count]
    hidden_out, hidden_shared_out, share_out = refs[4 + count : 7 + count]
    outs = refs[7 + count :]
    inner_shared, gate, up, gate_shared, up_shared = [
        jnp.concatenate([one[...], other[...]], axis=0) for one, other in zip(near, far)
    ]
    total, width = gate.shape
    size = total // count
    shared_count = shared_b.shape[0]
    store_count = columns.shape[1] // count
    wide, per, _ = message_layout(count, store_count)
    own = columns[2:3, :1]

    meta = jnp.concatenate(
        [ref[store_count : store_count + size, wide - META :] for ref in messages], axis=0
    ).astype(F32)
    lane = lax.broadcasted_iota(jnp.int32, meta.shape, 1)
    mine = (lane < 3 * experts) & (lane % experts == own)
    share = jnp.sum(jnp.where(mine, meta, 0.0), axis=1, keepdims=True)
    row_tenant = jnp.sum(jnp.where(lane == 3 * experts, meta, 0.0), axis=1, keepdims=True)
    row_tenant = row_tenant.astype(jnp.int32)

    lifted = []
    for k in range(count):
        parts = []
        for h in range(0, count, 2):
            sender = h + k % 2
            n = (k ^ sender) // 2
            rows = slice(store_count + n // per * size, store_count + (n // per + 1) * size)
            lanes = slice(n % per * 2 * store_count, (n % per + 1) * 2 * store_count)
            block = messages[sender][rows, lanes]
            if k % 2:
                block = jnp.concatenate([block[:, store_count:], block[:, :store_count]], axis=1)
            parts.append(block)
        lifted.append(jnp.concatenate(parts, axis=1))
    lifted = jnp.concatenate(lifted, axis=0)
    zero = jnp.zeros((), BF16)
    lifted = jnp.where(row_tenant == columns[1:2], lifted, zero)
    shared_tenant = columns[0:1, :shared_count]
    lifted_shared = jnp.where(row_tenant == shared_tenant, inner_shared, zero)
    factor = jnp.concatenate([ref[:store_count, :width] for ref in messages], axis=0)
    upward = up + jnp.dot(lifted, factor, preferred_element_type=F32)
    hidden = (silu(gate) * upward).astype(BF16)
    upward = up_shared + jnp.dot(lifted_shared, shared_b[...], preferred_element_type=F32)
    here = (row_tenant >= shared_tenant[:, :1]) & (row_tenant <= shared_tenant[:, shared_count - 1 :])
    hidden_shared = jnp.where(here, silu(gate_shared) * upward, 0.0).astype(BF16)

    hidden_out[...] = hidden
    hidden_shared_out[...] = hidden_shared
    share_out[...] = jnp.broadcast_to(share, share_out.shape)
    down_blocks(hidden, hidden_shared, share, down, down_shared, outs, chunks, order)


def down_outs(rows, depth, chunks, order):
    size = rows // len(order)
    part = depth // lax.axis_size("tensor")
    outs = []
    for chunk in chunks:
        outs += [jax.ShapeDtypeStruct((len(order) // 2, len(chunk), size, part), BF16)] * 2
    return outs


def down_cost(rows, down, chunks):
    part = sum(len(chunk) for chunk in chunks) * down.size // lax.axis_size("tensor")
    return cost(4 * rows * part, 4 * part)


def down_products(near, far, columns, shared_b, messages, down, down_shared, experts, chunks, order):
    rows, width = near[1].shape[0] + far[1].shape[0], near[1].shape[1]
    whole = [*near, *far, columns, shared_b, *messages, down, down_shared]
    outs = [jax.ShapeDtypeStruct((rows, width), BF16)] * 2
    outs += [jax.ShapeDtypeStruct((rows, 128), F32)]
    outs += down_outs(rows, down.shape[1], chunks, order)
    return pl.pallas_call(
        functools.partial(down_kernel, experts, chunks, order),
        in_specs=[VMEM_SPEC] * len(whole),
        out_specs=[VMEM_SPEC] * len(outs),
        out_shape=outs,
        compiler_params=params(16),
        cost_estimate=down_cost(rows, down, chunks),
    )(*[in_vmem(x) for x in whole])


def down_next(hidden, down, down_shared, chunks, order):
    rows = hidden[0].shape[0]
    whole = [*hidden, down, down_shared]
    outs = down_outs(rows, down.shape[1], chunks, order)
    return pl.pallas_call(
        functools.partial(down_next_kernel, chunks, order),
        in_specs=[VMEM_SPEC] * len(whole),
        out_specs=[VMEM_SPEC] * len(outs),
        out_shape=outs,
        compiler_params=params(16),
        cost_estimate=down_cost(rows, down, chunks),
    )(*[in_vmem(x) for x in whole])


def local(
    tokens,
    expert_ids,
    gate_values,
    tenant_ids,
    w_gate,
    w_up,
    routed_down_weight,
    shared_gate,
    shared_up,
    shared_down,
    store_a,
    store_b,
    pair_slot,
    shared_a,
    shared_b,
):
    experts = pair_slot.shape[0]
    adapted, rank, model_width = store_a.shape
    hid = store_b.shape[2]
    steps, size, _ = expert_ids.shape
    count = lax.axis_size("expert")
    n_tensor = lax.axis_size("tensor")
    shared_count, store_count = shared_a.shape[0] * rank, adapted * rank

    rows_own = tokens.reshape(steps * size, model_width)
    arrived = swap(rows_own, count // 2)
    store_other = swap(store_a, 1).reshape(store_count, model_width)
    first = first_call(
        experts,
        jnp.swapaxes(expert_ids, 1, 2),
        jnp.swapaxes(gate_values, 1, 2),
        tenant_ids.reshape(1, size),
        pair_slot,
        [
            rows_own,
            store_b.reshape(store_count, hid),
            shared_b.reshape(shared_count, hid),
            store_a.reshape(store_count, model_width),
            shared_a.reshape(shared_count, model_width),
            w_gate[0],
            w_up[0],
            shared_gate,
            shared_up,
            routed_down_weight[0],
            shared_down,
        ],
    )
    meta, columns, rows_held, store_b_held, shared_b_held, factor_store, factor_shared = first[:7]
    weights, down, down_own = first[7:11], first[11], first[12]
    near = gate_up([rows_held, swap(rows_own, 1)], factor_shared, weights)
    arrived, near, store_other, rows_held = lax.optimization_barrier(
        (arrived, near, store_other, rows_held)
    )
    came = far_rows(arrived, rows_own)
    message = make_message([rows_held, *came], factor_store, store_other, store_b_held, meta)
    messages = [message] + [swap(message, r) for r in range(1, count)]
    came, message = lax.optimization_barrier((came, message))
    rows = []
    for value in came:
        rows += [value, swap(value, 1)]
    far = gate_up(rows, factor_shared, weights)

    order = [0]
    bit = count // 2
    while bit >= 1:
        order = order + [r | bit for r in order]
        bit //= 2
    chunks = [[j] for j in range(n_tensor - 1, 1, -1)] + [[1, 0]]
    hidden = down_products(
        near, far, columns, shared_b_held, messages, down, down_own, experts, chunks[:-1], order
    )
    hidden, outs = hidden[:3], list(hidden[3:])
    outs += down_next(hidden, down, down_own, chunks[-1:], order)
    held, leaving = list(outs[0::2]), list(outs[1::2])
    bit = 1
    while bit < count:
        half = count // (2 * bit) // 2
        if bit > 1:
            leaving[1], *_ = lax.optimization_barrier((leaving[1], leaving[0]))
        arrived = [swap(value, bit) for value in leaving]
        if bit > 1:
            arrived[0], *_ = lax.optimization_barrier((arrived[0], *leaving))
        if 2 * bit < count:
            leaving = [add(h[half:], a[half:]) for h, a in zip(held, arrived)]
            held = [add(h[:half], a[:half]) for h, a in zip(held, arrived)]
        bit *= 2
    parts = {}
    for n, chunk in enumerate(chunks):
        for place, j in enumerate(chunk):
            parts[j] = [held[n][0, place], arrived[n][0, place]]
    bit = 1
    while bit < n_tensor:
        for j in sorted([j for j in parts if j & bit], reverse=True):
            parts[j ^ bit].append(swap(total_of(parts.pop(j)), bit, "tensor"))
        bit *= 2
    return total_of(parts[0]).reshape(steps, size, model_width // n_tensor)


def solution(mesh):
    return jax.shard_map(
        local,
        mesh=mesh,
        in_specs=(
            P(None, ("groups", "expert"), None),
            P(None, ("groups", "expert"), None),
            P(None, ("groups", "expert"), None),
            P(("groups", "expert")),
            P("expert", None, "tensor"),
            P("expert", None, "tensor"),
            P("expert", "tensor", None),
            P(None, "tensor"),
            P(None, "tensor"),
            P("tensor", None),
            P("expert", None, None),
            P("expert", None, "tensor"),
            P(),
            P("expert", None, None),
            P("expert", None, "tensor"),
        ),
        out_specs=P(None, ("groups", "expert"), "tensor"),
        check_vma=False,
    )
```

```python
import functools

import jax
import jax.numpy as jnp
from jax import lax
from jax.experimental import pallas as pl
from jax.experimental.pallas import tpu as pltpu
from jax.sharding import PartitionSpec as P

F32 = jnp.float32
BF16 = jnp.bfloat16
MIB = 1024 * 1024


def params(mebibytes):
    return pltpu.CompilerParams(vmem_limit_bytes=mebibytes * MIB)


def cost(flops, moved):
    return pl.CostEstimate(flops=int(flops), bytes_accessed=int(moved), transcendentals=0)


def in_vmem(value):
    return pltpu.with_memory_space_constraint(value, pltpu.VMEM)


def in_hbm(value):
    return pltpu.with_memory_space_constraint(value, pltpu.HBM)


def vmem_shape(value):
    return pltpu.VMEM(value.shape, value.dtype)


VMEM_SPEC = pl.BlockSpec(memory_space=pltpu.VMEM)
HBM_SPEC = pl.BlockSpec(memory_space=pltpu.HBM)


def swap(value, bits, axis="expert"):
    count = lax.axis_size(axis)
    return lax.ppermute(value, axis, [(i, i ^ bits) for i in range(count)])


def add(one, other):
    return (one.astype(F32) + other.astype(F32)).astype(BF16)


def total_of(values):
    return sum(value.astype(F32) for value in values).astype(BF16)


def far_rows(arrived, rows_own):
    count = lax.axis_size("expert")
    bit = count // 2
    pieces = {0: rows_own, bit: arrived}
    bit //= 2
    while bit > 1:
        pieces.update({r ^ bit: swap(piece, bit) for r, piece in list(pieces.items())})
        bit //= 2
    return [pieces[r] for r in range(2, count, 2)]


def tile_of(width):
    return 256 if width % 256 == 0 else 128


def column_of(row, size):
    lane = lax.broadcasted_iota(jnp.int32, (size, row.shape[1]), 1)
    place = lax.broadcasted_iota(jnp.int32, (size, row.shape[1]), 0)
    return jnp.sum(jnp.where(lane == place, row.astype(F32), 0.0), axis=1, keepdims=True)


def first_kernel(
    experts, ids, values, tenants, pair_slot, rows, store_b, shared_b, factor_store, factor_shared,
    gate_weight, up_weight, gate_shared, up_shared, down, down_shared, meta, columns, *refs
):
    targets, (ids_held, values_held, tenants_held, pair_slot_held, small_sems, sems) = refs[:-6], refs[-6:]
    own, own_part = lax.axis_index("expert"), lax.axis_index("tensor")
    parts = lax.axis_size("tensor")
    small = [
        (ids, ids_held), (values, values_held), (tenants, tenants_held), (pair_slot, pair_slot_held)
    ]
    small = [
        pltpu.make_async_copy(source, target, small_sems.at[n])
        for n, (source, target) in enumerate(small)
    ]
    sources = [
        rows, store_b, shared_b, factor_store, factor_shared, gate_weight, up_weight, gate_shared,
        up_shared, down, down_shared,
    ]
    staged = list(zip(sources[:5], targets[:5]))
    piece = gate_weight.shape[0] // parts
    for source, target in zip(sources[5:9], targets[5:9]):
        for k in range(parts):
            part = pl.ds(k * piece, piece)
            staged.append((source.at[part], target.at[part]))
    for source, target in zip(sources[9:], targets[9:]):
        for j in range(parts):
            start = pl.multiple_of((own_part ^ j) * piece, piece)
            staged.append((source.at[:, pl.ds(start, piece)], target.at[:, pl.ds(j * piece, piece)]))
    staged = [
        pltpu.make_async_copy(source, target, sems.at[n])
        for n, (source, target) in enumerate(staged)
    ]
    for copy in (*small, *staged):
        copy.start()
    for copy in small:
        copy.wait()

    steps, top, size = ids_held.shape
    tenant = column_of(tenants_held[...], size)
    lane = lax.broadcasted_iota(jnp.int32, (size, meta.shape[1]), 1)
    for s in range(steps):
        weight = jnp.zeros(lane.shape, F32)
        for k in range(top):
            expert = column_of(ids_held[s, k : k + 1], size).astype(jnp.int32)
            value = column_of(values_held[s, k : k + 1], size)
            weight = weight + jnp.where(expert == lane % experts, value, 0.0)
        high = weight.astype(BF16).astype(F32)
        middle = (weight - high).astype(BF16).astype(F32)
        low = weight - high - middle
        found = jnp.where(lane < experts, high, jnp.where(lane < 2 * experts, middle, low))
        found = jnp.where(lane < 3 * experts, found, tenant)
        meta[s * size : (s + 1) * size] = found.astype(BF16)

    tenant_count = pair_slot_held.shape[1]
    place = lax.broadcasted_iota(jnp.int32, pair_slot_held.shape, 0)
    own_row = jnp.sum(
        jnp.where(place == own, pair_slot_held[...].astype(F32), 0.0), axis=0, keepdims=True
    )
    own_slots = column_of(own_row, tenant_count).astype(jnp.int32)
    total = columns.shape[1]
    per_device = tenant_count // lax.axis_size("expert")
    shared_count, store_count = shared_b.shape[0], store_b.shape[0]
    rank = shared_count // per_device
    column = lax.broadcasted_iota(jnp.int32, (1, total), 1)
    shared_tenant = own * per_device + column % shared_count // rank
    slot = (own ^ (column // store_count)) * (store_count // rank) + column % store_count // rank
    tenant_number = lax.broadcasted_iota(jnp.int32, (tenant_count, total), 0)
    slot_tenant = jnp.max(jnp.where(own_slots == slot, tenant_number, -1), axis=0, keepdims=True)
    columns[0:1] = shared_tenant
    columns[1:2] = slot_tenant
    columns[2:3] = jnp.full((1, total), own, jnp.int32)
    columns[3:8] = jnp.zeros((5, total), jnp.int32)
    for copy in staged:
        copy.wait()


def first_call(experts, ids, values, tenants, pair_slot, staged):
    parts = lax.axis_size("tensor")
    steps, _, size = ids.shape
    columns = max(lax.axis_size("expert") * staged[1].shape[0], staged[2].shape[0])
    outs = [
        jax.ShapeDtypeStruct((steps * size, META), BF16),
        jax.ShapeDtypeStruct((8, columns), jnp.int32),
        *[vmem_shape(value) for value in staged],
    ]
    inputs = [ids, values, tenants, pair_slot, *staged]
    return pl.pallas_call(
        functools.partial(first_kernel, experts),
        in_specs=[HBM_SPEC] * len(inputs),
        out_specs=[VMEM_SPEC] * len(outs),
        out_shape=outs,
        scratch_shapes=[
            pltpu.VMEM(ids.shape, jnp.int32),
            pltpu.VMEM(values.shape, F32),
            pltpu.VMEM(tenants.shape, jnp.int32),
            pltpu.VMEM(pair_slot.shape, jnp.int32),
            pltpu.SemaphoreType.DMA((4,)),
            pltpu.SemaphoreType.DMA((5 + 6 * parts,)),
        ],
        compiler_params=params(4),
        cost_estimate=cost(0, 2 * sum(value.size for value in staged)),
    )(*[in_hbm(value) for value in inputs])


META = 128


def message_layout(count, store_count):
    wide = max(128, 2 * store_count)
    per = wide // (2 * store_count)
    return wide + META, per, -(-(count // 2) // per)


def message_kernel(chunk, *refs):
    half = len(refs) - 5
    rows, (factor, factor_other, store_b, meta, out) = refs[:half], refs[half:]
    size, depth = rows[0].shape
    store_count, width = store_b.shape
    total = 0.0
    for k in range(depth // chunk):
        part = pl.ds(k * chunk, chunk)
        total += lax.dot_general(
            jnp.concatenate([ref[:, part] for ref in rows], axis=0),
            jnp.concatenate([factor[:, part], factor_other[:, part]], axis=0),
            (((1,), (1,)), ((), ())),
            preferred_element_type=F32,
        )
    total = total.astype(BF16)
    wide, per, lines = message_layout(2 * half, store_count)
    out[:store_count, :width] = store_b[...]
    if width < wide:
        out[:store_count, width:] = jnp.zeros((store_count, wide - width), BF16)
    for line in range(lines):
        blocks = [
            total[n * size : (n + 1) * size] if n < half else jnp.zeros((size, 2 * store_count), BF16)
            for n in range(line * per, (line + 1) * per)
        ]
        blocks.append(meta[...] if line == 0 else jnp.zeros(meta.shape, BF16))
        start = store_count + line * size
        out[start : start + size] = jnp.concatenate(blocks, axis=1)


def make_message(rows, factor, factor_other, store_b, meta):
    size, depth = rows[0].shape
    store_count = store_b.shape[0]
    wide, _, lines = message_layout(2 * len(rows), store_count)
    inputs = [*rows, factor, factor_other, store_b, meta]
    return pl.pallas_call(
        functools.partial(message_kernel, 1024),
        in_specs=[VMEM_SPEC] * len(inputs),
        out_specs=VMEM_SPEC,
        out_shape=jax.ShapeDtypeStruct((store_count + lines * size, wide), BF16),
        compiler_params=params(8),
        cost_estimate=cost(4 * size * len(rows) * depth * store_count, 2 * depth * store_count * 2),
    )(*[in_vmem(value) for value in inputs])


def gate_up_kernel(count, chunk, *refs):
    rows, factor, weights, inner, outs = refs[:count], refs[count], refs[count + 1 : count + 5], refs[count + 5], refs[count + 6 :]
    depth = factor.shape[1]
    pieces = [pl.ds(k * chunk, chunk) for k in range(depth // chunk)]
    for weight, out in zip(weights, outs):
        total = jnp.zeros(out.shape, F32)
        for part in pieces:
            block = jnp.concatenate([ref[:, part] for ref in rows], axis=0)
            total += jnp.dot(block, weight[part], preferred_element_type=F32)
        out[...] = total
    total = jnp.zeros(inner.shape, F32)
    for part in pieces:
        block = jnp.concatenate([ref[:, part] for ref in rows], axis=0)
        total += lax.dot_general(
            block, factor[:, part], (((1,), (1,)), ((), ())), preferred_element_type=F32
        )
    inner[...] = total.astype(BF16)


def gate_up(rows, factor, weights):
    depth, width = weights[0].shape
    total = rows[0].shape[0] * len(rows)
    inputs = [*rows, factor, *weights]
    out = jax.ShapeDtypeStruct((total, width), F32)
    return pl.pallas_call(
        functools.partial(gate_up_kernel, len(rows), 1024),
        in_specs=[VMEM_SPEC] * len(inputs),
        out_specs=[VMEM_SPEC] * (1 + len(weights)),
        out_shape=[jax.ShapeDtypeStruct((total, factor.shape[0]), BF16)] + [out] * len(weights),
        compiler_params=params(12),
        cost_estimate=cost(2 * len(weights) * total * depth * width, 2 * len(weights) * depth * width),
    )(*[in_vmem(x) for x in inputs])


def silu(value):
    return value / (1.0 + jnp.exp(-value))


def down_blocks(hidden, hidden_shared, share, down, down_shared, outs, chunks, order):
    size = hidden.shape[0] // len(order)
    half = len(order) // 2
    part = outs[0].shape[-1]
    tile = tile_of(part)
    for n, chunk in enumerate(chunks):
        keep, send = outs[2 * n : 2 * n + 2]
        for place, j in enumerate(chunk):
            for c in range(part // tile):
                cut = slice(j * part + c * tile, j * part + (c + 1) * tile)
                routed = jnp.dot(hidden, down[:, cut], preferred_element_type=F32) * share
                routed += jnp.dot(hidden_shared, down_shared[:, cut], preferred_element_type=F32)
                for at, r in enumerate(order):
                    block = routed[r * size : (r + 1) * size].astype(BF16)
                    target, row = (keep, at) if at < half else (send, at - half)
                    target[row, place, :, c * tile : (c + 1) * tile] = block


def down_next_kernel(chunks, order, hidden, hidden_shared, share, down, down_shared, *outs):
    down_blocks(
        hidden[...], hidden_shared[...], share[:, :1], down, down_shared, outs, chunks, order
    )


def down_kernel(experts, chunks, order, *refs):
    count = len(order)
    half = count // 2
    inner_shared, gate, up, gate_shared, up_shared = [ref[...] for ref in refs[:5]]
    refs = refs[5:]
    columns, shared_b = refs[:2]
    messages = refs[2 : 2 + count]
    down, down_shared = refs[2 + count : 4 + count]
    hidden_out, hidden_shared_out, share_out = refs[4 + count : 7 + count]
    outs = refs[7 + count :]
    total, width = gate.shape
    size = total // count
    shared_count = shared_b.shape[0]
    store_count = columns.shape[1] // count
    wide, per, _ = message_layout(count, store_count)
    own = columns[2:3, :1]

    meta = jnp.concatenate(
        [ref[store_count : store_count + size, wide - META :] for ref in messages], axis=0
    ).astype(F32)
    lane = lax.broadcasted_iota(jnp.int32, meta.shape, 1)
    mine = (lane < 3 * experts) & (lane % experts == own)
    share = jnp.sum(jnp.where(mine, meta, 0.0), axis=1, keepdims=True)
    row_tenant = jnp.sum(jnp.where(lane == 3 * experts, meta, 0.0), axis=1, keepdims=True)
    row_tenant = row_tenant.astype(jnp.int32)

    lifted = []
    for k in range(count):
        parts = []
        for h in range(0, count, 2):
            sender = h + k % 2
            n = (k ^ sender) // 2
            rows = slice(store_count + n // per * size, store_count + (n // per + 1) * size)
            lanes = slice(n % per * 2 * store_count, (n % per + 1) * 2 * store_count)
            block = messages[sender][rows, lanes]
            if k % 2:
                block = jnp.concatenate([block[:, store_count:], block[:, :store_count]], axis=1)
            parts.append(block)
        lifted.append(jnp.concatenate(parts, axis=1))
    lifted = jnp.concatenate(lifted, axis=0)
    zero = jnp.zeros((), BF16)
    lifted = jnp.where(row_tenant == columns[1:2], lifted, zero)
    shared_tenant = columns[0:1, :shared_count]
    lifted_shared = jnp.where(row_tenant == shared_tenant, inner_shared, zero)
    factor = jnp.concatenate([ref[:store_count, :width] for ref in messages], axis=0)
    upward = up + jnp.dot(lifted, factor, preferred_element_type=F32)
    hidden = (silu(gate) * upward).astype(BF16)
    upward = up_shared + jnp.dot(lifted_shared, shared_b[...], preferred_element_type=F32)
    here = (row_tenant >= shared_tenant[:, :1]) & (row_tenant <= shared_tenant[:, shared_count - 1 :])
    hidden_shared = jnp.where(here, silu(gate_shared) * upward, 0.0).astype(BF16)

    hidden_out[...] = hidden
    hidden_shared_out[...] = hidden_shared
    share_out[...] = jnp.broadcast_to(share, share_out.shape)
    down_blocks(hidden, hidden_shared, share, down, down_shared, outs, chunks, order)


def down_outs(rows, depth, chunks, order):
    size = rows // len(order)
    part = depth // lax.axis_size("tensor")
    outs = []
    for chunk in chunks:
        outs += [jax.ShapeDtypeStruct((len(order) // 2, len(chunk), size, part), BF16)] * 2
    return outs


def down_cost(rows, down, chunks):
    part = sum(len(chunk) for chunk in chunks) * down.size // lax.axis_size("tensor")
    return cost(4 * rows * part, 0)


def down_products(gated, columns, shared_b, messages, down, down_shared, experts, chunks, order):
    rows, width = gated[1].shape
    whole = [*gated, columns, shared_b, *messages, down, down_shared]
    outs = [jax.ShapeDtypeStruct((rows, width), BF16)] * 2
    outs += [jax.ShapeDtypeStruct((rows, 128), F32)]
    outs += down_outs(rows, down.shape[1], chunks, order)
    return pl.pallas_call(
        functools.partial(down_kernel, experts, chunks, order),
        in_specs=[VMEM_SPEC] * len(whole),
        out_specs=[VMEM_SPEC] * len(outs),
        out_shape=outs,
        compiler_params=params(16),
        cost_estimate=down_cost(rows, down, chunks),
    )(*[in_vmem(x) for x in whole])


def down_next(hidden, down, down_shared, chunks, order):
    rows = hidden[0].shape[0]
    whole = [*hidden, down, down_shared]
    outs = down_outs(rows, down.shape[1], chunks, order)
    return pl.pallas_call(
        functools.partial(down_next_kernel, chunks, order),
        in_specs=[VMEM_SPEC] * len(whole),
        out_specs=[VMEM_SPEC] * len(outs),
        out_shape=outs,
        compiler_params=params(16),
        cost_estimate=down_cost(rows, down, chunks),
    )(*[in_vmem(x) for x in whole])


def local(
    tokens,
    expert_ids,
    gate_values,
    tenant_ids,
    w_gate,
    w_up,
    routed_down_weight,
    shared_gate,
    shared_up,
    shared_down,
    store_a,
    store_b,
    pair_slot,
    shared_a,
    shared_b,
):
    experts = pair_slot.shape[0]
    adapted, rank, model_width = store_a.shape
    hid = store_b.shape[2]
    steps, size, _ = expert_ids.shape
    count = lax.axis_size("expert")
    n_tensor = lax.axis_size("tensor")
    shared_count, store_count = shared_a.shape[0] * rank, adapted * rank

    rows_own = tokens.reshape(steps * size, model_width)
    arrived = swap(rows_own, count // 2)
    store_other = swap(store_a, 1).reshape(store_count, model_width)
    first = first_call(
        experts,
        jnp.swapaxes(expert_ids, 1, 2),
        jnp.swapaxes(gate_values, 1, 2),
        tenant_ids.reshape(1, size),
        pair_slot,
        [
            rows_own,
            store_b.reshape(store_count, hid),
            shared_b.reshape(shared_count, hid),
            store_a.reshape(store_count, model_width),
            shared_a.reshape(shared_count, model_width),
            w_gate[0],
            w_up[0],
            shared_gate,
            shared_up,
            routed_down_weight[0],
            shared_down,
        ],
    )
    meta, columns, rows_held, store_b_held, shared_b_held, factor_store, factor_shared = first[:7]
    weights, down, down_own = first[7:11], first[11], first[12]
    arrived, rows_held, store_other = lax.optimization_barrier((arrived, rows_held, store_other))
    came = far_rows(arrived, rows_own)
    message = make_message([rows_held, *came], factor_store, store_other, store_b_held, meta)
    messages = [message] + [swap(message, r) for r in range(1, count)]
    came, message = lax.optimization_barrier((came, message))
    rows = [rows_held, swap(rows_own, 1)]
    for value in came:
        rows += [value, swap(value, 1)]
    gated = gate_up(rows, factor_shared, weights)

    order = [0]
    bit = count // 2
    while bit >= 1:
        order = order + [r | bit for r in order]
        bit //= 2
    chunks = [[j] for j in range(n_tensor - 1, -1, -1)]
    hidden = down_products(
        gated, columns, shared_b_held, messages, down, down_own, experts, chunks[:-2], order
    )
    hidden, held, leaving = hidden[:3], list(hidden[3::2]), list(hidden[4::2])
    bit = 1
    while bit < count:
        half = count // (2 * bit) // 2
        if bit > 1:
            leaving[1], *_ = lax.optimization_barrier((leaving[1], leaving[0]))
        arrived = [swap(value, bit) for value in (leaving if bit == 1 else leaving[:-1])]
        if bit == 1:
            ready = add(held[0][half:], arrived[0][half:])
            hidden, ready = lax.optimization_barrier((hidden, ready))
            rest = down_next(hidden, down, down_own, chunks[len(held) :], order)
            held += rest[0::2]
            arrived += [swap(value, bit) for value in rest[1::2]]
        else:
            arrived[0], *leaving = lax.optimization_barrier((arrived[0], *leaving))
            arrived.append(swap(leaving[-1], bit))
        if 2 * bit < count:
            leaving = [add(h[half:], a[half:]) for h, a in zip(held, arrived)]
            held = [add(h[:half], a[:half]) for h, a in zip(held, arrived)]
        bit *= 2
    parts = {}
    for n, chunk in enumerate(chunks):
        for place, j in enumerate(chunk):
            parts[j] = [held[n][0, place], arrived[n][0, place]]
    bit = 1
    while bit < n_tensor:
        for j in sorted([j for j in parts if j & bit], reverse=True):
            parts[j ^ bit].append(swap(total_of(parts.pop(j)), bit, "tensor"))
        bit *= 2
    return total_of(parts[0]).reshape(steps, size, model_width // n_tensor)


def solution(mesh):
    return jax.shard_map(
        local,
        mesh=mesh,
        in_specs=(
            P(None, ("groups", "expert"), None),
            P(None, ("groups", "expert"), None),
            P(None, ("groups", "expert"), None),
            P(("groups", "expert")),
            P("expert", None, "tensor"),
            P("expert", None, "tensor"),
            P("expert", "tensor", None),
            P(None, "tensor"),
            P(None, "tensor"),
            P("tensor", None),
            P("expert", None, None),
            P("expert", None, "tensor"),
            P(),
            P("expert", None, None),
            P("expert", None, "tensor"),
        ),
        out_specs=P(None, ("groups", "expert"), "tensor"),
        check_vma=False,
    )
```

```python
import functools

import jax
import jax.numpy as jnp
from jax import lax
from jax.experimental import pallas as pl
from jax.experimental.pallas import tpu as pltpu
from jax.sharding import PartitionSpec as P

F32 = jnp.float32
BF16 = jnp.bfloat16
MIB = 1024 * 1024


def params(mebibytes):
    return pltpu.CompilerParams(vmem_limit_bytes=mebibytes * MIB)


def cost(flops, moved):
    return pl.CostEstimate(flops=int(flops), bytes_accessed=int(moved), transcendentals=0)


def in_vmem(value):
    return pltpu.with_memory_space_constraint(value, pltpu.VMEM)


def in_hbm(value):
    return pltpu.with_memory_space_constraint(value, pltpu.HBM)


def vmem_shape(value):
    return pltpu.VMEM(value.shape, value.dtype)


VMEM_SPEC = pl.BlockSpec(memory_space=pltpu.VMEM)
HBM_SPEC = pl.BlockSpec(memory_space=pltpu.HBM)


def swap(value, bits, axis="expert"):
    count = lax.axis_size(axis)
    return lax.ppermute(value, axis, [(i, i ^ bits) for i in range(count)])


def add(one, other):
    return (one.astype(F32) + other.astype(F32)).astype(BF16)


def total_of(values):
    return sum(value.astype(F32) for value in values).astype(BF16)


def far_rows(arrived, rows_own):
    count = lax.axis_size("expert")
    bit = count // 2
    pieces = {0: rows_own, bit: arrived}
    bit //= 2
    while bit > 1:
        pieces.update({r ^ bit: swap(piece, bit) for r, piece in list(pieces.items())})
        bit //= 2
    return [pieces[r] for r in range(2, count, 2)]


def tile_of(width):
    return 256 if width % 256 == 0 else 128


def column_of(row, size):
    lane = lax.broadcasted_iota(jnp.int32, (size, row.shape[1]), 1)
    place = lax.broadcasted_iota(jnp.int32, (size, row.shape[1]), 0)
    return jnp.sum(jnp.where(lane == place, row.astype(F32), 0.0), axis=1, keepdims=True)


def first_kernel(
    experts, ids, values, tenants, pair_slot, rows, store_b, shared_b, factor_store, factor_shared,
    gate_weight, up_weight, gate_shared, up_shared, down, down_shared, meta, columns, *refs
):
    targets, (ids_held, values_held, tenants_held, pair_slot_held, small_sems, sems) = refs[:-6], refs[-6:]
    own, own_part = lax.axis_index("expert"), lax.axis_index("tensor")
    parts = lax.axis_size("tensor")
    small = [
        (ids, ids_held), (values, values_held), (tenants, tenants_held), (pair_slot, pair_slot_held)
    ]
    small = [
        pltpu.make_async_copy(source, target, small_sems.at[n])
        for n, (source, target) in enumerate(small)
    ]
    sources = [
        rows, store_b, shared_b, factor_store, factor_shared, gate_weight, up_weight, gate_shared,
        up_shared, down, down_shared,
    ]
    staged = list(zip(sources[:5], targets[:5]))
    piece = gate_weight.shape[0] // parts
    for source, target in zip(sources[5:9], targets[5:9]):
        for k in range(parts):
            part = pl.ds(k * piece, piece)
            staged.append((source.at[part], target.at[part]))
    for source, target in zip(sources[9:], targets[9:]):
        for j in range(parts):
            start = pl.multiple_of((own_part ^ j) * piece, piece)
            staged.append((source.at[:, pl.ds(start, piece)], target.at[:, pl.ds(j * piece, piece)]))
    staged = [
        pltpu.make_async_copy(source, target, sems.at[n])
        for n, (source, target) in enumerate(staged)
    ]
    for copy in (*small, *staged):
        copy.start()
    for copy in small:
        copy.wait()

    steps, top, size = ids_held.shape
    tenant = column_of(tenants_held[...], size)
    lane = lax.broadcasted_iota(jnp.int32, (size, meta.shape[1]), 1)
    for s in range(steps):
        weight = jnp.zeros(lane.shape, F32)
        for k in range(top):
            expert = column_of(ids_held[s, k : k + 1], size).astype(jnp.int32)
            value = column_of(values_held[s, k : k + 1], size)
            weight = weight + jnp.where(expert == lane % experts, value, 0.0)
        high = weight.astype(BF16).astype(F32)
        middle = (weight - high).astype(BF16).astype(F32)
        low = weight - high - middle
        found = jnp.where(lane < experts, high, jnp.where(lane < 2 * experts, middle, low))
        found = jnp.where(lane < 3 * experts, found, tenant)
        meta[s * size : (s + 1) * size] = found.astype(BF16)

    tenant_count = pair_slot_held.shape[1]
    place = lax.broadcasted_iota(jnp.int32, pair_slot_held.shape, 0)
    own_row = jnp.sum(
        jnp.where(place == own, pair_slot_held[...].astype(F32), 0.0), axis=0, keepdims=True
    )
    own_slots = column_of(own_row, tenant_count).astype(jnp.int32)
    total = columns.shape[1]
    per_device = tenant_count // lax.axis_size("expert")
    shared_count, store_count = shared_b.shape[0], store_b.shape[0]
    rank = shared_count // per_device
    column = lax.broadcasted_iota(jnp.int32, (1, total), 1)
    shared_tenant = own * per_device + column % shared_count // rank
    slot = (own ^ (column // store_count)) * (store_count // rank) + column % store_count // rank
    tenant_number = lax.broadcasted_iota(jnp.int32, (tenant_count, total), 0)
    slot_tenant = jnp.max(jnp.where(own_slots == slot, tenant_number, -1), axis=0, keepdims=True)
    columns[0:1] = shared_tenant
    columns[1:2] = slot_tenant
    columns[2:3] = jnp.full((1, total), own, jnp.int32)
    columns[3:8] = jnp.zeros((5, total), jnp.int32)
    for copy in staged:
        copy.wait()


def first_call(experts, ids, values, tenants, pair_slot, staged):
    parts = lax.axis_size("tensor")
    steps, _, size = ids.shape
    columns = max(lax.axis_size("expert") * staged[1].shape[0], staged[2].shape[0])
    outs = [
        jax.ShapeDtypeStruct((steps * size, META), BF16),
        jax.ShapeDtypeStruct((8, columns), jnp.int32),
        *[vmem_shape(value) for value in staged],
    ]
    inputs = [ids, values, tenants, pair_slot, *staged]
    return pl.pallas_call(
        functools.partial(first_kernel, experts),
        in_specs=[HBM_SPEC] * len(inputs),
        out_specs=[VMEM_SPEC] * len(outs),
        out_shape=outs,
        scratch_shapes=[
            pltpu.VMEM(ids.shape, jnp.int32),
            pltpu.VMEM(values.shape, F32),
            pltpu.VMEM(tenants.shape, jnp.int32),
            pltpu.VMEM(pair_slot.shape, jnp.int32),
            pltpu.SemaphoreType.DMA((4,)),
            pltpu.SemaphoreType.DMA((5 + 6 * parts,)),
        ],
        compiler_params=params(4),
        cost_estimate=cost(0, 2 * sum(value.size for value in staged)),
    )(*[in_hbm(value) for value in inputs])


META = 128


def message_layout(count, store_count):
    wide = max(128, 2 * store_count)
    per = wide // (2 * store_count)
    return wide + META, per, -(-(count // 2) // per)


def message_kernel(chunk, *refs):
    half = len(refs) - 5
    rows, (factor, factor_other, store_b, meta, out) = refs[:half], refs[half:]
    size, depth = rows[0].shape
    store_count, width = store_b.shape
    total = 0.0
    for k in range(depth // chunk):
        part = pl.ds(k * chunk, chunk)
        total += lax.dot_general(
            jnp.concatenate([ref[:, part] for ref in rows], axis=0),
            jnp.concatenate([factor[:, part], factor_other[:, part]], axis=0),
            (((1,), (1,)), ((), ())),
            preferred_element_type=F32,
        )
    total = total.astype(BF16)
    wide, per, lines = message_layout(2 * half, store_count)
    out[:store_count, :width] = store_b[...]
    if width < wide:
        out[:store_count, width:] = jnp.zeros((store_count, wide - width), BF16)
    for line in range(lines):
        blocks = [
            total[n * size : (n + 1) * size] if n < half else jnp.zeros((size, 2 * store_count), BF16)
            for n in range(line * per, (line + 1) * per)
        ]
        blocks.append(meta[...] if line == 0 else jnp.zeros(meta.shape, BF16))
        start = store_count + line * size
        out[start : start + size] = jnp.concatenate(blocks, axis=1)


def make_message(rows, factor, factor_other, store_b, meta):
    size, depth = rows[0].shape
    store_count = store_b.shape[0]
    wide, _, lines = message_layout(2 * len(rows), store_count)
    inputs = [*rows, factor, factor_other, store_b, meta]
    return pl.pallas_call(
        functools.partial(message_kernel, 1024),
        in_specs=[VMEM_SPEC] * len(inputs),
        out_specs=VMEM_SPEC,
        out_shape=jax.ShapeDtypeStruct((store_count + lines * size, wide), BF16),
        compiler_params=params(8),
        cost_estimate=cost(4 * size * len(rows) * depth * store_count, 2 * depth * store_count * 2),
    )(*[in_vmem(value) for value in inputs])


def gate_up_kernel(count, chunk, *refs):
    rows, factor, weights, inner, outs = refs[:count], refs[count], refs[count + 1 : count + 5], refs[count + 5], refs[count + 6 :]
    depth = factor.shape[1]
    pieces = [pl.ds(k * chunk, chunk) for k in range(depth // chunk)]
    for weight, out in zip(weights, outs):
        total = jnp.zeros(out.shape, F32)
        for part in pieces:
            block = jnp.concatenate([ref[:, part] for ref in rows], axis=0)
            total += jnp.dot(block, weight[part], preferred_element_type=F32)
        out[...] = total
    total = jnp.zeros(inner.shape, F32)
    for part in pieces:
        block = jnp.concatenate([ref[:, part] for ref in rows], axis=0)
        total += lax.dot_general(
            block, factor[:, part], (((1,), (1,)), ((), ())), preferred_element_type=F32
        )
    inner[...] = total.astype(BF16)


def gate_up(rows, factor, weights):
    depth, width = weights[0].shape
    total = rows[0].shape[0] * len(rows)
    inputs = [*rows, factor, *weights]
    out = jax.ShapeDtypeStruct((total, width), F32)
    return pl.pallas_call(
        functools.partial(gate_up_kernel, len(rows), 1024),
        in_specs=[VMEM_SPEC] * len(inputs),
        out_specs=[VMEM_SPEC] * (1 + len(weights)),
        out_shape=[jax.ShapeDtypeStruct((total, factor.shape[0]), BF16)] + [out] * len(weights),
        compiler_params=params(12),
        cost_estimate=cost(2 * len(weights) * total * depth * width, 2 * len(weights) * depth * width),
    )(*[in_vmem(x) for x in inputs])


def silu(value):
    return value / (1.0 + jnp.exp(-value))


def down_blocks(hidden, hidden_shared, share, down, down_shared, outs, chunks, order):
    size = hidden.shape[0] // len(order)
    half = len(order) // 2
    part = outs[0].shape[-1]
    tile = tile_of(part)
    for n, chunk in enumerate(chunks):
        keep, send = outs[2 * n : 2 * n + 2]
        for place, j in enumerate(chunk):
            for c in range(part // tile):
                cut = slice(j * part + c * tile, j * part + (c + 1) * tile)
                routed = jnp.dot(hidden, down[:, cut], preferred_element_type=F32) * share
                routed += jnp.dot(hidden_shared, down_shared[:, cut], preferred_element_type=F32)
                for at, r in enumerate(order):
                    block = routed[r * size : (r + 1) * size].astype(BF16)
                    target, row = (keep, at) if at < half else (send, at - half)
                    target[row, place, :, c * tile : (c + 1) * tile] = block


def down_next_kernel(chunks, order, hidden, hidden_shared, share, down, down_shared, *outs):
    down_blocks(
        hidden[...], hidden_shared[...], share[:, :1], down, down_shared, outs, chunks, order
    )


def down_kernel(experts, chunks, order, *refs):
    count = len(order)
    half = count // 2
    inner_shared, gate, up, gate_shared, up_shared = [ref[...] for ref in refs[:5]]
    refs = refs[5:]
    columns, shared_b = refs[:2]
    messages = refs[2 : 2 + count]
    down, down_shared = refs[2 + count : 4 + count]
    hidden_out, hidden_shared_out, share_out = refs[4 + count : 7 + count]
    outs = refs[7 + count :]
    total, width = gate.shape
    size = total // count
    shared_count = shared_b.shape[0]
    store_count = columns.shape[1] // count
    wide, per, _ = message_layout(count, store_count)
    own = columns[2:3, :1]

    meta = jnp.concatenate(
        [ref[store_count : store_count + size, wide - META :] for ref in messages], axis=0
    ).astype(F32)
    lane = lax.broadcasted_iota(jnp.int32, meta.shape, 1)
    mine = (lane < 3 * experts) & (lane % experts == own)
    share = jnp.sum(jnp.where(mine, meta, 0.0), axis=1, keepdims=True)
    row_tenant = jnp.sum(jnp.where(lane == 3 * experts, meta, 0.0), axis=1, keepdims=True)
    row_tenant = row_tenant.astype(jnp.int32)

    lifted = []
    for k in range(count):
        parts = []
        for h in range(0, count, 2):
            sender = h + k % 2
            n = (k ^ sender) // 2
            rows = slice(store_count + n // per * size, store_count + (n // per + 1) * size)
            lanes = slice(n % per * 2 * store_count, (n % per + 1) * 2 * store_count)
            block = messages[sender][rows, lanes]
            if k % 2:
                block = jnp.concatenate([block[:, store_count:], block[:, :store_count]], axis=1)
            parts.append(block)
        lifted.append(jnp.concatenate(parts, axis=1))
    lifted = jnp.concatenate(lifted, axis=0)
    zero = jnp.zeros((), BF16)
    lifted = jnp.where(row_tenant == columns[1:2], lifted, zero)
    shared_tenant = columns[0:1, :shared_count]
    lifted_shared = jnp.where(row_tenant == shared_tenant, inner_shared, zero)
    factor = jnp.concatenate([ref[:store_count, :width] for ref in messages], axis=0)
    upward = up + jnp.dot(lifted, factor, preferred_element_type=F32)
    hidden = (silu(gate) * upward).astype(BF16)
    upward = up_shared + jnp.dot(lifted_shared, shared_b[...], preferred_element_type=F32)
    here = (row_tenant >= shared_tenant[:, :1]) & (row_tenant <= shared_tenant[:, shared_count - 1 :])
    hidden_shared = jnp.where(here, silu(gate_shared) * upward, 0.0).astype(BF16)

    hidden_out[...] = hidden
    hidden_shared_out[...] = hidden_shared
    share_out[...] = jnp.broadcast_to(share, share_out.shape)
    down_blocks(hidden, hidden_shared, share, down, down_shared, outs, chunks, order)


def down_outs(rows, depth, chunks, order):
    size = rows // len(order)
    part = depth // lax.axis_size("tensor")
    outs = []
    for chunk in chunks:
        outs += [jax.ShapeDtypeStruct((len(order) // 2, len(chunk), size, part), BF16)] * 2
    return outs


def down_cost(rows, down, chunks):
    part = sum(len(chunk) for chunk in chunks) * down.size // lax.axis_size("tensor")
    return cost(4 * rows * part, 0)


def down_products(gated, columns, shared_b, messages, down, down_shared, experts, chunks, order):
    rows, width = gated[1].shape
    whole = [*gated, columns, shared_b, *messages, down, down_shared]
    outs = [jax.ShapeDtypeStruct((rows, width), BF16)] * 2
    outs += [jax.ShapeDtypeStruct((rows, 128), F32)]
    outs += down_outs(rows, down.shape[1], chunks, order)
    return pl.pallas_call(
        functools.partial(down_kernel, experts, chunks, order),
        in_specs=[VMEM_SPEC] * len(whole),
        out_specs=[VMEM_SPEC] * len(outs),
        out_shape=outs,
        compiler_params=params(16),
        cost_estimate=down_cost(rows, down, chunks),
    )(*[in_vmem(x) for x in whole])


def down_next(hidden, down, down_shared, chunks, order):
    rows = hidden[0].shape[0]
    whole = [*hidden, down, down_shared]
    outs = down_outs(rows, down.shape[1], chunks, order)
    return pl.pallas_call(
        functools.partial(down_next_kernel, chunks, order),
        in_specs=[VMEM_SPEC] * len(whole),
        out_specs=[VMEM_SPEC] * len(outs),
        out_shape=outs,
        compiler_params=params(16),
        cost_estimate=down_cost(rows, down, chunks),
    )(*[in_vmem(x) for x in whole])


def local(
    tokens,
    expert_ids,
    gate_values,
    tenant_ids,
    w_gate,
    w_up,
    routed_down_weight,
    shared_gate,
    shared_up,
    shared_down,
    store_a,
    store_b,
    pair_slot,
    shared_a,
    shared_b,
):
    experts = pair_slot.shape[0]
    adapted, rank, model_width = store_a.shape
    hid = store_b.shape[2]
    steps, size, _ = expert_ids.shape
    count = lax.axis_size("expert")
    n_tensor = lax.axis_size("tensor")
    shared_count, store_count = shared_a.shape[0] * rank, adapted * rank

    rows_own = tokens.reshape(steps * size, model_width)
    arrived = swap(rows_own, count // 2)
    store_other = swap(store_a, 1).reshape(store_count, model_width)
    first = first_call(
        experts,
        jnp.swapaxes(expert_ids, 1, 2),
        jnp.swapaxes(gate_values, 1, 2),
        tenant_ids.reshape(1, size),
        pair_slot,
        [
            rows_own,
            store_b.reshape(store_count, hid),
            shared_b.reshape(shared_count, hid),
            store_a.reshape(store_count, model_width),
            shared_a.reshape(shared_count, model_width),
            w_gate[0],
            w_up[0],
            shared_gate,
            shared_up,
            routed_down_weight[0],
            shared_down,
        ],
    )
    meta, columns, rows_held, store_b_held, shared_b_held, factor_store, factor_shared = first[:7]
    weights, down, down_own = first[7:11], first[11], first[12]
    arrived, rows_held, store_other = lax.optimization_barrier((arrived, rows_held, store_other))
    came = far_rows(arrived, rows_own)
    message = make_message([rows_held, *came], factor_store, store_other, store_b_held, meta)
    messages = [message] + [swap(message, r) for r in range(1, count)]
    came, message = lax.optimization_barrier((came, message))
    rows = [rows_held, swap(rows_own, 1)]
    for value in came:
        rows += [value, swap(value, 1)]
    gated = gate_up(rows, factor_shared, weights)

    order = [0]
    bit = count // 2
    while bit >= 1:
        order = order + [r | bit for r in order]
        bit //= 2
    chunks = [[j] for j in range(n_tensor - 1, 1, -1)] + [[1, 0]]
    hidden = down_products(
        gated, columns, shared_b_held, messages, down, down_own, experts, chunks[:-1], order
    )
    hidden, held, leaving = hidden[:3], list(hidden[3::2]), list(hidden[4::2])
    bit = 1
    while bit < count:
        half = count // (2 * bit) // 2
        if bit > 1:
            leaving[1], *_ = lax.optimization_barrier((leaving[1], leaving[0]))
        arrived = [swap(value, bit) for value in leaving]
        if bit == 1:
            ready = add(held[0][half:], arrived[0][half:])
            hidden, ready = lax.optimization_barrier((hidden, ready))
            rest = down_next(hidden, down, down_own, chunks[len(held) :], order)
            held += rest[0::2]
            arrived += [swap(value, bit) for value in rest[1::2]]
        if 2 * bit < count:
            leaving = [add(h[half:], a[half:]) for h, a in zip(held, arrived)]
            held = [add(h[:half], a[:half]) for h, a in zip(held, arrived)]
        bit *= 2
    parts = {}
    for n, chunk in enumerate(chunks):
        for place, j in enumerate(chunk):
            parts[j] = [held[n][0, place], arrived[n][0, place]]
    bit = 1
    while bit < n_tensor:
        for j in sorted([j for j in parts if j & bit], reverse=True):
            parts[j ^ bit].append(swap(total_of(parts.pop(j)), bit, "tensor"))
        bit *= 2
    return total_of(parts[0]).reshape(steps, size, model_width // n_tensor)


def solution(mesh):
    return jax.shard_map(
        local,
        mesh=mesh,
        in_specs=(
            P(None, ("groups", "expert"), None),
            P(None, ("groups", "expert"), None),
            P(None, ("groups", "expert"), None),
            P(("groups", "expert")),
            P("expert", None, "tensor"),
            P("expert", None, "tensor"),
            P("expert", "tensor", None),
            P(None, "tensor"),
            P(None, "tensor"),
            P("tensor", None),
            P("expert", None, None),
            P("expert", None, "tensor"),
            P(),
            P("expert", None, None),
            P("expert", None, "tensor"),
        ),
        out_specs=P(None, ("groups", "expert"), "tensor"),
        check_vma=False,
    )
```

```python
import functools

import jax
import jax.numpy as jnp
from jax import lax
from jax.experimental import pallas as pl
from jax.experimental.pallas import tpu as pltpu
from jax.sharding import PartitionSpec as P

F32 = jnp.float32
BF16 = jnp.bfloat16
MIB = 1024 * 1024


def params(mebibytes):
    return pltpu.CompilerParams(vmem_limit_bytes=mebibytes * MIB)


def cost(flops, moved):
    return pl.CostEstimate(flops=int(flops), bytes_accessed=int(moved), transcendentals=0)


def in_vmem(value):
    return pltpu.with_memory_space_constraint(value, pltpu.VMEM)


def in_hbm(value):
    return pltpu.with_memory_space_constraint(value, pltpu.HBM)


def vmem_shape(value):
    return pltpu.VMEM(value.shape, value.dtype)


VMEM_SPEC = pl.BlockSpec(memory_space=pltpu.VMEM)
HBM_SPEC = pl.BlockSpec(memory_space=pltpu.HBM)


def swap(value, bits, axis="expert"):
    count = lax.axis_size(axis)
    return lax.ppermute(value, axis, [(i, i ^ bits) for i in range(count)])


def add(one, other):
    return (one.astype(F32) + other.astype(F32)).astype(BF16)


def total_of(values):
    return sum(value.astype(F32) for value in values).astype(BF16)


def far_rows(arrived, rows_own):
    count = lax.axis_size("expert")
    bit = count // 2
    pieces = {0: rows_own, bit: arrived}
    bit //= 2
    while bit > 1:
        pieces.update({r ^ bit: swap(piece, bit) for r, piece in list(pieces.items())})
        bit //= 2
    return [pieces[r] for r in range(2, count, 2)]


def tile_of(width):
    return 256 if width % 256 == 0 else 128


def column_of(row, size):
    lane = lax.broadcasted_iota(jnp.int32, (size, row.shape[1]), 1)
    place = lax.broadcasted_iota(jnp.int32, (size, row.shape[1]), 0)
    return jnp.sum(jnp.where(lane == place, row.astype(F32), 0.0), axis=1, keepdims=True)


def first_kernel(
    experts, ids, values, tenants, pair_slot, rows, store_b, shared_b, factor_store, factor_shared,
    gate_weight, up_weight, gate_shared, up_shared, down, down_shared, meta, columns, *refs
):
    targets, (ids_held, values_held, tenants_held, pair_slot_held, small_sems, sems) = refs[:-6], refs[-6:]
    own, own_part = lax.axis_index("expert"), lax.axis_index("tensor")
    parts = lax.axis_size("tensor")
    small = [
        (ids, ids_held), (values, values_held), (tenants, tenants_held), (pair_slot, pair_slot_held)
    ]
    small = [
        pltpu.make_async_copy(source, target, small_sems.at[n])
        for n, (source, target) in enumerate(small)
    ]
    sources = [
        rows, store_b, shared_b, factor_store, factor_shared, gate_weight, up_weight, gate_shared,
        up_shared, down, down_shared,
    ]
    staged = list(zip(sources[:5], targets[:5]))
    piece = gate_weight.shape[0] // parts
    for source, target in zip(sources[5:9], targets[5:9]):
        for k in range(parts):
            part = pl.ds(k * piece, piece)
            staged.append((source.at[part], target.at[part]))
    for source, target in zip(sources[9:], targets[9:]):
        for j in range(parts):
            start = pl.multiple_of((own_part ^ j) * piece, piece)
            staged.append((source.at[:, pl.ds(start, piece)], target.at[:, pl.ds(j * piece, piece)]))
    staged = [
        pltpu.make_async_copy(source, target, sems.at[n])
        for n, (source, target) in enumerate(staged)
    ]
    for copy in (*small, *staged):
        copy.start()
    for copy in small:
        copy.wait()

    steps, top, size = ids_held.shape
    tenant = column_of(tenants_held[...], size)
    lane = lax.broadcasted_iota(jnp.int32, (size, meta.shape[1]), 1)
    for s in range(steps):
        weight = jnp.zeros(lane.shape, F32)
        for k in range(top):
            expert = column_of(ids_held[s, k : k + 1], size).astype(jnp.int32)
            value = column_of(values_held[s, k : k + 1], size)
            weight = weight + jnp.where(expert == lane % experts, value, 0.0)
        high = weight.astype(BF16).astype(F32)
        middle = (weight - high).astype(BF16).astype(F32)
        low = weight - high - middle
        found = jnp.where(lane < experts, high, jnp.where(lane < 2 * experts, middle, low))
        found = jnp.where(lane < 3 * experts, found, tenant)
        meta[s * size : (s + 1) * size] = found.astype(BF16)

    tenant_count = pair_slot_held.shape[1]
    place = lax.broadcasted_iota(jnp.int32, pair_slot_held.shape, 0)
    own_row = jnp.sum(
        jnp.where(place == own, pair_slot_held[...].astype(F32), 0.0), axis=0, keepdims=True
    )
    own_slots = column_of(own_row, tenant_count).astype(jnp.int32)
    total = columns.shape[1]
    per_device = tenant_count // lax.axis_size("expert")
    shared_count, store_count = shared_b.shape[0], store_b.shape[0]
    rank = shared_count // per_device
    column = lax.broadcasted_iota(jnp.int32, (1, total), 1)
    shared_tenant = own * per_device + column % shared_count // rank
    slot = (own ^ (column // store_count)) * (store_count // rank) + column % store_count // rank
    tenant_number = lax.broadcasted_iota(jnp.int32, (tenant_count, total), 0)
    slot_tenant = jnp.max(jnp.where(own_slots == slot, tenant_number, -1), axis=0, keepdims=True)
    columns[0:1] = shared_tenant
    columns[1:2] = slot_tenant
    columns[2:3] = jnp.full((1, total), own, jnp.int32)
    columns[3:8] = jnp.zeros((5, total), jnp.int32)
    for copy in staged:
        copy.wait()


def first_call(experts, ids, values, tenants, pair_slot, staged):
    parts = lax.axis_size("tensor")
    steps, _, size = ids.shape
    columns = max(lax.axis_size("expert") * staged[1].shape[0], staged[2].shape[0])
    outs = [
        jax.ShapeDtypeStruct((steps * size, META), BF16),
        jax.ShapeDtypeStruct((8, columns), jnp.int32),
        *[vmem_shape(value) for value in staged],
    ]
    inputs = [ids, values, tenants, pair_slot, *staged]
    return pl.pallas_call(
        functools.partial(first_kernel, experts),
        in_specs=[HBM_SPEC] * len(inputs),
        out_specs=[VMEM_SPEC] * len(outs),
        out_shape=outs,
        scratch_shapes=[
            pltpu.VMEM(ids.shape, jnp.int32),
            pltpu.VMEM(values.shape, F32),
            pltpu.VMEM(tenants.shape, jnp.int32),
            pltpu.VMEM(pair_slot.shape, jnp.int32),
            pltpu.SemaphoreType.DMA((4,)),
            pltpu.SemaphoreType.DMA((5 + 6 * parts,)),
        ],
        compiler_params=params(4),
        cost_estimate=cost(0, 2 * sum(value.size for value in staged)),
    )(*[in_hbm(value) for value in inputs])


META = 128


def message_layout(count, store_count):
    wide = max(128, 2 * store_count)
    per = wide // (2 * store_count)
    return wide + META, per, -(-(count // 2) // per)


def message_kernel(chunk, *refs):
    half = len(refs) - 5
    rows, (factor, factor_other, store_b, meta, out) = refs[:half], refs[half:]
    size, depth = rows[0].shape
    store_count, width = store_b.shape
    total = 0.0
    for k in range(depth // chunk):
        part = pl.ds(k * chunk, chunk)
        total += lax.dot_general(
            jnp.concatenate([ref[:, part] for ref in rows], axis=0),
            jnp.concatenate([factor[:, part], factor_other[:, part]], axis=0),
            (((1,), (1,)), ((), ())),
            preferred_element_type=F32,
        )
    total = total.astype(BF16)
    wide, per, lines = message_layout(2 * half, store_count)
    out[:store_count, :width] = store_b[...]
    if width < wide:
        out[:store_count, width:] = jnp.zeros((store_count, wide - width), BF16)
    for line in range(lines):
        blocks = [
            total[n * size : (n + 1) * size] if n < half else jnp.zeros((size, 2 * store_count), BF16)
            for n in range(line * per, (line + 1) * per)
        ]
        blocks.append(meta[...] if line == 0 else jnp.zeros(meta.shape, BF16))
        start = store_count + line * size
        out[start : start + size] = jnp.concatenate(blocks, axis=1)


def make_message(rows, factor, factor_other, store_b, meta):
    size, depth = rows[0].shape
    store_count = store_b.shape[0]
    wide, _, lines = message_layout(2 * len(rows), store_count)
    inputs = [*rows, factor, factor_other, store_b, meta]
    return pl.pallas_call(
        functools.partial(message_kernel, 1024),
        in_specs=[VMEM_SPEC] * len(inputs),
        out_specs=VMEM_SPEC,
        out_shape=jax.ShapeDtypeStruct((store_count + lines * size, wide), BF16),
        compiler_params=params(8),
        cost_estimate=cost(4 * size * len(rows) * depth * store_count, 2 * depth * store_count * 2),
    )(*[in_vmem(value) for value in inputs])


def gate_up_kernel(count, chunk, *refs):
    rows, factor, weights, inner, outs = refs[:count], refs[count], refs[count + 1 : count + 5], refs[count + 5], refs[count + 6 :]
    depth = factor.shape[1]
    pieces = [pl.ds(k * chunk, chunk) for k in range(depth // chunk)]
    for weight, out in zip(weights, outs):
        total = jnp.zeros(out.shape, F32)
        for part in pieces:
            block = jnp.concatenate([ref[:, part] for ref in rows], axis=0)
            total += jnp.dot(block, weight[part], preferred_element_type=F32)
        out[...] = total
    total = jnp.zeros(inner.shape, F32)
    for part in pieces:
        block = jnp.concatenate([ref[:, part] for ref in rows], axis=0)
        total += lax.dot_general(
            block, factor[:, part], (((1,), (1,)), ((), ())), preferred_element_type=F32
        )
    inner[...] = total.astype(BF16)


def gate_up(rows, factor, weights):
    depth, width = weights[0].shape
    total = rows[0].shape[0] * len(rows)
    inputs = [*rows, factor, *weights]
    out = jax.ShapeDtypeStruct((total, width), F32)
    return pl.pallas_call(
        functools.partial(gate_up_kernel, len(rows), 1024),
        in_specs=[VMEM_SPEC] * len(inputs),
        out_specs=[VMEM_SPEC] * (1 + len(weights)),
        out_shape=[jax.ShapeDtypeStruct((total, factor.shape[0]), BF16)] + [out] * len(weights),
        compiler_params=params(12),
        cost_estimate=cost(2 * len(weights) * total * depth * width, 2 * len(weights) * depth * width),
    )(*[in_vmem(x) for x in inputs])


def silu(value):
    return value / (1.0 + jnp.exp(-value))


def down_blocks(hidden, hidden_shared, share, down, down_shared, outs, chunks, order):
    size = hidden.shape[0] // len(order)
    half = len(order) // 2
    part = outs[0].shape[-1]
    tile = tile_of(part)
    for n, chunk in enumerate(chunks):
        keep, send = outs[2 * n : 2 * n + 2]
        for place, j in enumerate(chunk):
            for c in range(part // tile):
                cut = slice(j * part + c * tile, j * part + (c + 1) * tile)
                routed = jnp.dot(hidden, down[:, cut], preferred_element_type=F32) * share
                routed += jnp.dot(hidden_shared, down_shared[:, cut], preferred_element_type=F32)
                for at, r in enumerate(order):
                    block = routed[r * size : (r + 1) * size].astype(BF16)
                    target, row = (keep, at) if at < half else (send, at - half)
                    target[row, place, :, c * tile : (c + 1) * tile] = block


def down_next_kernel(chunks, order, hidden, hidden_shared, share, down, down_shared, *outs):
    down_blocks(
        hidden[...], hidden_shared[...], share[:, :1], down, down_shared, outs, chunks, order
    )


def down_kernel(experts, chunks, order, *refs):
    count = len(order)
    half = count // 2
    inner_shared, gate, up, gate_shared, up_shared = [ref[...] for ref in refs[:5]]
    refs = refs[5:]
    columns, shared_b = refs[:2]
    messages = refs[2 : 2 + count]
    down, down_shared = refs[2 + count : 4 + count]
    hidden_out, hidden_shared_out, share_out = refs[4 + count : 7 + count]
    outs = refs[7 + count :]
    total, width = gate.shape
    size = total // count
    shared_count = shared_b.shape[0]
    store_count = columns.shape[1] // count
    wide, per, _ = message_layout(count, store_count)
    own = columns[2:3, :1]

    meta = jnp.concatenate(
        [ref[store_count : store_count + size, wide - META :] for ref in messages], axis=0
    ).astype(F32)
    lane = lax.broadcasted_iota(jnp.int32, meta.shape, 1)
    mine = (lane < 3 * experts) & (lane % experts == own)
    share = jnp.sum(jnp.where(mine, meta, 0.0), axis=1, keepdims=True)
    row_tenant = jnp.sum(jnp.where(lane == 3 * experts, meta, 0.0), axis=1, keepdims=True)
    row_tenant = row_tenant.astype(jnp.int32)

    lifted = []
    for k in range(count):
        parts = []
        for h in range(0, count, 2):
            sender = h + k % 2
            n = (k ^ sender) // 2
            rows = slice(store_count + n // per * size, store_count + (n // per + 1) * size)
            lanes = slice(n % per * 2 * store_count, (n % per + 1) * 2 * store_count)
            block = messages[sender][rows, lanes]
            if k % 2:
                block = jnp.concatenate([block[:, store_count:], block[:, :store_count]], axis=1)
            parts.append(block)
        lifted.append(jnp.concatenate(parts, axis=1))
    lifted = jnp.concatenate(lifted, axis=0)
    zero = jnp.zeros((), BF16)
    lifted = jnp.where(row_tenant == columns[1:2], lifted, zero)
    shared_tenant = columns[0:1, :shared_count]
    lifted_shared = jnp.where(row_tenant == shared_tenant, inner_shared, zero)
    factor = jnp.concatenate([ref[:store_count, :width] for ref in messages], axis=0)
    upward = up + jnp.dot(lifted, factor, preferred_element_type=F32)
    hidden = (silu(gate) * upward).astype(BF16)
    upward = up_shared + jnp.dot(lifted_shared, shared_b[...], preferred_element_type=F32)
    here = (row_tenant >= shared_tenant[:, :1]) & (row_tenant <= shared_tenant[:, shared_count - 1 :])
    hidden_shared = jnp.where(here, silu(gate_shared) * upward, 0.0).astype(BF16)

    hidden_out[...] = hidden
    hidden_shared_out[...] = hidden_shared
    share_out[...] = jnp.broadcast_to(share, share_out.shape)
    down_blocks(hidden, hidden_shared, share, down, down_shared, outs, chunks, order)


def down_outs(rows, depth, chunks, order):
    size = rows // len(order)
    part = depth // lax.axis_size("tensor")
    outs = []
    for chunk in chunks:
        outs += [jax.ShapeDtypeStruct((len(order) // 2, len(chunk), size, part), BF16)] * 2
    return outs


def down_cost(rows, down, chunks):
    part = sum(len(chunk) for chunk in chunks) * down.size // lax.axis_size("tensor")
    return cost(4 * rows * part, 0)


def down_products(gated, columns, shared_b, messages, down, down_shared, experts, chunks, order):
    rows, width = gated[1].shape
    whole = [*gated, columns, shared_b, *messages, down, down_shared]
    outs = [jax.ShapeDtypeStruct((rows, width), BF16)] * 2
    outs += [jax.ShapeDtypeStruct((rows, 128), F32)]
    outs += down_outs(rows, down.shape[1], chunks, order)
    return pl.pallas_call(
        functools.partial(down_kernel, experts, chunks, order),
        in_specs=[VMEM_SPEC] * len(whole),
        out_specs=[VMEM_SPEC] * len(outs),
        out_shape=outs,
        compiler_params=params(16),
        cost_estimate=down_cost(rows, down, chunks),
    )(*[in_vmem(x) for x in whole])


def down_next(hidden, down, down_shared, chunks, order):
    rows = hidden[0].shape[0]
    whole = [*hidden, down, down_shared]
    outs = down_outs(rows, down.shape[1], chunks, order)
    return pl.pallas_call(
        functools.partial(down_next_kernel, chunks, order),
        in_specs=[VMEM_SPEC] * len(whole),
        out_specs=[VMEM_SPEC] * len(outs),
        out_shape=outs,
        compiler_params=params(16),
        cost_estimate=down_cost(rows, down, chunks),
    )(*[in_vmem(x) for x in whole])


def local(
    tokens,
    expert_ids,
    gate_values,
    tenant_ids,
    w_gate,
    w_up,
    routed_down_weight,
    shared_gate,
    shared_up,
    shared_down,
    store_a,
    store_b,
    pair_slot,
    shared_a,
    shared_b,
):
    experts = pair_slot.shape[0]
    adapted, rank, model_width = store_a.shape
    hid = store_b.shape[2]
    steps, size, _ = expert_ids.shape
    count = lax.axis_size("expert")
    n_tensor = lax.axis_size("tensor")
    shared_count, store_count = shared_a.shape[0] * rank, adapted * rank

    rows_own = tokens.reshape(steps * size, model_width)
    arrived = swap(rows_own, count // 2)
    store_other = swap(store_a, 1).reshape(store_count, model_width)
    first = first_call(
        experts,
        jnp.swapaxes(expert_ids, 1, 2),
        jnp.swapaxes(gate_values, 1, 2),
        tenant_ids.reshape(1, size),
        pair_slot,
        [
            rows_own,
            store_b.reshape(store_count, hid),
            shared_b.reshape(shared_count, hid),
            store_a.reshape(store_count, model_width),
            shared_a.reshape(shared_count, model_width),
            w_gate[0],
            w_up[0],
            shared_gate,
            shared_up,
            routed_down_weight[0],
            shared_down,
        ],
    )
    meta, columns, rows_held, store_b_held, shared_b_held, factor_store, factor_shared = first[:7]
    weights, down, down_own = first[7:11], first[11], first[12]
    arrived, rows_held, store_other = lax.optimization_barrier((arrived, rows_held, store_other))
    came = far_rows(arrived, rows_own)
    message = make_message([rows_held, *came], factor_store, store_other, store_b_held, meta)
    messages = {r: swap(message, r) for r in [*range(2, count), 1]}
    messages = [message] + [messages[r] for r in range(1, count)]
    came, message = lax.optimization_barrier((came, message))
    rows = [rows_held, swap(rows_own, 1)]
    for value in came:
        rows += [value, swap(value, 1)]
    gated = gate_up(rows, factor_shared, weights)

    order = [0]
    bit = count // 2
    while bit >= 1:
        order = order + [r | bit for r in order]
        bit //= 2
    chunks = [[j] for j in range(n_tensor - 1, -1, -1)]
    hidden = down_products(
        gated, columns, shared_b_held, messages, down, down_own, experts, chunks[:-2], order
    )
    hidden, held, leaving = hidden[:3], list(hidden[3::2]), list(hidden[4::2])
    bit = 1
    while bit < count:
        half = count // (2 * bit) // 2
        if bit > 1:
            for n in range(1, len(leaving)):
                leaving[n], *_ = lax.optimization_barrier((leaving[n], leaving[n - 1]))
        arrived = [swap(value, bit) for value in leaving]
        if bit == 1:
            ready = add(held[0][half:], arrived[0][half:])
            hidden, ready = lax.optimization_barrier((hidden, ready))
            rest = down_next(hidden, down, down_own, chunks[len(held) :], order)
            held += rest[0::2]
            arrived += [swap(value, bit) for value in rest[1::2]]
        if 2 * bit < count:
            leaving = [add(h[half:], a[half:]) for h, a in zip(held, arrived)]
            held = [add(h[:half], a[:half]) for h, a in zip(held, arrived)]
        bit *= 2
    parts = {}
    for n, chunk in enumerate(chunks):
        for place, j in enumerate(chunk):
            parts[j] = [held[n][0, place], arrived[n][0, place]]
    bit = 1
    while bit < n_tensor:
        for j in sorted([j for j in parts if j & bit], reverse=True):
            parts[j ^ bit].append(swap(total_of(parts.pop(j)), bit, "tensor"))
        bit *= 2
    return total_of(parts[0]).reshape(steps, size, model_width // n_tensor)


def solution(mesh):
    return jax.shard_map(
        local,
        mesh=mesh,
        in_specs=(
            P(None, ("groups", "expert"), None),
            P(None, ("groups", "expert"), None),
            P(None, ("groups", "expert"), None),
            P(("groups", "expert")),
            P("expert", None, "tensor"),
            P("expert", None, "tensor"),
            P("expert", "tensor", None),
            P(None, "tensor"),
            P(None, "tensor"),
            P("tensor", None),
            P("expert", None, None),
            P("expert", None, "tensor"),
            P(),
            P("expert", None, None),
            P("expert", None, "tensor"),
        ),
        out_specs=P(None, ("groups", "expert"), "tensor"),
        check_vma=False,
    )
```

```python
import functools

import jax
import jax.numpy as jnp
from jax import lax
from jax.experimental import pallas as pl
from jax.experimental.pallas import tpu as pltpu
from jax.sharding import PartitionSpec as P

F32 = jnp.float32
BF16 = jnp.bfloat16
MIB = 1024 * 1024


def params(mebibytes):
    return pltpu.CompilerParams(vmem_limit_bytes=mebibytes * MIB)


def cost(flops, moved):
    return pl.CostEstimate(flops=int(flops), bytes_accessed=int(moved), transcendentals=0)


def in_vmem(value):
    return pltpu.with_memory_space_constraint(value, pltpu.VMEM)


def in_hbm(value):
    return pltpu.with_memory_space_constraint(value, pltpu.HBM)


def vmem_shape(value):
    return pltpu.VMEM(value.shape, value.dtype)


VMEM_SPEC = pl.BlockSpec(memory_space=pltpu.VMEM)
HBM_SPEC = pl.BlockSpec(memory_space=pltpu.HBM)


def swap(value, bits, axis="expert"):
    count = lax.axis_size(axis)
    return lax.ppermute(value, axis, [(i, i ^ bits) for i in range(count)])


def add(one, other):
    return (one.astype(F32) + other.astype(F32)).astype(BF16)


def total_of(values):
    return sum(value.astype(F32) for value in values).astype(BF16)


def far_rows(arrived, rows_own):
    count = lax.axis_size("expert")
    bit = count // 2
    pieces = {0: rows_own, bit: arrived}
    bit //= 2
    while bit > 1:
        pieces.update({r ^ bit: swap(piece, bit) for r, piece in list(pieces.items())})
        bit //= 2
    return [pieces[r] for r in range(2, count, 2)]


def tile_of(width):
    return 256 if width % 256 == 0 else 128


def column_of(row, size):
    lane = lax.broadcasted_iota(jnp.int32, (size, row.shape[1]), 1)
    place = lax.broadcasted_iota(jnp.int32, (size, row.shape[1]), 0)
    return jnp.sum(jnp.where(lane == place, row.astype(F32), 0.0), axis=1, keepdims=True)


def first_kernel(
    experts, ids, values, tenants, pair_slot, rows, store_b, shared_b, factor_store, factor_shared,
    gate_weight, up_weight, gate_shared, up_shared, down, down_shared, pack, columns, *refs
):
    targets, (ids_held, values_held, tenants_held, pair_slot_held, small_sems, sems) = refs[:-6], refs[-6:]
    own, own_part = lax.axis_index("expert"), lax.axis_index("tensor")
    parts = lax.axis_size("tensor")
    small = [
        (ids, ids_held), (values, values_held), (tenants, tenants_held), (pair_slot, pair_slot_held)
    ]
    small = [
        pltpu.make_async_copy(source, target, small_sems.at[n])
        for n, (source, target) in enumerate(small)
    ]
    sources = [
        rows, store_b, shared_b, factor_store, factor_shared, gate_weight, up_weight, gate_shared,
        up_shared, down, down_shared,
    ]
    shared_count, (store_count, width) = shared_b.shape[0], store_b.shape
    staged = list(zip(sources[:5], (targets[0], pack.at[pl.ds(0, store_count), pl.ds(0, width)], *targets[1:4])))
    targets = (None, *targets)
    piece = gate_weight.shape[0] // parts
    for source, target in zip(sources[5:9], targets[5:9]):
        for k in range(parts):
            part = pl.ds(k * piece, piece)
            staged.append((source.at[part], target.at[part]))
    for source, target in zip(sources[9:], targets[9:]):
        for j in range(parts):
            start = pl.multiple_of((own_part ^ j) * piece, piece)
            staged.append((source.at[:, pl.ds(start, piece)], target.at[:, pl.ds(j * piece, piece)]))
    staged = [
        pltpu.make_async_copy(source, target, sems.at[n])
        for n, (source, target) in enumerate(staged)
    ]
    for copy in (*small, *staged):
        copy.start()
    for copy in small:
        copy.wait()

    steps, top, size = ids_held.shape
    tenant = column_of(tenants_held[...], size)
    lane = lax.broadcasted_iota(jnp.int32, (size, META), 1)
    for s in range(steps):
        weight = jnp.zeros(lane.shape, F32)
        for k in range(top):
            expert = column_of(ids_held[s, k : k + 1], size).astype(jnp.int32)
            value = column_of(values_held[s, k : k + 1], size)
            weight = weight + jnp.where(expert == lane % experts, value, 0.0)
        high = weight.astype(BF16).astype(F32)
        middle = (weight - high).astype(BF16).astype(F32)
        low = weight - high - middle
        found = jnp.where(lane < experts, high, jnp.where(lane < 2 * experts, middle, low))
        found = jnp.where(lane < 3 * experts, found, tenant)
        start = store_count + s * size
        pack[start : start + size, :META] = found.astype(BF16)
        if pack.shape[1] > META:
            pack[start : start + size, META:] = jnp.zeros((size, pack.shape[1] - META), BF16)

    tenant_count = pair_slot_held.shape[1]
    place = lax.broadcasted_iota(jnp.int32, pair_slot_held.shape, 0)
    own_row = jnp.sum(
        jnp.where(place == own, pair_slot_held[...].astype(F32), 0.0), axis=0, keepdims=True
    )
    own_slots = column_of(own_row, tenant_count).astype(jnp.int32)
    total = columns.shape[1]
    per_device = tenant_count // lax.axis_size("expert")
    rank = shared_count // per_device
    column = lax.broadcasted_iota(jnp.int32, (1, total), 1)
    shared_tenant = own * per_device + column % shared_count // rank
    slot = (own ^ (column // store_count)) * (store_count // rank) + column % store_count // rank
    tenant_number = lax.broadcasted_iota(jnp.int32, (tenant_count, total), 0)
    slot_tenant = jnp.max(jnp.where(own_slots == slot, tenant_number, -1), axis=0, keepdims=True)
    columns[0:1] = shared_tenant
    columns[1:2] = slot_tenant
    columns[2:3] = jnp.full((1, total), own, jnp.int32)
    columns[3:8] = jnp.zeros((5, total), jnp.int32)
    for copy in staged:
        copy.wait()


def first_call(experts, ids, values, tenants, pair_slot, staged):
    parts = lax.axis_size("tensor")
    steps, _, size = ids.shape
    columns = max(lax.axis_size("expert") * staged[1].shape[0], staged[2].shape[0])
    outs = [
        jax.ShapeDtypeStruct((staged[1].shape[0] + steps * size, max(META, staged[1].shape[1])), BF16),
        jax.ShapeDtypeStruct((8, columns), jnp.int32),
        *[vmem_shape(value) for n, value in enumerate(staged) if n != 1],
    ]
    inputs = [ids, values, tenants, pair_slot, *staged]
    return pl.pallas_call(
        functools.partial(first_kernel, experts),
        in_specs=[HBM_SPEC] * len(inputs),
        out_specs=[VMEM_SPEC] * len(outs),
        out_shape=outs,
        scratch_shapes=[
            pltpu.VMEM(ids.shape, jnp.int32),
            pltpu.VMEM(values.shape, F32),
            pltpu.VMEM(tenants.shape, jnp.int32),
            pltpu.VMEM(pair_slot.shape, jnp.int32),
            pltpu.SemaphoreType.DMA((4,)),
            pltpu.SemaphoreType.DMA((5 + 6 * parts,)),
        ],
        compiler_params=params(4),
        cost_estimate=cost(0, 2 * sum(value.size for value in staged)),
    )(*[in_hbm(value) for value in inputs])


META = 128


def message_layout(count, store_count):
    wide = max(128, 2 * store_count)
    per = wide // (2 * store_count)
    return wide + META, per, -(-(count // 2) // per)


def message_kernel(chunk, *refs):
    half = len(refs) - 4
    rows, (factor, factor_other, pack, out) = refs[:half], refs[half:]
    size, depth = rows[0].shape
    store_count, width = factor.shape[0], pack.shape[1]
    meta = pack[store_count:, :META]
    total = 0.0
    for k in range(depth // chunk):
        part = pl.ds(k * chunk, chunk)
        total += lax.dot_general(
            jnp.concatenate([ref[:, part] for ref in rows], axis=0),
            jnp.concatenate([factor[:, part], factor_other[:, part]], axis=0),
            (((1,), (1,)), ((), ())),
            preferred_element_type=F32,
        )
    total = total.astype(BF16)
    wide, per, lines = message_layout(2 * half, store_count)
    out[:store_count, :width] = pack[:store_count]
    if width < wide:
        out[:store_count, width:] = jnp.zeros((store_count, wide - width), BF16)
    for line in range(lines):
        blocks = [
            total[n * size : (n + 1) * size] if n < half else jnp.zeros((size, 2 * store_count), BF16)
            for n in range(line * per, (line + 1) * per)
        ]
        blocks.append(meta if line == 0 else jnp.zeros(meta.shape, BF16))
        start = store_count + line * size
        out[start : start + size] = jnp.concatenate(blocks, axis=1)


def make_message(rows, factor, factor_other, pack):
    size, depth = rows[0].shape
    store_count = factor.shape[0]
    wide, _, lines = message_layout(2 * len(rows), store_count)
    inputs = [*rows, factor, factor_other, pack]
    return pl.pallas_call(
        functools.partial(message_kernel, 1024),
        in_specs=[VMEM_SPEC] * len(inputs),
        out_specs=VMEM_SPEC,
        out_shape=jax.ShapeDtypeStruct((store_count + lines * size, wide), BF16),
        compiler_params=params(8),
        cost_estimate=cost(4 * size * len(rows) * depth * store_count, 2 * depth * store_count * 2),
    )(*[in_vmem(value) for value in inputs])


def gate_up_kernel(count, chunk, *refs):
    rows, factors, weights = refs[:count], refs[count : count + 3], refs[count + 3 : count + 7]
    inner, outs = refs[count + 7], refs[count + 8 :]
    depth = rows[0].shape[1]
    pieces = [pl.ds(k * chunk, chunk) for k in range(depth // chunk)]
    for weight, out in zip(weights, outs):
        total = jnp.zeros(out.shape, F32)
        for part in pieces:
            block = jnp.concatenate([ref[:, part] for ref in rows], axis=0)
            total += jnp.dot(block, weight[part], preferred_element_type=F32)
        out[...] = total
    total = jnp.zeros(inner.shape, F32)
    for part in pieces:
        block = jnp.concatenate([ref[:, part] for ref in rows], axis=0)
        factor = jnp.concatenate([ref[:, part] for ref in factors], axis=0)
        total += lax.dot_general(
            block, factor, (((1,), (1,)), ((), ())), preferred_element_type=F32
        )
    inner[...] = total.astype(BF16)


def gate_up(rows, factors, weights):
    depth, width = weights[0].shape
    total = rows[0].shape[0] * len(rows)
    columns = sum(factor.shape[0] for factor in factors)
    inputs = [*rows, *factors, *weights]
    out = jax.ShapeDtypeStruct((total, width), F32)
    return pl.pallas_call(
        functools.partial(gate_up_kernel, len(rows), 1024),
        in_specs=[VMEM_SPEC] * len(inputs),
        out_specs=[VMEM_SPEC] * (1 + len(weights)),
        out_shape=[jax.ShapeDtypeStruct((total, columns), BF16)] + [out] * len(weights),
        compiler_params=params(12),
        cost_estimate=cost(2 * len(weights) * total * depth * width, 2 * len(weights) * depth * width),
    )(*[in_vmem(x) for x in inputs])


def silu(value):
    return value / (1.0 + jnp.exp(-value))


def down_blocks(hidden, hidden_shared, share, down, down_shared, outs, chunks, order):
    size = hidden.shape[0] // len(order)
    half = len(order) // 2
    part = outs[0].shape[-1]
    tile = tile_of(part)
    for n, chunk in enumerate(chunks):
        keep, send = outs[2 * n : 2 * n + 2]
        for place, j in enumerate(chunk):
            for c in range(part // tile):
                cut = slice(j * part + c * tile, j * part + (c + 1) * tile)
                routed = jnp.dot(hidden, down[:, cut], preferred_element_type=F32) * share
                routed += jnp.dot(hidden_shared, down_shared[:, cut], preferred_element_type=F32)
                for at, r in enumerate(order):
                    block = routed[r * size : (r + 1) * size].astype(BF16)
                    target, row = (keep, at) if at < half else (send, at - half)
                    target[row, place, :, c * tile : (c + 1) * tile] = block


def down_next_kernel(chunks, order, hidden, hidden_shared, share, down, down_shared, *outs):
    down_blocks(
        hidden[...], hidden_shared[...], share[:, :1], down, down_shared, outs, chunks, order
    )


def down_kernel(experts, chunks, order, *refs):
    count = len(order)
    half = count // 2
    inner, gate, up, gate_shared, up_shared = [ref[...] for ref in refs[:5]]
    refs = refs[5:]
    columns, shared_b = refs[:2]
    messages = refs[2 : 2 + count]
    down, down_shared = refs[2 + count : 4 + count]
    hidden_out, hidden_shared_out, share_out = refs[4 + count : 7 + count]
    outs = refs[7 + count :]
    total, width = gate.shape
    size = total // count
    shared_count = shared_b.shape[0]
    store_count = columns.shape[1] // count
    wide, per, _ = message_layout(count, store_count)
    own = columns[2:3, :1]

    rows = slice(store_count, store_count + size)
    meta = jnp.concatenate(
        [ref[rows, :META] for ref in messages[:2]] + [ref[rows, wide - META :] for ref in messages[2:]],
        axis=0,
    ).astype(F32)
    lane = lax.broadcasted_iota(jnp.int32, meta.shape, 1)
    mine = (lane < 3 * experts) & (lane % experts == own)
    share = jnp.sum(jnp.where(mine, meta, 0.0), axis=1, keepdims=True)
    row_tenant = jnp.sum(jnp.where(lane == 3 * experts, meta, 0.0), axis=1, keepdims=True)
    row_tenant = row_tenant.astype(jnp.int32)

    lifted = []
    for k in range(count):
        parts = [inner[k * size : (k + 1) * size, shared_count:]]
        for h in range(2, count, 2):
            sender = h + k % 2
            n = (k ^ sender) // 2
            rows = slice(store_count + n // per * size, store_count + (n // per + 1) * size)
            lanes = slice(n % per * 2 * store_count, (n % per + 1) * 2 * store_count)
            block = messages[sender][rows, lanes]
            if k % 2:
                block = jnp.concatenate([block[:, store_count:], block[:, :store_count]], axis=1)
            parts.append(block)
        lifted.append(jnp.concatenate(parts, axis=1))
    lifted = jnp.concatenate(lifted, axis=0)
    zero = jnp.zeros((), BF16)
    lifted = jnp.where(row_tenant == columns[1:2], lifted, zero)
    shared_tenant = columns[0:1, :shared_count]
    lifted_shared = jnp.where(row_tenant == shared_tenant, inner[:, :shared_count], zero)
    factor = jnp.concatenate([ref[:store_count, :width] for ref in messages], axis=0)
    upward = up + jnp.dot(lifted, factor, preferred_element_type=F32)
    hidden = (silu(gate) * upward).astype(BF16)
    upward = up_shared + jnp.dot(lifted_shared, shared_b[...], preferred_element_type=F32)
    here = (row_tenant >= shared_tenant[:, :1]) & (row_tenant <= shared_tenant[:, shared_count - 1 :])
    hidden_shared = jnp.where(here, silu(gate_shared) * upward, 0.0).astype(BF16)

    hidden_out[...] = hidden
    hidden_shared_out[...] = hidden_shared
    share_out[...] = jnp.broadcast_to(share, share_out.shape)
    down_blocks(hidden, hidden_shared, share, down, down_shared, outs, chunks, order)


def down_outs(rows, depth, chunks, order):
    size = rows // len(order)
    part = depth // lax.axis_size("tensor")
    outs = []
    for chunk in chunks:
        outs += [jax.ShapeDtypeStruct((len(order) // 2, len(chunk), size, part), BF16)] * 2
    return outs


def down_cost(rows, down, chunks):
    part = sum(len(chunk) for chunk in chunks) * down.size // lax.axis_size("tensor")
    return cost(4 * rows * part, 0)


def down_products(gated, columns, shared_b, messages, down, down_shared, experts, chunks, order):
    rows, width = gated[1].shape
    whole = [*gated, columns, shared_b, *messages, down, down_shared]
    outs = [jax.ShapeDtypeStruct((rows, width), BF16)] * 2
    outs += [jax.ShapeDtypeStruct((rows, 128), F32)]
    outs += down_outs(rows, down.shape[1], chunks, order)
    return pl.pallas_call(
        functools.partial(down_kernel, experts, chunks, order),
        in_specs=[VMEM_SPEC] * len(whole),
        out_specs=[VMEM_SPEC] * len(outs),
        out_shape=outs,
        compiler_params=params(16),
        cost_estimate=down_cost(rows, down, chunks),
    )(*[in_vmem(x) for x in whole])


def down_next(hidden, down, down_shared, chunks, order):
    rows = hidden[0].shape[0]
    whole = [*hidden, down, down_shared]
    outs = down_outs(rows, down.shape[1], chunks, order)
    return pl.pallas_call(
        functools.partial(down_next_kernel, chunks, order),
        in_specs=[VMEM_SPEC] * len(whole),
        out_specs=[VMEM_SPEC] * len(outs),
        out_shape=outs,
        compiler_params=params(16),
        cost_estimate=down_cost(rows, down, chunks),
    )(*[in_vmem(x) for x in whole])


def local(
    tokens,
    expert_ids,
    gate_values,
    tenant_ids,
    w_gate,
    w_up,
    routed_down_weight,
    shared_gate,
    shared_up,
    shared_down,
    store_a,
    store_b,
    pair_slot,
    shared_a,
    shared_b,
):
    experts = pair_slot.shape[0]
    adapted, rank, model_width = store_a.shape
    hid = store_b.shape[2]
    steps, size, _ = expert_ids.shape
    count = lax.axis_size("expert")
    n_tensor = lax.axis_size("tensor")
    shared_count, store_count = shared_a.shape[0] * rank, adapted * rank

    rows_own = tokens.reshape(steps * size, model_width)
    arrived = swap(rows_own, count // 2)
    store_other = swap(store_a, 1).reshape(store_count, model_width)
    first = first_call(
        experts,
        jnp.swapaxes(expert_ids, 1, 2),
        jnp.swapaxes(gate_values, 1, 2),
        tenant_ids.reshape(1, size),
        pair_slot,
        [
            rows_own,
            store_b.reshape(store_count, hid),
            shared_b.reshape(shared_count, hid),
            store_a.reshape(store_count, model_width),
            shared_a.reshape(shared_count, model_width),
            w_gate[0],
            w_up[0],
            shared_gate,
            shared_up,
            routed_down_weight[0],
            shared_down,
        ],
    )
    pack, columns, rows_held, shared_b_held, factor_store, factor_shared = first[:6]
    weights, down, down_own = first[6:10], first[10], first[11]
    pack_other = swap(pack, 1)
    arrived, rows_held, store_other, pack_other = lax.optimization_barrier(
        (arrived, rows_held, store_other, pack_other)
    )
    came = far_rows(arrived, rows_own)
    message = make_message([rows_held, *came], factor_store, store_other, pack)
    messages = [pack, pack_other] + [swap(message, r) for r in range(2, count)]
    came, message = lax.optimization_barrier((came, message))
    rows = [rows_held, swap(rows_own, 1)]
    for value in came:
        rows += [value, swap(value, 1)]
    gated = gate_up(rows, [factor_shared, factor_store, store_other], weights)

    order = [0]
    bit = count // 2
    while bit >= 1:
        order = order + [r | bit for r in order]
        bit //= 2
    chunks = [[j] for j in range(n_tensor - 1, -1, -1)]
    hidden = down_products(
        gated, columns, shared_b_held, messages, down, down_own, experts, chunks[:-2], order
    )
    hidden, held, leaving = hidden[:3], list(hidden[3::2]), list(hidden[4::2])
    bit = 1
    while bit < count:
        half = count // (2 * bit) // 2
        if bit > 1:
            for n in range(1, len(leaving)):
                leaving[n], *_ = lax.optimization_barrier((leaving[n], leaving[n - 1]))
        arrived = [swap(value, bit) for value in leaving]
        if bit == 1:
            ready = add(held[0][half:], arrived[0][half:])
            hidden, ready = lax.optimization_barrier((hidden, ready))
            rest = down_next(hidden, down, down_own, chunks[len(held) :], order)
            held += rest[0::2]
            arrived += [swap(value, bit) for value in rest[1::2]]
        if 2 * bit < count:
            leaving = [add(h[half:], a[half:]) for h, a in zip(held, arrived)]
            held = [add(h[:half], a[:half]) for h, a in zip(held, arrived)]
        bit *= 2
    parts = {}
    for n, chunk in enumerate(chunks):
        for place, j in enumerate(chunk):
            parts[j] = [held[n][0, place], arrived[n][0, place]]
    bit = 1
    while bit < n_tensor:
        for j in sorted([j for j in parts if j & bit], reverse=True):
            parts[j ^ bit].append(swap(total_of(parts.pop(j)), bit, "tensor"))
        bit *= 2
    return total_of(parts[0]).reshape(steps, size, model_width // n_tensor)


def solution(mesh):
    return jax.shard_map(
        local,
        mesh=mesh,
        in_specs=(
            P(None, ("groups", "expert"), None),
            P(None, ("groups", "expert"), None),
            P(None, ("groups", "expert"), None),
            P(("groups", "expert")),
            P("expert", None, "tensor"),
            P("expert", None, "tensor"),
            P("expert", "tensor", None),
            P(None, "tensor"),
            P(None, "tensor"),
            P("tensor", None),
            P("expert", None, None),
            P("expert", None, "tensor"),
            P(),
            P("expert", None, None),
            P("expert", None, "tensor"),
        ),
        out_specs=P(None, ("groups", "expert"), "tensor"),
        check_vma=False,
    )
```

```python
import functools

import jax
import jax.numpy as jnp
from jax import lax
from jax.experimental import pallas as pl
from jax.experimental.pallas import tpu as pltpu
from jax.sharding import PartitionSpec as P

F32 = jnp.float32
BF16 = jnp.bfloat16
MIB = 1024 * 1024


def params(mebibytes):
    return pltpu.CompilerParams(vmem_limit_bytes=mebibytes * MIB)


def cost(flops, moved):
    return pl.CostEstimate(flops=int(flops), bytes_accessed=int(moved), transcendentals=0)


def in_vmem(value):
    return pltpu.with_memory_space_constraint(value, pltpu.VMEM)


def in_hbm(value):
    return pltpu.with_memory_space_constraint(value, pltpu.HBM)


def vmem_shape(value):
    return pltpu.VMEM(value.shape, value.dtype)


VMEM_SPEC = pl.BlockSpec(memory_space=pltpu.VMEM)
HBM_SPEC = pl.BlockSpec(memory_space=pltpu.HBM)


def crossed(index):
    return index ^ ((index >> 1) & 1)


def swap(value, bits, axis="expert"):
    count = lax.axis_size(axis)
    number = crossed if axis == "expert" else int
    return lax.ppermute(value, axis, [(i, number(number(i) ^ bits)) for i in range(count)])


def add(one, other):
    return (one.astype(F32) + other.astype(F32)).astype(BF16)


def total_of(values):
    return sum(value.astype(F32) for value in values).astype(BF16)


def far_rows(arrived, rows_own):
    count = lax.axis_size("expert")
    bit = count // 2
    pieces = {0: rows_own, bit: arrived}
    bit //= 2
    while bit > 1:
        pieces.update({r ^ bit: swap(piece, bit) for r, piece in list(pieces.items())})
        bit //= 2
    return [pieces[r] for r in range(2, count, 2)]


def tile_of(width):
    return 256 if width % 256 == 0 else 128


def column_of(row, size):
    lane = lax.broadcasted_iota(jnp.int32, (size, row.shape[1]), 1)
    place = lax.broadcasted_iota(jnp.int32, (size, row.shape[1]), 0)
    return jnp.sum(jnp.where(lane == place, row.astype(F32), 0.0), axis=1, keepdims=True)


def first_kernel(
    experts, ids, values, tenants, pair_slot, rows, store_b, shared_b, factor_store, factor_shared,
    gate_weight, up_weight, gate_shared, up_shared, down, down_shared, pack, columns, *refs
):
    targets, (ids_held, values_held, tenants_held, pair_slot_held, small_sems, sems) = refs[:-6], refs[-6:]
    own, own_part = lax.axis_index("expert"), lax.axis_index("tensor")
    parts = lax.axis_size("tensor")
    small = [
        (ids, ids_held), (values, values_held), (tenants, tenants_held), (pair_slot, pair_slot_held)
    ]
    small = [
        pltpu.make_async_copy(source, target, small_sems.at[n])
        for n, (source, target) in enumerate(small)
    ]
    sources = [
        rows, store_b, shared_b, factor_store, factor_shared, gate_weight, up_weight, gate_shared,
        up_shared, down, down_shared,
    ]
    shared_count, (store_count, width) = shared_b.shape[0], store_b.shape
    staged = list(zip(sources[:5], (targets[0], pack.at[pl.ds(0, store_count), pl.ds(0, width)], *targets[1:4])))
    targets = (None, *targets)
    piece = gate_weight.shape[0] // parts
    for source, target in zip(sources[5:9], targets[5:9]):
        for k in range(parts):
            part = pl.ds(k * piece, piece)
            staged.append((source.at[part], target.at[part]))
    for source, target in zip(sources[9:], targets[9:]):
        for j in range(parts):
            start = pl.multiple_of((own_part ^ j) * piece, piece)
            staged.append((source.at[:, pl.ds(start, piece)], target.at[:, pl.ds(j * piece, piece)]))
    staged = [
        pltpu.make_async_copy(source, target, sems.at[n])
        for n, (source, target) in enumerate(staged)
    ]
    for copy in (*small, *staged):
        copy.start()
    for copy in small:
        copy.wait()

    steps, top, size = ids_held.shape
    tenant = column_of(tenants_held[...], size)
    lane = lax.broadcasted_iota(jnp.int32, (size, META), 1)
    for s in range(steps):
        weight = jnp.zeros(lane.shape, F32)
        for k in range(top):
            expert = column_of(ids_held[s, k : k + 1], size).astype(jnp.int32)
            value = column_of(values_held[s, k : k + 1], size)
            weight = weight + jnp.where(expert == lane % experts, value, 0.0)
        high = weight.astype(BF16).astype(F32)
        middle = (weight - high).astype(BF16).astype(F32)
        low = weight - high - middle
        found = jnp.where(lane < experts, high, jnp.where(lane < 2 * experts, middle, low))
        found = jnp.where(lane < 3 * experts, found, tenant)
        start = store_count + s * size
        pack[start : start + size, :META] = found.astype(BF16)
        if pack.shape[1] > META:
            pack[start : start + size, META:] = jnp.zeros((size, pack.shape[1] - META), BF16)

    tenant_count = pair_slot_held.shape[1]
    place = lax.broadcasted_iota(jnp.int32, pair_slot_held.shape, 0)
    own_row = jnp.sum(
        jnp.where(place == own, pair_slot_held[...].astype(F32), 0.0), axis=0, keepdims=True
    )
    own_slots = column_of(own_row, tenant_count).astype(jnp.int32)
    total = columns.shape[1]
    per_device = tenant_count // lax.axis_size("expert")
    rank = shared_count // per_device
    column = lax.broadcasted_iota(jnp.int32, (1, total), 1)
    shared_tenant = own * per_device + column % shared_count // rank
    holder = crossed(crossed(own) ^ (column // store_count))
    slot = holder * (store_count // rank) + column % store_count // rank
    tenant_number = lax.broadcasted_iota(jnp.int32, (tenant_count, total), 0)
    slot_tenant = jnp.max(jnp.where(own_slots == slot, tenant_number, -1), axis=0, keepdims=True)
    columns[0:1] = shared_tenant
    columns[1:2] = slot_tenant
    columns[2:3] = jnp.full((1, total), own, jnp.int32)
    columns[3:8] = jnp.zeros((5, total), jnp.int32)
    for copy in staged:
        copy.wait()


def first_call(experts, ids, values, tenants, pair_slot, staged):
    parts = lax.axis_size("tensor")
    steps, _, size = ids.shape
    columns = max(lax.axis_size("expert") * staged[1].shape[0], staged[2].shape[0])
    outs = [
        jax.ShapeDtypeStruct((staged[1].shape[0] + steps * size, max(META, staged[1].shape[1])), BF16),
        jax.ShapeDtypeStruct((8, columns), jnp.int32),
        *[vmem_shape(value) for n, value in enumerate(staged) if n != 1],
    ]
    inputs = [ids, values, tenants, pair_slot, *staged]
    return pl.pallas_call(
        functools.partial(first_kernel, experts),
        in_specs=[HBM_SPEC] * len(inputs),
        out_specs=[VMEM_SPEC] * len(outs),
        out_shape=outs,
        scratch_shapes=[
            pltpu.VMEM(ids.shape, jnp.int32),
            pltpu.VMEM(values.shape, F32),
            pltpu.VMEM(tenants.shape, jnp.int32),
            pltpu.VMEM(pair_slot.shape, jnp.int32),
            pltpu.SemaphoreType.DMA((4,)),
            pltpu.SemaphoreType.DMA((5 + 6 * parts,)),
        ],
        compiler_params=params(4),
        cost_estimate=cost(0, 2 * sum(value.size for value in staged)),
    )(*[in_hbm(value) for value in inputs])


META = 128


def message_layout(count, store_count):
    wide = max(128, 2 * store_count)
    per = wide // (2 * store_count)
    return wide + META, per, -(-(count // 2) // per)


def message_kernel(chunk, *refs):
    half = len(refs) - 4
    rows, (factor, factor_other, pack, out) = refs[:half], refs[half:]
    size, depth = rows[0].shape
    store_count, width = factor.shape[0], pack.shape[1]
    meta = pack[store_count:, :META]
    total = 0.0
    for k in range(depth // chunk):
        part = pl.ds(k * chunk, chunk)
        total += lax.dot_general(
            jnp.concatenate([ref[:, part] for ref in rows], axis=0),
            jnp.concatenate([factor[:, part], factor_other[:, part]], axis=0),
            (((1,), (1,)), ((), ())),
            preferred_element_type=F32,
        )
    total = total.astype(BF16)
    wide, per, lines = message_layout(2 * half, store_count)
    out[:store_count, :width] = pack[:store_count]
    if width < wide:
        out[:store_count, width:] = jnp.zeros((store_count, wide - width), BF16)
    for line in range(lines):
        blocks = [
            total[n * size : (n + 1) * size] if n < half else jnp.zeros((size, 2 * store_count), BF16)
            for n in range(line * per, (line + 1) * per)
        ]
        blocks.append(meta if line == 0 else jnp.zeros(meta.shape, BF16))
        start = store_count + line * size
        out[start : start + size] = jnp.concatenate(blocks, axis=1)


def make_message(rows, factor, factor_other, pack):
    size, depth = rows[0].shape
    store_count = factor.shape[0]
    wide, _, lines = message_layout(2 * len(rows), store_count)
    inputs = [*rows, factor, factor_other, pack]
    return pl.pallas_call(
        functools.partial(message_kernel, 1024),
        in_specs=[VMEM_SPEC] * len(inputs),
        out_specs=VMEM_SPEC,
        out_shape=jax.ShapeDtypeStruct((store_count + lines * size, wide), BF16),
        compiler_params=params(8),
        cost_estimate=cost(4 * size * len(rows) * depth * store_count, 2 * depth * store_count * 2),
    )(*[in_vmem(value) for value in inputs])


def gate_up_kernel(count, chunk, *refs):
    rows, factors, weights = refs[:count], refs[count : count + 3], refs[count + 3 : count + 7]
    inner, outs = refs[count + 7], refs[count + 8 :]
    depth = rows[0].shape[1]
    pieces = [pl.ds(k * chunk, chunk) for k in range(depth // chunk)]
    for weight, out in zip(weights, outs):
        total = jnp.zeros(out.shape, F32)
        for part in pieces:
            block = jnp.concatenate([ref[:, part] for ref in rows], axis=0)
            total += jnp.dot(block, weight[part], preferred_element_type=F32)
        out[...] = total
    total = jnp.zeros(inner.shape, F32)
    for part in pieces:
        block = jnp.concatenate([ref[:, part] for ref in rows], axis=0)
        factor = jnp.concatenate([ref[:, part] for ref in factors], axis=0)
        total += lax.dot_general(
            block, factor, (((1,), (1,)), ((), ())), preferred_element_type=F32
        )
    inner[...] = total.astype(BF16)


def gate_up(rows, factors, weights):
    depth, width = weights[0].shape
    total = rows[0].shape[0] * len(rows)
    columns = sum(factor.shape[0] for factor in factors)
    inputs = [*rows, *factors, *weights]
    out = jax.ShapeDtypeStruct((total, width), F32)
    return pl.pallas_call(
        functools.partial(gate_up_kernel, len(rows), 1024),
        in_specs=[VMEM_SPEC] * len(inputs),
        out_specs=[VMEM_SPEC] * (1 + len(weights)),
        out_shape=[jax.ShapeDtypeStruct((total, columns), BF16)] + [out] * len(weights),
        compiler_params=params(12),
        cost_estimate=cost(2 * len(weights) * total * depth * width, 2 * len(weights) * depth * width),
    )(*[in_vmem(x) for x in inputs])


def silu(value):
    return value / (1.0 + jnp.exp(-value))


def down_blocks(hidden, hidden_shared, share, down, down_shared, outs, chunks, order):
    size = hidden.shape[0] // len(order)
    half = len(order) // 2
    part = outs[0].shape[-1]
    tile = tile_of(part)
    for n, chunk in enumerate(chunks):
        keep, send = outs[2 * n : 2 * n + 2]
        for place, j in enumerate(chunk):
            for c in range(part // tile):
                cut = slice(j * part + c * tile, j * part + (c + 1) * tile)
                routed = jnp.dot(hidden, down[:, cut], preferred_element_type=F32) * share
                routed += jnp.dot(hidden_shared, down_shared[:, cut], preferred_element_type=F32)
                for at, r in enumerate(order):
                    block = routed[r * size : (r + 1) * size].astype(BF16)
                    target, row = (keep, at) if at < half else (send, at - half)
                    target[row, place, :, c * tile : (c + 1) * tile] = block


def down_next_kernel(chunks, order, hidden, hidden_shared, share, down, down_shared, *outs):
    down_blocks(
        hidden[...], hidden_shared[...], share[:, :1], down, down_shared, outs, chunks, order
    )


def down_kernel(experts, chunks, order, *refs):
    count = len(order)
    half = count // 2
    inner, gate, up, gate_shared, up_shared = [ref[...] for ref in refs[:5]]
    refs = refs[5:]
    columns, shared_b = refs[:2]
    messages = refs[2 : 2 + count]
    down, down_shared = refs[2 + count : 4 + count]
    hidden_out, hidden_shared_out, share_out = refs[4 + count : 7 + count]
    outs = refs[7 + count :]
    total, width = gate.shape
    size = total // count
    shared_count = shared_b.shape[0]
    store_count = columns.shape[1] // count
    wide, per, _ = message_layout(count, store_count)
    own = columns[2:3, :1]

    rows = slice(store_count, store_count + size)
    meta = jnp.concatenate(
        [ref[rows, :META] for ref in messages[:2]] + [ref[rows, wide - META :] for ref in messages[2:]],
        axis=0,
    ).astype(F32)
    lane = lax.broadcasted_iota(jnp.int32, meta.shape, 1)
    mine = (lane < 3 * experts) & (lane % experts == own)
    share = jnp.sum(jnp.where(mine, meta, 0.0), axis=1, keepdims=True)
    row_tenant = jnp.sum(jnp.where(lane == 3 * experts, meta, 0.0), axis=1, keepdims=True)
    row_tenant = row_tenant.astype(jnp.int32)

    lifted = []
    for k in range(count):
        parts = [inner[k * size : (k + 1) * size, shared_count:]]
        for h in range(2, count, 2):
            sender = h + k % 2
            n = (k ^ sender) // 2
            rows = slice(store_count + n // per * size, store_count + (n // per + 1) * size)
            lanes = slice(n % per * 2 * store_count, (n % per + 1) * 2 * store_count)
            block = messages[sender][rows, lanes]
            if k % 2:
                block = jnp.concatenate([block[:, store_count:], block[:, :store_count]], axis=1)
            parts.append(block)
        lifted.append(jnp.concatenate(parts, axis=1))
    lifted = jnp.concatenate(lifted, axis=0)
    zero = jnp.zeros((), BF16)
    lifted = jnp.where(row_tenant == columns[1:2], lifted, zero)
    shared_tenant = columns[0:1, :shared_count]
    lifted_shared = jnp.where(row_tenant == shared_tenant, inner[:, :shared_count], zero)
    factor = jnp.concatenate([ref[:store_count, :width] for ref in messages], axis=0)
    upward = up + jnp.dot(lifted, factor, preferred_element_type=F32)
    hidden = (silu(gate) * upward).astype(BF16)
    upward = up_shared + jnp.dot(lifted_shared, shared_b[...], preferred_element_type=F32)
    here = (row_tenant >= shared_tenant[:, :1]) & (row_tenant <= shared_tenant[:, shared_count - 1 :])
    hidden_shared = jnp.where(here, silu(gate_shared) * upward, 0.0).astype(BF16)

    hidden_out[...] = hidden
    hidden_shared_out[...] = hidden_shared
    share_out[...] = jnp.broadcast_to(share, share_out.shape)
    down_blocks(hidden, hidden_shared, share, down, down_shared, outs, chunks, order)


def down_outs(rows, depth, chunks, order):
    size = rows // len(order)
    part = depth // lax.axis_size("tensor")
    outs = []
    for chunk in chunks:
        outs += [jax.ShapeDtypeStruct((len(order) // 2, len(chunk), size, part), BF16)] * 2
    return outs


def down_cost(rows, down, chunks):
    part = sum(len(chunk) for chunk in chunks) * down.size // lax.axis_size("tensor")
    return cost(4 * rows * part, 0)


def down_products(gated, columns, shared_b, messages, down, down_shared, experts, chunks, order):
    rows, width = gated[1].shape
    whole = [*gated, columns, shared_b, *messages, down, down_shared]
    outs = [jax.ShapeDtypeStruct((rows, width), BF16)] * 2
    outs += [jax.ShapeDtypeStruct((rows, 128), F32)]
    outs += down_outs(rows, down.shape[1], chunks, order)
    return pl.pallas_call(
        functools.partial(down_kernel, experts, chunks, order),
        in_specs=[VMEM_SPEC] * len(whole),
        out_specs=[VMEM_SPEC] * len(outs),
        out_shape=outs,
        compiler_params=params(16),
        cost_estimate=down_cost(rows, down, chunks),
    )(*[in_vmem(x) for x in whole])


def down_next(hidden, down, down_shared, chunks, order):
    rows = hidden[0].shape[0]
    whole = [*hidden, down, down_shared]
    outs = down_outs(rows, down.shape[1], chunks, order)
    return pl.pallas_call(
        functools.partial(down_next_kernel, chunks, order),
        in_specs=[VMEM_SPEC] * len(whole),
        out_specs=[VMEM_SPEC] * len(outs),
        out_shape=outs,
        compiler_params=params(16),
        cost_estimate=down_cost(rows, down, chunks),
    )(*[in_vmem(x) for x in whole])


def local(
    tokens,
    expert_ids,
    gate_values,
    tenant_ids,
    w_gate,
    w_up,
    routed_down_weight,
    shared_gate,
    shared_up,
    shared_down,
    store_a,
    store_b,
    pair_slot,
    shared_a,
    shared_b,
):
    experts = pair_slot.shape[0]
    adapted, rank, model_width = store_a.shape
    hid = store_b.shape[2]
    steps, size, _ = expert_ids.shape
    count = lax.axis_size("expert")
    n_tensor = lax.axis_size("tensor")
    shared_count, store_count = shared_a.shape[0] * rank, adapted * rank

    rows_own = tokens.reshape(steps * size, model_width)
    arrived = swap(rows_own, count // 2)
    store_other = swap(store_a, 1).reshape(store_count, model_width)
    first = first_call(
        experts,
        jnp.swapaxes(expert_ids, 1, 2),
        jnp.swapaxes(gate_values, 1, 2),
        tenant_ids.reshape(1, size),
        pair_slot,
        [
            rows_own,
            store_b.reshape(store_count, hid),
            shared_b.reshape(shared_count, hid),
            store_a.reshape(store_count, model_width),
            shared_a.reshape(shared_count, model_width),
            w_gate[0],
            w_up[0],
            shared_gate,
            shared_up,
            routed_down_weight[0],
            shared_down,
        ],
    )
    pack, columns, rows_held, shared_b_held, factor_store, factor_shared = first[:6]
    weights, down, down_own = first[6:10], first[10], first[11]
    pack_other = swap(pack, 1)
    arrived, rows_held, store_other, pack_other = lax.optimization_barrier(
        (arrived, rows_held, store_other, pack_other)
    )
    came = far_rows(arrived, rows_own)
    message = make_message([rows_held, *came], factor_store, store_other, pack)
    messages = [pack, pack_other] + [swap(message, r) for r in range(2, count)]
    came, message = lax.optimization_barrier((came, message))
    rows = [rows_held, swap(rows_own, 1)]
    for value in came:
        rows += [value, swap(value, 1)]
    gated = gate_up(rows, [factor_shared, factor_store, store_other], weights)

    order = [0]
    bit = count // 2
    while bit >= 1:
        order = order + [r | bit for r in order]
        bit //= 2
    chunks = [[j] for j in range(n_tensor - 1, -1, -1)]
    hidden = down_products(
        gated, columns, shared_b_held, messages, down, down_own, experts, chunks[:-2], order
    )
    hidden, held, leaving = hidden[:3], list(hidden[3::2]), list(hidden[4::2])
    bit = 1
    while bit < count:
        half = count // (2 * bit) // 2
        if bit > 1:
            for n in range(1, len(leaving)):
                leaving[n], *_ = lax.optimization_barrier((leaving[n], leaving[n - 1]))
        arrived = [swap(value, bit) for value in leaving]
        if bit == 1:
            ready = add(held[0][half:], arrived[0][half:])
            hidden, ready = lax.optimization_barrier((hidden, ready))
            rest = down_next(hidden, down, down_own, chunks[len(held) :], order)
            held += rest[0::2]
            arrived += [swap(value, bit) for value in rest[1::2]]
        if 2 * bit < count:
            leaving = [add(h[half:], a[half:]) for h, a in zip(held, arrived)]
            held = [add(h[:half], a[:half]) for h, a in zip(held, arrived)]
        bit *= 2
    parts = {}
    for n, chunk in enumerate(chunks):
        for place, j in enumerate(chunk):
            parts[j] = [held[n][0, place], arrived[n][0, place]]
    bit = 1
    while bit < n_tensor:
        for j in sorted([j for j in parts if j & bit], reverse=True):
            parts[j ^ bit].append(swap(total_of(parts.pop(j)), bit, "tensor"))
        bit *= 2
    return total_of(parts[0]).reshape(steps, size, model_width // n_tensor)


def solution(mesh):
    return jax.shard_map(
        local,
        mesh=mesh,
        in_specs=(
            P(None, ("groups", "expert"), None),
            P(None, ("groups", "expert"), None),
            P(None, ("groups", "expert"), None),
            P(("groups", "expert")),
            P("expert", None, "tensor"),
            P("expert", None, "tensor"),
            P("expert", "tensor", None),
            P(None, "tensor"),
            P(None, "tensor"),
            P("tensor", None),
            P("expert", None, None),
            P("expert", None, "tensor"),
            P(),
            P("expert", None, None),
            P("expert", None, "tensor"),
        ),
        out_specs=P(None, ("groups", "expert"), "tensor"),
        check_vma=False,
    )
```

```python
import functools

import jax
import jax.numpy as jnp
from jax import lax
from jax.experimental import pallas as pl
from jax.experimental.pallas import tpu as pltpu
from jax.sharding import PartitionSpec as P

F32 = jnp.float32
BF16 = jnp.bfloat16
MIB = 1024 * 1024


def params(mebibytes):
    return pltpu.CompilerParams(vmem_limit_bytes=mebibytes * MIB)


def cost(flops, moved):
    return pl.CostEstimate(flops=int(flops), bytes_accessed=int(moved), transcendentals=0)


def in_vmem(value):
    return pltpu.with_memory_space_constraint(value, pltpu.VMEM)


def in_hbm(value):
    return pltpu.with_memory_space_constraint(value, pltpu.HBM)


def vmem_shape(value):
    return pltpu.VMEM(value.shape, value.dtype)


VMEM_SPEC = pl.BlockSpec(memory_space=pltpu.VMEM)
HBM_SPEC = pl.BlockSpec(memory_space=pltpu.HBM)


def swap(value, bits, axis="expert"):
    count = lax.axis_size(axis)
    return lax.ppermute(value, axis, [(i, i ^ bits) for i in range(count)])


def add(one, other):
    return (one.astype(F32) + other.astype(F32)).astype(BF16)


def total_of(values):
    return sum(value.astype(F32) for value in values).astype(BF16)


def far_rows(arrived, rows_own):
    count = lax.axis_size("expert")
    bit = count // 2
    pieces = {0: rows_own, bit: arrived}
    bit //= 2
    while bit > 1:
        pieces.update({r ^ bit: swap(piece, bit) for r, piece in list(pieces.items())})
        bit //= 2
    return [pieces[r] for r in range(2, count, 2)]


def tile_of(width):
    return 256 if width % 256 == 0 else 128


def column_of(row, size):
    lane = lax.broadcasted_iota(jnp.int32, (size, row.shape[1]), 1)
    place = lax.broadcasted_iota(jnp.int32, (size, row.shape[1]), 0)
    return jnp.sum(jnp.where(lane == place, row.astype(F32), 0.0), axis=1, keepdims=True)


def first_kernel(
    experts, ids, values, tenants, pair_slot, rows, store_b, shared_b, factor_store, factor_shared,
    gate_weight, up_weight, gate_shared, up_shared, down, down_shared, pack, columns, *refs
):
    targets, (ids_held, values_held, tenants_held, pair_slot_held, small_sems, sems) = refs[:-6], refs[-6:]
    own, own_part = lax.axis_index("expert"), lax.axis_index("tensor")
    parts = lax.axis_size("tensor")
    small = [
        (ids, ids_held), (values, values_held), (tenants, tenants_held), (pair_slot, pair_slot_held)
    ]
    small = [
        pltpu.make_async_copy(source, target, small_sems.at[n])
        for n, (source, target) in enumerate(small)
    ]
    sources = [
        rows, store_b, shared_b, factor_store, factor_shared, gate_weight, up_weight, gate_shared,
        up_shared, down, down_shared,
    ]
    shared_count, (store_count, width) = shared_b.shape[0], store_b.shape
    staged = list(zip(sources[:5], (targets[0], pack.at[pl.ds(0, store_count), pl.ds(0, width)], *targets[1:4])))
    targets = (None, *targets)
    piece = gate_weight.shape[0] // parts
    for source, target in zip(sources[5:9], targets[5:9]):
        for k in range(parts):
            part = pl.ds(k * piece, piece)
            staged.append((source.at[part], target.at[part]))
    for source, target in zip(sources[9:], targets[9:]):
        for j in range(parts):
            start = pl.multiple_of((own_part ^ j) * piece, piece)
            staged.append((source.at[:, pl.ds(start, piece)], target.at[:, pl.ds(j * piece, piece)]))
    staged = [
        pltpu.make_async_copy(source, target, sems.at[n])
        for n, (source, target) in enumerate(staged)
    ]
    for copy in (*small, *staged):
        copy.start()
    for copy in small:
        copy.wait()

    steps, top, size = ids_held.shape
    tenant = column_of(tenants_held[...], size)
    lane = lax.broadcasted_iota(jnp.int32, (size, META), 1)
    for s in range(steps):
        weight = jnp.zeros(lane.shape, F32)
        for k in range(top):
            expert = column_of(ids_held[s, k : k + 1], size).astype(jnp.int32)
            value = column_of(values_held[s, k : k + 1], size)
            weight = weight + jnp.where(expert == lane % experts, value, 0.0)
        high = weight.astype(BF16).astype(F32)
        middle = (weight - high).astype(BF16).astype(F32)
        low = weight - high - middle
        found = jnp.where(lane < experts, high, jnp.where(lane < 2 * experts, middle, low))
        found = jnp.where(lane < 3 * experts, found, tenant)
        start = store_count + s * size
        pack[start : start + size, :META] = found.astype(BF16)
        if pack.shape[1] > META:
            pack[start : start + size, META:] = jnp.zeros((size, pack.shape[1] - META), BF16)

    tenant_count = pair_slot_held.shape[1]
    place = lax.broadcasted_iota(jnp.int32, pair_slot_held.shape, 0)
    own_row = jnp.sum(
        jnp.where(place == own, pair_slot_held[...].astype(F32), 0.0), axis=0, keepdims=True
    )
    own_slots = column_of(own_row, tenant_count).astype(jnp.int32)
    total = columns.shape[1]
    per_device = tenant_count // lax.axis_size("expert")
    rank = shared_count // per_device
    column = lax.broadcasted_iota(jnp.int32, (1, total), 1)
    shared_tenant = own * per_device + column % shared_count // rank
    slot = (own ^ (column // store_count)) * (store_count // rank) + column % store_count // rank
    tenant_number = lax.broadcasted_iota(jnp.int32, (tenant_count, total), 0)
    slot_tenant = jnp.max(jnp.where(own_slots == slot, tenant_number, -1), axis=0, keepdims=True)
    columns[0:1] = shared_tenant
    columns[1:2] = slot_tenant
    columns[2:3] = jnp.full((1, total), own, jnp.int32)
    columns[3:8] = jnp.zeros((5, total), jnp.int32)
    for copy in staged:
        copy.wait()


def first_call(experts, ids, values, tenants, pair_slot, staged):
    parts = lax.axis_size("tensor")
    steps, _, size = ids.shape
    columns = max(lax.axis_size("expert") * staged[1].shape[0], staged[2].shape[0])
    outs = [
        jax.ShapeDtypeStruct((staged[1].shape[0] + steps * size, max(META, staged[1].shape[1])), BF16),
        jax.ShapeDtypeStruct((8, columns), jnp.int32),
        *[vmem_shape(value) for n, value in enumerate(staged) if n != 1],
    ]
    inputs = [ids, values, tenants, pair_slot, *staged]
    return pl.pallas_call(
        functools.partial(first_kernel, experts),
        in_specs=[HBM_SPEC] * len(inputs),
        out_specs=[VMEM_SPEC] * len(outs),
        out_shape=outs,
        scratch_shapes=[
            pltpu.VMEM(ids.shape, jnp.int32),
            pltpu.VMEM(values.shape, F32),
            pltpu.VMEM(tenants.shape, jnp.int32),
            pltpu.VMEM(pair_slot.shape, jnp.int32),
            pltpu.SemaphoreType.DMA((4,)),
            pltpu.SemaphoreType.DMA((5 + 6 * parts,)),
        ],
        compiler_params=params(4),
        cost_estimate=cost(0, 2 * sum(value.size for value in staged)),
    )(*[in_hbm(value) for value in inputs])


META = 128


def message_layout(count, store_count):
    wide = max(128, 2 * store_count)
    per = wide // (2 * store_count)
    return wide + META, per, -(-(count // 2) // per)


def message_kernel(chunk, *refs):
    half = len(refs) - 4
    rows, (factor, factor_other, pack, out) = refs[:half], refs[half:]
    size, depth = rows[0].shape
    store_count, width = factor.shape[0], pack.shape[1]
    meta = pack[store_count:, :META]
    total = 0.0
    for k in range(depth // chunk):
        part = pl.ds(k * chunk, chunk)
        total += lax.dot_general(
            jnp.concatenate([ref[:, part] for ref in rows], axis=0),
            jnp.concatenate([factor[:, part], factor_other[:, part]], axis=0),
            (((1,), (1,)), ((), ())),
            preferred_element_type=F32,
        )
    total = total.astype(BF16)
    wide, per, lines = message_layout(2 * half, store_count)
    out[:store_count, :width] = pack[:store_count]
    if width < wide:
        out[:store_count, width:] = jnp.zeros((store_count, wide - width), BF16)
    for line in range(lines):
        blocks = [
            total[n * size : (n + 1) * size] if n < half else jnp.zeros((size, 2 * store_count), BF16)
            for n in range(line * per, (line + 1) * per)
        ]
        blocks.append(meta if line == 0 else jnp.zeros(meta.shape, BF16))
        start = store_count + line * size
        out[start : start + size] = jnp.concatenate(blocks, axis=1)


def make_message(rows, factor, factor_other, pack):
    size, depth = rows[0].shape
    store_count = factor.shape[0]
    wide, _, lines = message_layout(2 * len(rows), store_count)
    inputs = [*rows, factor, factor_other, pack]
    return pl.pallas_call(
        functools.partial(message_kernel, 1024),
        in_specs=[VMEM_SPEC] * len(inputs),
        out_specs=VMEM_SPEC,
        out_shape=jax.ShapeDtypeStruct((store_count + lines * size, wide), BF16),
        compiler_params=params(8),
        cost_estimate=cost(4 * size * len(rows) * depth * store_count, 2 * depth * store_count * 2),
    )(*[in_vmem(value) for value in inputs])


def gate_up_kernel(count, chunk, *refs):
    rows, factors, weights = refs[:count], refs[count : count + 3], refs[count + 3 : count + 7]
    inner, outs = refs[count + 7], refs[count + 8 :]
    depth = rows[0].shape[1]
    pieces = [pl.ds(k * chunk, chunk) for k in range(depth // chunk)]
    for weight, out in zip(weights, outs):
        total = jnp.zeros(out.shape, F32)
        for part in pieces:
            block = jnp.concatenate([ref[:, part] for ref in rows], axis=0)
            total += jnp.dot(block, weight[part], preferred_element_type=F32)
        out[...] = total
    total = jnp.zeros(inner.shape, F32)
    for part in pieces:
        block = jnp.concatenate([ref[:, part] for ref in rows], axis=0)
        factor = jnp.concatenate([ref[:, part] for ref in factors], axis=0)
        total += lax.dot_general(
            block, factor, (((1,), (1,)), ((), ())), preferred_element_type=F32
        )
    inner[...] = total.astype(BF16)


def gate_up(rows, factors, weights):
    depth, width = weights[0].shape
    total = rows[0].shape[0] * len(rows)
    columns = sum(factor.shape[0] for factor in factors)
    inputs = [*rows, *factors, *weights]
    out = jax.ShapeDtypeStruct((total, width), F32)
    return pl.pallas_call(
        functools.partial(gate_up_kernel, len(rows), 1024),
        in_specs=[VMEM_SPEC] * len(inputs),
        out_specs=[VMEM_SPEC] * (1 + len(weights)),
        out_shape=[jax.ShapeDtypeStruct((total, columns), BF16)] + [out] * len(weights),
        compiler_params=params(12),
        cost_estimate=cost(2 * len(weights) * total * depth * width, 2 * len(weights) * depth * width),
    )(*[in_vmem(x) for x in inputs])


def silu(value):
    return value / (1.0 + jnp.exp(-value))


def down_blocks(hidden, hidden_shared, share, down, down_shared, outs, chunks, order):
    size = hidden.shape[0] // len(order)
    half = len(order) // 2
    part = outs[0].shape[-1]
    tile = tile_of(part)
    for n, chunk in enumerate(chunks):
        keep, send = outs[2 * n : 2 * n + 2]
        for place, j in enumerate(chunk):
            for c in range(part // tile):
                cut = slice(j * part + c * tile, j * part + (c + 1) * tile)
                routed = jnp.dot(hidden, down[:, cut], preferred_element_type=F32) * share
                routed += jnp.dot(hidden_shared, down_shared[:, cut], preferred_element_type=F32)
                for at, r in enumerate(order):
                    block = routed[r * size : (r + 1) * size].astype(BF16)
                    target, row = (keep, at) if at < half else (send, at - half)
                    if at >= half and len(outs) % 2 and n == 0:
                        target, row = (outs[-1], 0) if at == half else (send, at - half - 1)
                    target[row, place, :, c * tile : (c + 1) * tile] = block


def down_next_kernel(chunks, order, hidden, hidden_shared, share, down, down_shared, *outs):
    down_blocks(
        hidden[...], hidden_shared[...], share[:, :1], down, down_shared, outs, chunks, order
    )


def down_kernel(experts, chunks, order, *refs):
    count = len(order)
    half = count // 2
    inner, gate, up, gate_shared, up_shared = [ref[...] for ref in refs[:5]]
    refs = refs[5:]
    columns, shared_b = refs[:2]
    messages = refs[2 : 2 + count]
    down, down_shared = refs[2 + count : 4 + count]
    hidden_out, hidden_shared_out, share_out = refs[4 + count : 7 + count]
    outs = refs[7 + count :]
    total, width = gate.shape
    size = total // count
    shared_count = shared_b.shape[0]
    store_count = columns.shape[1] // count
    wide, per, _ = message_layout(count, store_count)
    own = columns[2:3, :1]

    rows = slice(store_count, store_count + size)
    meta = jnp.concatenate(
        [ref[rows, :META] for ref in messages[:2]] + [ref[rows, wide - META :] for ref in messages[2:]],
        axis=0,
    ).astype(F32)
    lane = lax.broadcasted_iota(jnp.int32, meta.shape, 1)
    mine = (lane < 3 * experts) & (lane % experts == own)
    share = jnp.sum(jnp.where(mine, meta, 0.0), axis=1, keepdims=True)
    row_tenant = jnp.sum(jnp.where(lane == 3 * experts, meta, 0.0), axis=1, keepdims=True)
    row_tenant = row_tenant.astype(jnp.int32)

    lifted = []
    for k in range(count):
        parts = [inner[k * size : (k + 1) * size, shared_count:]]
        for h in range(2, count, 2):
            sender = h + k % 2
            n = (k ^ sender) // 2
            rows = slice(store_count + n // per * size, store_count + (n // per + 1) * size)
            lanes = slice(n % per * 2 * store_count, (n % per + 1) * 2 * store_count)
            block = messages[sender][rows, lanes]
            if k % 2:
                block = jnp.concatenate([block[:, store_count:], block[:, :store_count]], axis=1)
            parts.append(block)
        lifted.append(jnp.concatenate(parts, axis=1))
    lifted = jnp.concatenate(lifted, axis=0)
    zero = jnp.zeros((), BF16)
    lifted = jnp.where(row_tenant == columns[1:2], lifted, zero)
    shared_tenant = columns[0:1, :shared_count]
    lifted_shared = jnp.where(row_tenant == shared_tenant, inner[:, :shared_count], zero)
    factor = jnp.concatenate([ref[:store_count, :width] for ref in messages], axis=0)
    upward = up + jnp.dot(lifted, factor, preferred_element_type=F32)
    hidden = (silu(gate) * upward).astype(BF16)
    upward = up_shared + jnp.dot(lifted_shared, shared_b[...], preferred_element_type=F32)
    here = (row_tenant >= shared_tenant[:, :1]) & (row_tenant <= shared_tenant[:, shared_count - 1 :])
    hidden_shared = jnp.where(here, silu(gate_shared) * upward, 0.0).astype(BF16)

    hidden_out[...] = hidden
    hidden_shared_out[...] = hidden_shared
    share_out[...] = jnp.broadcast_to(share, share_out.shape)
    down_blocks(hidden, hidden_shared, share, down, down_shared, outs, chunks, order)


def down_outs(rows, depth, chunks, order):
    size = rows // len(order)
    part = depth // lax.axis_size("tensor")
    outs = []
    for chunk in chunks:
        outs += [jax.ShapeDtypeStruct((len(order) // 2, len(chunk), size, part), BF16)] * 2
    return outs


def down_cost(rows, down, chunks):
    part = sum(len(chunk) for chunk in chunks) * down.size // lax.axis_size("tensor")
    return cost(4 * rows * part, 0)


def down_products(gated, columns, shared_b, messages, down, down_shared, experts, chunks, order):
    rows, width = gated[1].shape
    whole = [*gated, columns, shared_b, *messages, down, down_shared]
    outs = [jax.ShapeDtypeStruct((rows, width), BF16)] * 2
    outs += [jax.ShapeDtypeStruct((rows, 128), F32)]
    outs += down_outs(rows, down.shape[1], chunks, order)
    apart = outs[4].shape
    outs[4] = jax.ShapeDtypeStruct((apart[0] - 1, *apart[1:]), BF16)
    outs.append(jax.ShapeDtypeStruct((1, *apart[1:]), BF16))
    return pl.pallas_call(
        functools.partial(down_kernel, experts, chunks, order),
        in_specs=[VMEM_SPEC] * len(whole),
        out_specs=[VMEM_SPEC] * len(outs),
        out_shape=outs,
        compiler_params=params(16),
        cost_estimate=down_cost(rows, down, chunks),
    )(*[in_vmem(x) for x in whole])


def down_next(hidden, down, down_shared, chunks, order):
    rows = hidden[0].shape[0]
    whole = [*hidden, down, down_shared]
    outs = down_outs(rows, down.shape[1], chunks, order)
    return pl.pallas_call(
        functools.partial(down_next_kernel, chunks, order),
        in_specs=[VMEM_SPEC] * len(whole),
        out_specs=[VMEM_SPEC] * len(outs),
        out_shape=outs,
        compiler_params=params(16),
        cost_estimate=down_cost(rows, down, chunks),
    )(*[in_vmem(x) for x in whole])


def local(
    tokens,
    expert_ids,
    gate_values,
    tenant_ids,
    w_gate,
    w_up,
    routed_down_weight,
    shared_gate,
    shared_up,
    shared_down,
    store_a,
    store_b,
    pair_slot,
    shared_a,
    shared_b,
):
    experts = pair_slot.shape[0]
    adapted, rank, model_width = store_a.shape
    hid = store_b.shape[2]
    steps, size, _ = expert_ids.shape
    count = lax.axis_size("expert")
    n_tensor = lax.axis_size("tensor")
    shared_count, store_count = shared_a.shape[0] * rank, adapted * rank

    rows_own = tokens.reshape(steps * size, model_width)
    arrived = swap(rows_own, count // 2)
    store_other = swap(store_a, 1).reshape(store_count, model_width)
    first = first_call(
        experts,
        jnp.swapaxes(expert_ids, 1, 2),
        jnp.swapaxes(gate_values, 1, 2),
        tenant_ids.reshape(1, size),
        pair_slot,
        [
            rows_own,
            store_b.reshape(store_count, hid),
            shared_b.reshape(shared_count, hid),
            store_a.reshape(store_count, model_width),
            shared_a.reshape(shared_count, model_width),
            w_gate[0],
            w_up[0],
            shared_gate,
            shared_up,
            routed_down_weight[0],
            shared_down,
        ],
    )
    pack, columns, rows_held, shared_b_held, factor_store, factor_shared = first[:6]
    weights, down, down_own = first[6:10], first[10], first[11]
    pack_other = swap(pack, 1)
    arrived, rows_held, store_other, pack_other = lax.optimization_barrier(
        (arrived, rows_held, store_other, pack_other)
    )
    came = far_rows(arrived, rows_own)
    message = make_message([rows_held, *came], factor_store, store_other, pack)
    messages = [pack, pack_other] + [swap(message, r) for r in range(2, count)]
    came, message = lax.optimization_barrier((came, message))
    rows = [rows_held, swap(rows_own, 1)]
    for value in came:
        rows += [value, swap(value, 1)]
    gated = gate_up(rows, [factor_shared, factor_store, store_other], weights)

    order = [0]
    bit = count // 2
    while bit >= 1:
        order = order + [r | bit for r in order]
        bit //= 2
    chunks = [[j] for j in range(n_tensor - 1, -1, -1)]
    hidden = down_products(
        gated, columns, shared_b_held, messages, down, down_own, experts, chunks[:-2], order
    )
    hidden, held, leaving, apart = hidden[:3], hidden[3:-1:2], hidden[4:-1:2], hidden[-1]
    held, leaving = list(held), list(leaving)
    bit = 1
    while bit < count:
        half = count // (2 * bit) // 2
        if bit > 1:
            for n in range(1, len(leaving)):
                leaving[n], *_ = lax.optimization_barrier((leaving[n], leaving[n - 1]))
        arrived = [swap(value, bit) for value in leaving]
        if bit == 1:
            ready = add(held[0][half:], arrived[0][half - 1 :])
            arrived[0] = jnp.concatenate([swap(apart, bit), arrived[0]], axis=0)
            hidden, ready = lax.optimization_barrier((hidden, ready))
            rest = down_next(hidden, down, down_own, chunks[len(held) :], order)
            held += rest[0::2]
            arrived += [swap(value, bit) for value in rest[1::2]]
        if 2 * bit < count:
            leaving = [add(h[half:], a[half:]) for h, a in zip(held, arrived)]
            held = [add(h[:half], a[:half]) for h, a in zip(held, arrived)]
        bit *= 2
    parts = {}
    for n, chunk in enumerate(chunks):
        for place, j in enumerate(chunk):
            parts[j] = [held[n][0, place], arrived[n][0, place]]
    bit = 1
    while bit < n_tensor:
        for j in sorted([j for j in parts if j & bit], reverse=True):
            parts[j ^ bit].append(swap(total_of(parts.pop(j)), bit, "tensor"))
        bit *= 2
    return total_of(parts[0]).reshape(steps, size, model_width // n_tensor)


def solution(mesh):
    return jax.shard_map(
        local,
        mesh=mesh,
        in_specs=(
            P(None, ("groups", "expert"), None),
            P(None, ("groups", "expert"), None),
            P(None, ("groups", "expert"), None),
            P(("groups", "expert")),
            P("expert", None, "tensor"),
            P("expert", None, "tensor"),
            P("expert", "tensor", None),
            P(None, "tensor"),
            P(None, "tensor"),
            P("tensor", None),
            P("expert", None, None),
            P("expert", None, "tensor"),
            P(),
            P("expert", None, None),
            P("expert", None, "tensor"),
        ),
        out_specs=P(None, ("groups", "expert"), "tensor"),
        check_vma=False,
    )
```
